512 devices in a mesh: lon: 32 (over z_hi, y), lat: 16 (over x, z_lo, core).
Axes of the slice: x: 4, y: 8, z: 8 (z_hi: 4, z_lo: 2; z = z_hi * 2 + z_lo), core: 2. Of those that a mesh axis runs over, the one named last changes fastest.
Arguments:
- thermal_anomaly: float32 [1, 1536, 4096], P(None, 'lat', 'lon'), may hold values from -6 to 6
- saltiness_anomaly: float32 [1, 1536, 4096], P(None, 'lat', 'lon'), may hold values from -6 to 6
- zonal_current: float32 [1, 1536, 4096], P(None, 'lat', 'lon'), may hold values from -3 to 3
- meridional_current: float32 [1, 1536, 4096], P(None, 'lat', 'lon'), may hold values from -3 to 3
- wet_indicator: int32 [1, 1536, 4096], P(None, 'lat', 'lon'), may hold values from 0 to 1, as said below
- opposite_meridian: int32 [4096], P('lon'), may hold values from 0 to 4095, as said below
Outputs:
- temperature_new: float32 [1, 1536, 4096], P(None, 'lat', 'lon')
- salinity_new: float32 [1, 1536, 4096], P(None, 'lat', 'lon')
- zonal_new: float32 [1, 1536, 4096], P(None, 'lat', 'lon')
- meridional_new: float32 [1, 1536, 4096], P(None, 'lat', 'lon')
The draws below stay inside these ranges and needn't reach their ends.
Inputs may be any that keep to these rules, and one draw needn't show every extreme that they name: `wet_indicator`: A cell that is land at one level is land at every deeper level. `opposite_meridian`: column i's partner j satisfies j // 128 == (-(i // 128)) modulo 4096 // 128, and every column is the partner of exactly one column.
All inputs are finite; a program needn't handle non-finite values.
Results may differ from the reference program's by a relative error of at most 0.00002.
Values sent between devices are 32-bit elements; how exact they have to be, the bound alone decides.
No kernel may reach another device: no remote copies, remote signals or barrier semaphores. Data moves between devices by JAX's collectives and lax.ppermute only.
A program may use at most 64 MiB of HBM per device.

```python
import jax
import jax.numpy as jnp
from jax import lax

CX = 128
DEPTH_LAYERS = 1
STEPS = 4
MERIDIAN_NUMBER = 4096
PARALLEL_NUMBER = 1536


def draw_wet_indicator(key, part):
    key = jax.random.fold_in(key, 11)
    depth_key, shore_key = jax.random.split(key)
    depth = jax.random.randint(depth_key, (PARALLEL_NUMBER, MERIDIAN_NUMBER), 1, DEPTH_LAYERS + 1)
    shore = jax.random.randint(shore_key, (PARALLEL_NUMBER, MERIDIAN_NUMBER), 0, 10)
    depth = jnp.where(shore > 0, depth, 0)
    levels = jnp.arange(DEPTH_LAYERS, dtype=jnp.int32)[:, None, None]
    return (levels < depth[None]).astype(jnp.int32)


def draw_opposite_meridian(key, part):
    key = jax.random.fold_in(key, 23)
    blocks = MERIDIAN_NUMBER // CX
    block_keys = jax.random.split(key, blocks)
    shuffles = jax.vmap(lambda one_key: jax.random.permutation(one_key, CX))(block_keys)
    facing = ((blocks - jnp.arange(blocks, dtype=jnp.int32)) % blocks)[:, None] * CX
    return (facing + shuffles.astype(jnp.int32)).reshape(MERIDIAN_NUMBER).astype(jnp.int32)


def shard_levels(stream_key, extent, cuts, least, largest):
    gain = 1.0
    for position, shards_of in cuts:
        steps = jax.random.uniform(jax.random.fold_in(jax.random.fold_in(stream_key, 6), position), (shards_of,), jnp.float32, least / len(cuts), largest / len(cuts))
        gain = gain * jnp.repeat(jnp.exp(steps), extent[position] // shards_of).reshape((-1,) + (1,) * (len(extent) - 1 - position))
    return gain


def bell_draw(own_key, dims, scale, most, shards=(), kind=jnp.bfloat16):
    values = jax.random.normal(own_key, dims, jnp.float32) * scale
    if len(shards) > 0:
        values = shard_levels(own_key, dims, shards, -0.22, 0.18) * values
    return jnp.clip(values, min=-most, max=most).astype(kind)


def setup_inputs(seed: int = 0) -> dict:
    streams_of = jax.random.split(jax.random.key(seed), 7)
    thermal_anomaly = bell_draw(streams_of[0], (DEPTH_LAYERS, PARALLEL_NUMBER, MERIDIAN_NUMBER), 1.0, 6.0, ((1, 16), (2, 32)), jnp.float32)
    saltiness_anomaly = bell_draw(streams_of[1], (DEPTH_LAYERS, PARALLEL_NUMBER, MERIDIAN_NUMBER), 1.0, 6.0, ((1, 16), (2, 32)), jnp.float32)
    zonal_current = bell_draw(streams_of[2], (DEPTH_LAYERS, PARALLEL_NUMBER, MERIDIAN_NUMBER), 0.5, 3.0, ((1, 16), (2, 32)), jnp.float32)
    meridional_current = bell_draw(streams_of[3], (DEPTH_LAYERS, PARALLEL_NUMBER, MERIDIAN_NUMBER), 0.5, 3.0, ((1, 16), (2, 32)), jnp.float32)
    wet_indicator = draw_wet_indicator(jax.random.fold_in(streams_of[6], 71), 0)
    opposite_meridian = draw_opposite_meridian(jax.random.fold_in(streams_of[6], 71), 0)
    return {"thermal_anomaly": thermal_anomaly, "saltiness_anomaly": saltiness_anomaly, "zonal_current": zonal_current, "meridional_current": meridional_current, "wet_indicator": wet_indicator, "opposite_meridian": opposite_meridian}


TIME_STEP = 0.1
DIFFUSE = 0.15
VISCOUS = 0.15
EXPAND = 0.2
CONTRACT = 0.8
ROTATION = 0.5


def interior(array, width):
    return array[..., width:array.shape[-2] - width, width:array.shape[-1] - width]


def laplace(field, mask):
    centre = field[..., 1:-1, 1:-1]
    total = mask[..., 1:-1, 2:] * (field[..., 1:-1, 2:] - centre)
    total = total + mask[..., 1:-1, :-2] * (field[..., 1:-1, :-2] - centre)
    total = total + mask[..., 2:, 1:-1] * (field[..., 2:, 1:-1] - centre)
    total = total + mask[..., :-2, 1:-1] * (field[..., :-2, 1:-1] - centre)
    return mask[..., 1:-1, 1:-1] * total


def biharmonic(field, mask):
    return laplace(laplace(field, mask), mask[..., 1:-1, 1:-1])


def advection(tracer, zonal, merid, mask):
    centre = tracer[..., 1:-1, 1:-1]
    zonal_centre = zonal[..., 1:-1, 1:-1]
    merid_centre = merid[..., 1:-1, 1:-1]
    eastern = mask[..., 1:-1, 2:] * (zonal_centre + zonal[..., 1:-1, 2:]) * (centre + tracer[..., 1:-1, 2:])
    western = mask[..., 1:-1, :-2] * (zonal_centre + zonal[..., 1:-1, :-2]) * (centre + tracer[..., 1:-1, :-2])
    northern = mask[..., 2:, 1:-1] * (merid_centre + merid[..., 2:, 1:-1]) * (centre + tracer[..., 2:, 1:-1])
    southern = mask[..., :-2, 1:-1] * (merid_centre + merid[..., :-2, 1:-1]) * (centre + tracer[..., :-2, 1:-1])
    return 0.25 * mask[..., 1:-1, 1:-1] * (eastern - western + northern - southern)


def gradient(press, mask):
    centre = press[..., 1:-1, 1:-1]
    centre_mask = mask[..., 1:-1, 1:-1]
    grad_x = 0.5 * centre_mask * (mask[..., 1:-1, 2:] * (press[..., 1:-1, 2:] - centre)
                                  + mask[..., 1:-1, :-2] * (centre - press[..., 1:-1, :-2]))
    grad_y = 0.5 * centre_mask * (mask[..., 2:, 1:-1] * (press[..., 2:, 1:-1] - centre)
                                  + mask[..., :-2, 1:-1] * (centre - press[..., :-2, 1:-1]))
    return grad_x, grad_y


def advance(extended, mask_ext, press, coriolis):
    smooth = biharmonic(extended, mask_ext)
    edge_mask = interior(mask_ext, 1)
    transport = advection(interior(extended[0:2], 1), interior(extended[2], 1), interior(extended[3], 1), edge_mask)
    grad_x, grad_y = gradient(interior(press, 1), edge_mask)
    sea_inner = interior(mask_ext, 2)
    previous = interior(extended, 2)
    tracers = sea_inner * (previous[0:2] - TIME_STEP * (transport + DIFFUSE * smooth[0:2]))
    zonal = sea_inner * (previous[2] + TIME_STEP * (coriolis * previous[3] - grad_x - VISCOUS * smooth[2]))
    merid = sea_inner * (previous[3] + TIME_STEP * (-coriolis * previous[2] - grad_y - VISCOUS * smooth[3]))
    return jnp.concatenate([tracers, zonal[None], merid[None]], axis=0)


def extend_global(fields, partner, parity):
    total_rows = fields.shape[-2]
    upper_rows = jnp.flip(fields[..., total_rows - 2:, :], axis=-2)
    ghost_rows = jnp.take(upper_rows, partner, axis=-1) * parity[:, None, None]
    southern = jnp.zeros(fields.shape[:-2] + (2, fields.shape[-1]), jnp.float32)
    extended = jnp.concatenate([southern, fields, ghost_rows], axis=-2)
    return jnp.concatenate([extended[..., -2:], extended, extended[..., :2]], axis=-1)


def reference(thermal_anomaly, saltiness_anomaly, zonal_current, meridional_current, wet_indicator, opposite_meridian):
    prognostic_fields = jnp.stack([thermal_anomaly, saltiness_anomaly, zonal_current, meridional_current]).astype(jnp.float32)
    sea = wet_indicator.astype(jnp.float32)
    parity = jnp.array([1.0, 1.0, -1.0, -1.0], jnp.float32)
    single = jnp.ones((1,), jnp.float32)
    row_place = jnp.arange(PARALLEL_NUMBER, dtype=jnp.int32).astype(jnp.float32)
    coriolis = (ROTATION * (2.0 * (row_place + 0.5) / PARALLEL_NUMBER - 1.0))[:, None]

    def level_step(carry, level):
        fields, mask = level
        extended = extend_global(fields, opposite_meridian, parity)
        mask_ext = extend_global(mask[None], opposite_meridian, single)[0]
        density = mask_ext * (CONTRACT * extended[1] - EXPAND * extended[0])
        press = carry + 0.5 * density
        return carry + density, advance(extended, mask_ext, press, coriolis)

    for step_index in range(STEPS):
        start = jnp.zeros((PARALLEL_NUMBER + 4, MERIDIAN_NUMBER + 4), jnp.float32)
        unused, updated = lax.scan(level_step, start, (jnp.moveaxis(prognostic_fields, 1, 0), sea))
        prognostic_fields = jnp.moveaxis(updated, 0, 1)
    return (prognostic_fields[0], prognostic_fields[1], prognostic_fields[2], prognostic_fields[3])
```

```python
import functools

import jax
import jax.numpy as jnp
from jax import lax
from jax.experimental import pallas as pl
from jax.experimental.pallas import tpu as pltpu
from jax.sharding import PartitionSpec as P

STEPS = 4
TIME_STEP = 0.1
DIFFUSE = 0.15
EXPAND = 0.2
CONTRACT = 0.8
ROTATION = 0.5

HALO = 2 * STEPS
LANES = 128
FIELDS = 4
REACH = 4
ARC = 2 * REACH + 1
CAP = 48
PARITY = (1.0, 1.0, -1.0, -1.0)


def lane_index(rows=8):
    return lax.broadcasted_iota(jnp.int32, (rows, LANES), 1)


def roll(x, shift):
    shift = shift % LANES
    return x if shift == 0 else pltpu.roll(x, shift, 1)


def rows_kernel(t_ref, s_ref, u_ref, v_ref, m_ref, opp_ref, a_ref, b_ref):
    odd = lax.rem(lax.axis_index("lat"), 2) == 1
    height = t_ref.shape[1]
    for i, ref in enumerate((t_ref, s_ref, u_ref, v_ref, m_ref)):
        south = ref[0, 0:HALO, :].astype(jnp.float32)
        north = ref[0, height - HALO : height, :].astype(jnp.float32)
        a_ref[i * 8 : i * 8 + 8, :] = jnp.where(odd, south, north)
        b_ref[i * 8 : i * 8 + 8, :] = jnp.where(odd, north, south)
    b_ref[40:48, :] = jnp.broadcast_to(opp_ref[...].astype(jnp.float32), (8, LANES))


def halo_tiles(refs, ra_ref, rb_ref, odd, i):
    ra, rb = ra_ref[i * 8 : i * 8 + 8, :], rb_ref[i * 8 : i * 8 + 8, :]
    ref = refs[i]
    own = [
        ref[0, 8 * g : 8 * g + 8, :].astype(jnp.float32) for g in range(ref.shape[1] // 8)
    ]
    return [jnp.where(odd, ra, rb)] + own + [jnp.where(odd, rb, ra)]


def columns_kernel(t_ref, s_ref, u_ref, v_ref, m_ref, sb_ref, ra_ref, rb_ref, e_ref, w_ref):
    odd = lax.rem(lax.axis_index("lat"), 2) == 1
    lane = lane_index()
    refs = (t_ref, s_ref, u_ref, v_ref, m_ref)
    for i in range(5):
        tiles = halo_tiles(refs, ra_ref, rb_ref, odd, i)
        east = jnp.zeros((8, LANES), jnp.float32)
        west = jnp.zeros((8, LANES), jnp.float32)
        for g, tile in enumerate(tiles):
            here = (lane >= 8 * g) & (lane < 8 * g + 8)
            east = jnp.where(here, roll(tile, 8 * g - (LANES - HALO)), east)
            west = jnp.where(here, roll(tile, 8 * g), west)
        e_ref[i * 8 : i * 8 + 8, :] = east
        w_ref[i * 8 : i * 8 + 8, :] = west
    for ref in (e_ref, w_ref):
        ref[40 : 40 + CAP, :] = sb_ref[...]
        ref[40 + CAP : 40 + 2 * CAP, :] = rb_ref[...]


def first_pass(centre, north, south, east, west, sea, count, w_e, w_n, w_s, turn, roll_w):
    laps = [
        sea * (((east[i] + west[i]) + (north[i] + south[i])) - count * centre[i])
        for i in range(FIELDS)
    ]
    t, s, u, v = centre
    flow_e = w_e * (u + east[2])
    flow_n = w_n * (v + north[3])
    flow_s = w_s * (v + south[3])
    partial = []
    for i in (0, 1):
        c = centre[i]
        x = flow_e * (c + east[i])
        y = flow_n * (c + north[i]) - flow_s * (c + south[i])
        partial.append(c - (0.25 * TIME_STEP) * ((x - roll_w(x)) + y))
    ratio = EXPAND / CONTRACT
    slope = 0.25 * TIME_STEP * CONTRACT
    q = s - ratio * t
    q_e = east[1] - ratio * east[0]
    q_n = north[1] - ratio * north[0]
    q_s = south[1] - ratio * south[0]
    d = w_e * (q_e - q)
    partial.append(u + (turn * v - slope * (d + roll_w(d))))
    partial.append(v - (turn * u + slope * (w_n * (q_n - q) + w_s * (q - q_s))))
    return laps, partial


def second_pass(partial, lap, north, south, east, west, sea, count):
    mix = ((east + west) + (north + south)) - count * lap
    return sea * (partial - (TIME_STEP * DIFFUSE) * mix)


def steps_kernel(
    lat_count,
    t_ref,
    s_ref,
    u_ref,
    v_ref,
    m_ref,
    sb_ref,
    ra_ref,
    rb_ref,
    rw_ref,
    re_ref,
    w3_ref,
    e3_ref,
    t_out,
    s_out,
    u_out,
    v_out,
    state,
    laps,
    part,
    stat,
    turn_ref,
    cap,
    cap_lap,
    cap_part,
    cap_stat,
    cap_opp,
):
    lat = lax.axis_index("lat")
    odd = lax.rem(lat, 2) == 1
    top = lat == lat_count - 1
    lane = lane_index()
    height = t_ref.shape[1]
    total_rows = height * lat_count
    tiles_n = height // 8 + 2
    band = 8 * tiles_n
    refs = (t_ref, s_ref, u_ref, v_ref, m_ref)
    tile_rows = [8 + 8 * g for g in range(2 * tiles_n)]

    for i in range(5):
        tiles = halo_tiles(refs, ra_ref, rb_ref, odd, i)
        from_w, from_e = rw_ref[i * 8 : i * 8 + 8, :], re_ref[i * 8 : i * 8 + 8, :]
        for g, tile in enumerate(tiles):
            west = jnp.where(lane < HALO, roll(from_w, -8 * g), roll(tile, HALO))
            east = jnp.where(
                lane >= LANES - HALO, roll(from_e, LANES - HALO - 8 * g), roll(tile, -HALO)
            )
            if i < FIELDS:
                state[i, 8 + 8 * g : 16 + 8 * g, :] = west
                state[i, 8 + band + 8 * g : 16 + band + 8 * g, :] = east
            else:
                stat[0, 8 + 8 * g : 16 + 8 * g, :] = west
                stat[0, 8 + band + 8 * g : 16 + band + 8 * g, :] = east
    nothing = jnp.zeros((8, LANES), jnp.float32)
    for row in (0, 8 + 2 * band):
        for i in range(FIELDS):
            state[i, row : row + 8, :] = nothing
            laps[i, row : row + 8, :] = nothing
        for i in range(4):
            stat[i, row : row + 8, :] = nothing

    def ghosts_to_main(source, target):
        for side_row, low, high, shift in ((8, 3, 4, HALO), (8 + band, 4, 5, -HALO)):
            row = side_row + band - HALO
            a, b = source(low), source(high)
            if shift > 0:
                value = jnp.where(lane[0:2] < HALO, roll(a, shift), roll(b, shift))
            else:
                value = jnp.where(lane[0:2] >= LANES - HALO, roll(b, shift), roll(a, shift))
            target(row, value)

    def fill_ghosts(ref, i, parity):
        for side in (0, 1):
            for k in range(ARC):
                index = cap_opp[side, k]
                rows = ref[1 - side, i, ARC - 1 - k, 0:8, :]
                ghost = jnp.take_along_axis(rows, index, axis=1, mode="promise_in_bounds")
                ref[side, i, k, 8:9, :] = parity * ghost[7:8, :]
                ref[side, i, k, 9:10, :] = parity * ghost[6:7, :]

    def main_ghosts():
        for i in range(FIELDS):

            def put(row, value, i=i):
                state[i, row : row + 2, :] = value

            ghosts_to_main(lambda k, i=i: cap[0, i, k, 8:10, :], put)

    def cap_rolls(rows_of, side):
        blocks = [rows_of(side, k) for k in range(ARC)]
        return blocks, *arc_neighbours(blocks)

    def arc_neighbours(blocks):
        e, w = [roll(x, -1) for x in blocks], [roll(x, 1) for x in blocks]
        east = [
            jnp.where(lane == LANES - 1, e[min(k + 1, ARC - 1)], e[k]) for k in range(ARC)
        ]
        west = [jnp.where(lane == 0, w[max(k - 1, 0)], w[k]) for k in range(ARC)]
        return east, west

    @pl.when(top)
    def _():
        pieces = []
        for n in range(3):
            pieces.append((n - REACH, w3_ref, n * 2 * CAP))
        pieces.append((-1, rw_ref, 40))
        pieces.append((1, re_ref, 40))
        for n in range(3):
            pieces.append((n + 2, e3_ref, n * 2 * CAP))
        blocks = [(o + REACH, ref, base, ref, base + CAP) for o, ref, base in pieces]
        blocks.append((REACH, sb_ref, 0, rb_ref, 0))
        for k, own, own_base, facing, facing_base in blocks:
            for side, place, ref, base in (
                (0, k, own, own_base),
                (1, ARC - 1 - k, facing, facing_base),
            ):
                sea = ref[base + 32 : base + 40, :]
                cap_stat[side, 0, place, 0:8, :] = sea
                cap_stat[side, 0, place, 10:16, :] = nothing[0:6]
                for i in range(FIELDS):
                    cap[side, i, place, 0:8, :] = sea * ref[base + 8 * i : base + 8 * i + 8, :]
                    cap[side, i, place, 10:16, :] = nothing[0:6]
                    cap_lap[side, i, place, 0:8, :] = nothing
                    cap_lap[side, i, place, 8:16, :] = nothing
                opp = ref[base + 40 : base + 48, :].astype(jnp.int32)
                cap_opp[side, place] = lax.rem(opp, LANES)
        fill_ghosts(cap_stat, 0, 1.0)
        for i in range(FIELDS):
            fill_ghosts(cap, i, PARITY[i])
        for side in (0, 1):
            for start in (0, 1):
                seas = [cap_stat[side, 0, k, start : start + 8, :] for k in range(ARC)]
                east, west = arc_neighbours(seas)
                for k in range(ARC):
                    north = cap_stat[side, 0, k, start + 1 : start + 9, :]
                    if start:
                        south = cap_stat[side, 0, k, start - 1 : start + 7, :]
                        cap_stat[side, 1, k, start : start + 8, :] = (
                            (east[k] + west[k]) + (north + south)
                        )
                    cap_stat[side, 2, k, start : start + 8, :] = seas[k] * east[k]
                    cap_stat[side, 3, k, start : start + 8, :] = seas[k] * north

        def put(row, value):
            stat[0, row : row + 2, :] = value

        ghosts_to_main(lambda k: cap_stat[0, 0, k, 8:10, :], put)
        main_ghosts()

    base_row = (lat * height - HALO).astype(jnp.float32)
    sub = lax.broadcasted_iota(jnp.int32, (8, LANES), 0).astype(jnp.float32)

    def turning(row):
        return (TIME_STEP * ROTATION) * (2.0 * (row + 0.5) / total_rows - 1.0)

    for n, r in enumerate(tile_rows):
        sea = stat[0, r : r + 8, :]
        north = stat[0, r + 1 : r + 9, :]
        south = stat[0, r - 1 : r + 7, :]
        east, west = roll(sea, -1), roll(sea, 1)
        stat[1, r : r + 8, :] = (east + west) + (north + south)
        stat[2, r : r + 8, :] = sea * east
        stat[3, r : r + 8, :] = sea * north
        for i in range(FIELDS):
            state[i, r : r + 8, :] = sea * state[i, r : r + 8, :]
        if n < tiles_n:
            turn_ref[r : r + 8, :] = turning(base_row + float(8 * n) + sub)

    def main_first(r):
        centre = [state[i, r : r + 8, :] for i in range(FIELDS)]
        north = [state[i, r + 1 : r + 9, :] for i in range(FIELDS)]
        south = [state[i, r - 1 : r + 7, :] for i in range(FIELDS)]
        east = [roll(x, -1) for x in centre]
        west = [roll(x, 1) for x in centre]
        turn_row = r if r < 8 + band else r - band
        lap, partial = first_pass(
            centre,
            north,
            south,
            east,
            west,
            stat[0, r : r + 8, :],
            stat[1, r : r + 8, :],
            stat[2, r : r + 8, :],
            stat[3, r : r + 8, :],
            stat[3, r - 1 : r + 7, :],
            turn_ref[turn_row : turn_row + 8, :],
            lambda x: roll(x, 1),
        )
        for i in range(FIELDS):
            laps[i, r : r + 8, :] = lap[i]
            part[i, r : r + 8, :] = partial[i]

    def main_second(r):
        sea, count = stat[0, r : r + 8, :], stat[1, r : r + 8, :]
        for i in range(FIELDS):
            lap = laps[i, r : r + 8, :]
            state[i, r : r + 8, :] = second_pass(
                part[i, r : r + 8, :],
                lap,
                laps[i, r + 1 : r + 9, :],
                laps[i, r - 1 : r + 7, :],
                roll(lap, -1),
                roll(lap, 1),
                sea,
                count,
            )

    cap_turn = turning(float(total_rows - HALO + 1) + sub)

    def cap_first():
        for side in (0, 1):
            fields = [
                cap_rolls(lambda sd, k, i=i: cap[sd, i, k, 1:9, :], side) for i in range(FIELDS)
            ]
            for k in range(ARC):
                centre = [fields[i][0][k] for i in range(FIELDS)]
                east = [fields[i][1][k] for i in range(FIELDS)]
                west = [fields[i][2][k] for i in range(FIELDS)]
                north = [cap[side, i, k, 2:10, :] for i in range(FIELDS)]
                south = [cap[side, i, k, 0:8, :] for i in range(FIELDS)]
                before = max(k - 1, 0)
                w_e = cap_stat[side, 2, k, 1:9, :]
                w_e_before = cap_stat[side, 2, before, 1:9, :]

                def roll_w(x, kind=iter(range(3))):
                    which = next(kind)
                    b = [fields[i][0][before] for i in range(FIELDS)]
                    be = [fields[i][1][before] for i in range(FIELDS)]
                    if which < 2:
                        other = w_e_before * (b[2] + be[2]) * (b[which] + be[which])
                    else:
                        ratio = EXPAND / CONTRACT
                        other = w_e_before * ((be[1] - ratio * be[0]) - (b[1] - ratio * b[0]))
                    return roll(jnp.where(lane == LANES - 1, other, x), 1)

                lap, partial = first_pass(
                    centre,
                    north,
                    south,
                    east,
                    west,
                    cap_stat[side, 0, k, 1:9, :],
                    cap_stat[side, 1, k, 1:9, :],
                    w_e,
                    cap_stat[side, 3, k, 1:9, :],
                    cap_stat[side, 3, k, 0:8, :],
                    cap_turn,
                    roll_w,
                )
                for i in range(FIELDS):
                    cap_lap[side, i, k, 1:9, :] = lap[i]
                    cap_part[side, i, k, 0:8, :] = partial[i]

    def cap_second():
        for side in (0, 1):
            for i in range(FIELDS):
                blocks, east, west = cap_rolls(
                    lambda sd, k, i=i: cap_lap[sd, i, k, 1:9, :], side
                )
                for k in range(ARC):
                    cap[side, i, k, 1:9, :] = second_pass(
                        cap_part[side, i, k, 0:8, :],
                        blocks[k],
                        cap_lap[side, i, k, 2:10, :],
                        cap_lap[side, i, k, 0:8, :],
                        east[k],
                        west[k],
                        cap_stat[side, 0, k, 1:9, :],
                        cap_stat[side, 1, k, 1:9, :],
                    )

    def step(n, carry):
        for r in tile_rows:
            main_first(r)
        for r in tile_rows:
            main_second(r)

        @pl.when(top & (n < STEPS - 1))
        def _():
            cap_first()
            cap_second()
            for i in range(FIELDS):
                fill_ghosts(cap, i, PARITY[i])
            main_ghosts()

        return carry

    lax.fori_loop(0, STEPS, step, 0)

    for i, out in enumerate((t_out, s_out, u_out, v_out)):
        for g in range(height // 8):
            r = 8 + HALO + 8 * g
            west, east = state[i, r : r + 8, :], state[i, r + band : r + band + 8, :]
            out[0, 8 * g : 8 * g + 8, :] = jnp.where(
                lane < LANES // 2, roll(west, -HALO), roll(east, HALO)
            )


def body(lon_count, lat_count, t, s, u, v, m, opp):
    fields = (t, s, u, v, m)
    height = t.shape[1]
    whole = pl.BlockSpec(memory_space=pltpu.VMEM)
    f32 = jnp.float32
    limit = pltpu.CompilerParams(vmem_limit_bytes=32 * 1024 * 1024)

    def call(kernel, inputs, shapes, scratch=()):
        return pl.pallas_call(
            kernel,
            out_shape=[jax.ShapeDtypeStruct(shape, f32) for shape in shapes],
            in_specs=[whole] * len(inputs),
            out_specs=[whole] * len(shapes),
            scratch_shapes=list(scratch),
            compiler_params=limit,
        )(*inputs)

    def place(lon, lat):
        return (lon % lon_count) * lat_count + lat

    lons, lats = range(lon_count), range(lat_count)
    last = lat_count - 1
    pairs_a = [(place(i, j), place(i, j ^ 1)) for i in lons for j in lats]
    pairs_b = [(place(i, j), place(i, ((j - 1) ^ 1) + 1)) for i in lons for j in lats[1:last]]
    pairs_b += [(place(i, last), place(-i, last)) for i in lons]

    def shift(x, by, rows):
        pairs = [(place(i, j), place(i + by, j)) for i in lons for j in rows]
        return lax.ppermute(x, ("lon", "lat"), pairs)

    send_a, send_b = call(rows_kernel, (*fields, opp.reshape(1, LANES)), [(CAP, LANES)] * 2)
    from_a = lax.ppermute(send_a, ("lon", "lat"), pairs_a)
    from_b = lax.ppermute(send_b, ("lon", "lat"), pairs_b)
    wide = 40 + 2 * CAP
    send_e, send_w = call(
        columns_kernel, (*fields, send_b, from_a, from_b), [(wide, LANES)] * 2
    )
    from_w = shift(send_e, 1, lats)
    from_e = shift(send_w, -1, lats)
    three = jnp.concatenate([from_w[40:], send_e[40:], from_e[40:]], axis=0)
    far_w = shift(three, 3, [last])
    far_e = shift(three, -3, [last])
    rows = 16 + 2 * (height + 2 * HALO)
    return tuple(
        call(
            functools.partial(steps_kernel, lat_count),
            (*fields, send_b, from_a, from_b, from_w, from_e, far_w, far_e),
            [t.shape] * 4,
            [
                pltpu.VMEM((FIELDS, rows, LANES), f32),
                pltpu.VMEM((FIELDS, rows, LANES), f32),
                pltpu.VMEM((FIELDS, rows, LANES), f32),
                pltpu.VMEM((4, rows, LANES), f32),
                pltpu.VMEM((8 + height + 2 * HALO, LANES), f32),
                pltpu.VMEM((2, FIELDS, ARC, 16, LANES), f32),
                pltpu.VMEM((2, FIELDS, ARC, 16, LANES), f32),
                pltpu.VMEM((2, FIELDS, ARC, 8, LANES), f32),
                pltpu.VMEM((2, 4, ARC, 16, LANES), f32),
                pltpu.VMEM((2, ARC, 8, LANES), jnp.int32),
            ],
        )
    )


def solution(mesh):
    placed = P(None, "lat", "lon")
    return jax.shard_map(
        functools.partial(body, mesh.shape["lon"], mesh.shape["lat"]),
        mesh=mesh,
        in_specs=(placed,) * 5 + (P("lon"),),
        out_specs=(placed,) * 4,
        check_vma=False,
    )
```

```python
import functools

import jax
import jax.numpy as jnp
from jax import lax
from jax.experimental import pallas as pl
from jax.experimental.pallas import tpu as pltpu
from jax.sharding import PartitionSpec as P

STEPS = 4
TIME_STEP = 0.1
DIFFUSE = 0.15
EXPAND = 0.2
CONTRACT = 0.8
ROTATION = 0.5

HALO = 2 * STEPS
LANES = 128
FIELDS = 4
REACH = 4
ARC = 2 * REACH + 1
CAP = 48
PARITY = (1.0, 1.0, -1.0, -1.0)
GROUP = 14
FAR_ROWS = (2, 4, 6)
FAR = 128
UPPER = 24


def lane_index(rows=8):
    return lax.broadcasted_iota(jnp.int32, (rows, LANES), 1)


def roll(x, shift):
    shift = shift % LANES
    return x if shift == 0 else pltpu.roll(x, shift, 1)


def is_odd():
    return lax.rem(lax.axis_index("lat"), 2) == 1


def is_top():
    return lax.axis_index("lat") == lax.axis_size("lat") - 1


def edge_rows(refs, start, buffer, ints, sems):
    copies = []
    for i, ref in enumerate(refs):
        target = buffer.at[pl.ds(8 * i, 8), :] if i < FIELDS else ints.at[pl.ds(0, 8), :]
        copies.append(
            pltpu.make_async_copy(ref.at[0, pl.ds(start, HALO), :], target, sems.at[i])
        )
    return copies


def fold_rows_kernel(t_ref, s_ref, u_ref, v_ref, m_ref, opp_ref, b_ref, ints, sems):
    height = t_ref.shape[1]
    start = pl.multiple_of(jnp.where(is_odd(), height - HALO, 0), 8)
    copies = edge_rows((t_ref, s_ref, u_ref, v_ref, m_ref), start, b_ref, ints, sems)
    copies.append(pltpu.make_async_copy(opp_ref, ints.at[pl.ds(8, 1), :], sems.at[5]))
    for copy in copies:
        copy.start()
    for copy in copies:
        copy.wait()
    b_ref[32:40, :] = ints[0:8, :].astype(jnp.float32)
    b_ref[40:48, :] = jnp.broadcast_to(ints[8:9, :].astype(jnp.float32), (8, LANES))


def load_kernel(t_ref, s_ref, u_ref, v_ref, m_ref, b_ref, fields, a_ref, ints, sems):
    height = t_ref.shape[1]
    copies = []
    for i, ref in enumerate((t_ref, s_ref, u_ref, v_ref, m_ref)):
        target = fields.at[i] if i < FIELDS else ints
        copies.append(pltpu.make_async_copy(ref.at[0], target, sems.at[i]))
    for copy in copies:
        copy.start()
    for copy in copies:
        copy.wait()
    fields[FIELDS] = ints[...].astype(jnp.float32)
    odd = is_odd()
    for i in range(5):
        a_ref[i * 8 : i * 8 + 8, :] = jnp.where(
            odd, fields[i, 0:HALO, :], fields[i, height - HALO : height, :]
        )


def halo_tiles(fields, ra_ref, rb_ref, odd, i):
    ra, rb = ra_ref[i * 8 : i * 8 + 8, :], rb_ref[i * 8 : i * 8 + 8, :]
    own = [fields[i, 8 * g : 8 * g + 8, :] for g in range(fields.shape[1] // 8)]
    return [jnp.where(odd, ra, rb)] + own + [jnp.where(odd, rb, ra)]


def columns_kernel(fields, sb_ref, ra_ref, rb_ref, e_ref, w_ref):
    odd = is_odd()
    lane = lane_index()
    for i in range(5):
        tiles = halo_tiles(fields, ra_ref, rb_ref, odd, i)
        east = jnp.zeros((8, LANES), jnp.float32)
        west = jnp.zeros((8, LANES), jnp.float32)
        for g, tile in enumerate(tiles):
            here = (lane >= 8 * g) & (lane < 8 * g + 8)
            east = jnp.where(here, roll(tile, 8 * g - (LANES - HALO)), east)
            west = jnp.where(here, roll(tile, 8 * g), west)
        e_ref[i * 8 : i * 8 + 8, :] = east
        w_ref[i * 8 : i * 8 + 8, :] = west
    for ref in (e_ref, w_ref):
        ref[40 : 40 + CAP, :] = sb_ref[...]
        ref[40 + CAP : 40 + 2 * CAP, :] = rb_ref[...]


def far_places(counts):
    base = 0
    for j, n in enumerate(counts):
        for side in (0, 1):
            yield j, side, n, base
            base += 5 * n + 1


def far_kernel(sb_ref, rb_ref, rw_ref, re_ref, e_ref, w_ref):
    @pl.when(is_top())
    def _():
        sources = (
            ((rw_ref, 40), (rw_ref, 40 + CAP)),
            ((sb_ref, 0), (rb_ref, 0)),
            ((re_ref, 40), (re_ref, 40 + CAP)),
        )
        for out, counts in ((e_ref, FAR_ROWS), (w_ref, FAR_ROWS[::-1])):
            for j, side, n, base in far_places(counts):
                ref, at = sources[j][side]
                for i in range(5):
                    out[base + i * n : base + i * n + n, :] = ref[
                        at + 8 * i + 8 - n : at + 8 * i + 8, :
                    ]
                out[base + 5 * n : base + 5 * n + 1, :] = ref[at + 40 : at + 41, :]
            out[FAR - 2 : FAR, :] = jnp.zeros((2, LANES), jnp.float32)


def first_pass(centre, north, south, east, west, sea, count, w_e, w_n, w_s, turn, roll_w):
    laps = [
        sea * (((east[i] + west[i]) + (north[i] + south[i])) - count * centre[i])
        for i in range(FIELDS)
    ]
    t, s, u, v = centre
    flow_e = w_e * (u + east[2])
    flow_n = w_n * (v + north[3])
    flow_s = w_s * (v + south[3])
    partial = []
    for i in (0, 1):
        c = centre[i]
        x = flow_e * (c + east[i])
        y = flow_n * (c + north[i]) - flow_s * (c + south[i])
        partial.append(c - (0.25 * TIME_STEP) * ((x - roll_w[i](x)) + y))
    ratio = EXPAND / CONTRACT
    slope = 0.25 * TIME_STEP * CONTRACT
    q = s - ratio * t
    q_e = east[1] - ratio * east[0]
    q_n = north[1] - ratio * north[0]
    q_s = south[1] - ratio * south[0]
    d = w_e * (q_e - q)
    partial.append(u + (turn * v - slope * (d + roll_w[2](d))))
    partial.append(v - (turn * u + slope * (w_n * (q_n - q) + w_s * (q - q_s))))
    return laps, partial


def second_pass(partial, lap, north, south, east, west, sea, count):
    mix = ((east + west) + (north + south)) - count * lap
    return sea * (partial - (TIME_STEP * DIFFUSE) * mix)


class Band:
    def __init__(self, state, laps, part, stat):
        self.state, self.laps, self.part, self.stat = state, laps, part, stat
        self.tiles = state.shape[1] // 8 - 2

    def pad(self):
        nothing = jnp.zeros((8, LANES), jnp.float32)
        for row in (0, 8 + 8 * self.tiles):
            for i in range(FIELDS):
                self.state[i, row : row + 8, :] = nothing
                self.laps[i, row : row + 8, :] = nothing
            for i in range(4):
                self.stat[i, row : row + 8, :] = nothing

    def each_tile(self, work, group):
        def trip(n, carry):
            start = pl.multiple_of(8 + 8 * group * n, 8)
            for j in range(group):
                work(start + 8 * j)
            return carry

        lax.fori_loop(0, self.tiles // group, trip, 0)

    def weigh(self, turning):
        def work(r):
            sea = self.stat[0, pl.ds(r, 8), :]
            north = self.stat[0, pl.ds(r + 1, 8), :]
            south = self.stat[0, pl.ds(r - 1, 8), :]
            east, west = roll(sea, -1), roll(sea, 1)
            self.stat[1, pl.ds(r, 8), :] = (east + west) + (north + south)
            self.stat[2, pl.ds(r, 8), :] = sea * east
            self.stat[3, pl.ds(r, 8), :] = sea * north
            self.stat[4, pl.ds(r, 8), :] = turning(r)
            for i in range(FIELDS):
                self.state[i, pl.ds(r, 8), :] = sea * self.state[i, pl.ds(r, 8), :]

        return work

    def first(self, r):
        def rows(ref, i, by=0):
            return ref[i, pl.ds(r + by, 8), :]

        centre = [rows(self.state, i) for i in range(FIELDS)]
        lap, partial = first_pass(
            centre,
            [rows(self.state, i, 1) for i in range(FIELDS)],
            [rows(self.state, i, -1) for i in range(FIELDS)],
            [roll(x, -1) for x in centre],
            [roll(x, 1) for x in centre],
            rows(self.stat, 0),
            rows(self.stat, 1),
            rows(self.stat, 2),
            rows(self.stat, 3),
            rows(self.stat, 3, -1),
            rows(self.stat, 4),
            (lambda x: roll(x, 1),) * 3,
        )
        for i in range(FIELDS):
            self.laps[i, pl.ds(r, 8), :] = lap[i]
            self.part[i, pl.ds(r, 8), :] = partial[i]

    def second(self, r):
        sea, count = self.stat[0, pl.ds(r, 8), :], self.stat[1, pl.ds(r, 8), :]
        for i in range(FIELDS):
            lap = self.laps[i, pl.ds(r, 8), :]
            self.state[i, pl.ds(r, 8), :] = second_pass(
                self.part[i, pl.ds(r, 8), :],
                lap,
                self.laps[i, pl.ds(r + 1, 8), :],
                self.laps[i, pl.ds(r - 1, 8), :],
                roll(lap, -1),
                roll(lap, 1),
                sea,
                count,
            )

    def step(self, group):
        self.each_tile(self.first, group)
        self.each_tile(self.second, group)


def shifted_ghosts(blocks):
    before, here, after = blocks
    lane = lane_index(here.shape[0])
    return (
        jnp.where(lane < HALO, roll(before, HALO), roll(here, HALO)),
        jnp.where(lane >= LANES - HALO, roll(after, -HALO), roll(here, -HALO)),
    )


def turning_of(row, total_rows):
    return (TIME_STEP * ROTATION) * (2.0 * (row + 0.5) / total_rows - 1.0)


def row_in_tile():
    return lax.broadcasted_iota(jnp.int32, (8, LANES), 0).astype(jnp.float32)


def main_kernel(
    fields,
    sb_ref,
    ra_ref,
    rb_ref,
    rw_ref,
    re_ref,
    t_out,
    s_out,
    u_out,
    v_out,
    upper_state,
    upper_stat,
    state,
    laps,
    part,
    stat,
):
    odd, top = is_odd(), is_top()
    lane = lane_index()
    height = fields.shape[1]
    total_rows = height * lax.axis_size("lat")
    tiles_n = height // 8 + 2
    band = 8 * tiles_n
    bands = Band(state, laps, part, stat)

    for i in range(5):
        tiles = halo_tiles(fields, ra_ref, rb_ref, odd, i)
        from_w, from_e = rw_ref[i * 8 : i * 8 + 8, :], re_ref[i * 8 : i * 8 + 8, :]
        ref, at = (state, i) if i < FIELDS else (stat, 0)
        for g, tile in enumerate(tiles):
            ref[at, 8 + 8 * g : 16 + 8 * g, :] = jnp.where(
                lane < HALO, roll(from_w, -8 * g), roll(tile, HALO)
            )
            ref[at, 8 + band + 8 * g : 16 + band + 8 * g, :] = jnp.where(
                lane >= LANES - HALO, roll(from_e, LANES - HALO - 8 * g), roll(tile, -HALO)
            )
    bands.pad()

    @pl.when(top)
    def _():
        pairs = ((rw_ref, 40, rw_ref, 40 + CAP), (sb_ref, 0, rb_ref, 0), (re_ref, 40, re_ref, 40 + CAP))
        for i in range(5):
            ghosts = []
            for own, own_at, facing, facing_at in pairs:
                index = lax.rem(own[own_at + 40 : own_at + 48, :].astype(jnp.int32), LANES)
                rows = facing[facing_at + 8 * i : facing_at + 8 * i + 8, :]
                ghosts.append(
                    (PARITY + (1.0,))[i]
                    * jnp.take_along_axis(rows, index, axis=1, mode="promise_in_bounds")
                )
            ref, at = (state, i) if i < FIELDS else (stat, 0)
            for which, ghost in enumerate(shifted_ghosts(ghosts)):
                row = 8 + band * (which + 1) - HALO
                ref[at, row : row + 1, :] = ghost[7:8, :]
                ref[at, row + 1 : row + 2, :] = ghost[6:7, :]

    base_row = (lax.axis_index("lat") * height - HALO).astype(jnp.float32)
    sub = row_in_tile()
    bands.each_tile(
        bands.weigh(
            lambda r: turning_of(
                base_row + lax.rem(r - 8, band).astype(jnp.float32) + sub, total_rows
            )
        ),
        GROUP,
    )

    def step(n, carry):
        bands.step(GROUP)

        @pl.when(top & (n == 0))
        def _():
            for which in (0, 1):
                row = 8 + band * (which + 1) - UPPER
                for i in range(FIELDS):
                    upper_state[i, which] = state[i, row : row + UPPER, :]
                for i in range(5):
                    upper_stat[i, which] = stat[i, row : row + UPPER, :]

        return carry

    lax.fori_loop(0, STEPS, step, 0)

    for i, out in enumerate((t_out, s_out, u_out, v_out)):
        for g in range(height // 8):
            r = 8 + HALO + 8 * g
            west, east = state[i, r : r + 8, :], state[i, r + band : r + band + 8, :]
            out[0, 8 * g : 8 * g + 8, :] = jnp.where(
                lane < LANES // 2, roll(west, -HALO), roll(east, HALO)
            )


def arc_neighbours(blocks):
    lane = lane_index()
    last = len(blocks) - 1
    e, w = [roll(x, -1) for x in blocks], [roll(x, 1) for x in blocks]
    east = [jnp.where(lane == LANES - 1, e[min(k + 1, last)], e[k]) for k in range(last + 1)]
    west = [jnp.where(lane == 0, w[max(k - 1, 0)], w[k]) for k in range(last + 1)]
    return east, west


def cap_kernel(
    t_in,
    s_in,
    u_in,
    v_in,
    upper_state,
    upper_stat,
    sb_ref,
    rb_ref,
    rw_ref,
    re_ref,
    w3_ref,
    e3_ref,
    t_out,
    s_out,
    u_out,
    v_out,
    state,
    laps,
    part,
    stat,
    cap,
    cap_lap,
    cap_part,
    cap_stat,
    cap_opp,
    rows_out,
    sems,
):
    lane = lane_index()
    height = t_out.shape[1]
    total_rows = height * lax.axis_size("lat")
    bands = Band(state, laps, part, stat)
    nothing = jnp.zeros((8, LANES), jnp.float32)
    cap_turn = turning_of(float(total_rows - HALO + 1) + row_in_tile(), total_rows)

    def fill_ghosts(ref, parities, low, high, sides):
        def one(side, carry):
            ghosts = {}
            for k in range(low, high):
                index = cap_opp[side, k]
                for i, parity in enumerate(parities):
                    rows = ref[1 - side, i, ARC - 1 - k, 0:8, :]
                    ghosts[k, i] = parity * jnp.take_along_axis(
                        rows, index, axis=1, mode="promise_in_bounds"
                    )
            for (k, i), ghost in ghosts.items():
                ref[side, i, k, 8:9, :] = ghost[7:8, :]
                ref[side, i, k, 9:10, :] = ghost[6:7, :]
            return carry

        lax.fori_loop(0, sides, one, 0)

    def put_block(side, place, ref, base, n):
        sea = ref[base + 4 * n : base + 5 * n, :]
        cap_stat[side, 0, place, 8 - n : 8, :] = sea
        cap_stat[side, 0, place, 10:16, :] = nothing[0:6]
        if n < 8:
            cap_stat[side, 0, place, 0 : 8 - n, :] = nothing[n:8]
        for i in range(FIELDS):
            cap[side, i, place, 8 - n : 8, :] = sea * ref[base + n * i : base + n * i + n, :]
            if n < 8:
                cap[side, i, place, 0 : 8 - n, :] = nothing[n:8]
            cap[side, i, place, 10:16, :] = nothing[0:6]
            cap_lap[side, i, place, 0:8, :] = nothing
            cap_lap[side, i, place, 8:16, :] = nothing
        opp = jnp.broadcast_to(ref[base + 5 * n : base + 5 * n + 1, :], (8, LANES))
        cap_opp[side, place] = lax.rem(opp.astype(jnp.int32), LANES)

    def cap_weigh():
        for side in (0, 1):
            for start in (0, 1):
                seas = [cap_stat[side, 0, k, start : start + 8, :] for k in range(ARC)]
                east, west = arc_neighbours(seas)
                for k in range(ARC):
                    north = cap_stat[side, 0, k, start + 1 : start + 9, :]
                    if start:
                        south = cap_stat[side, 0, k, start - 1 : start + 7, :]
                        cap_stat[side, 1, k, 1:9, :] = (east[k] + west[k]) + (north + south)
                    cap_stat[side, 2, k, start : start + 8, :] = seas[k] * east[k]
                    cap_stat[side, 3, k, start : start + 8, :] = seas[k] * north

    def cap_first(side, low, high):
        ratio = EXPAND / CONTRACT
        span = range(low - 1, high + 1)
        fields = []
        for i in range(FIELDS):
            blocks = [cap[side, i, k, 1:9, :] for k in span]
            fields.append((blocks, *arc_neighbours(blocks)))
        for n, k in enumerate(span):
            b, be = [f[0][n - 1] for f in fields], [f[1][n - 1] for f in fields]
            w_e = cap_stat[side, 2, max(k - 1, 0), 1:9, :]
            flow = w_e * (b[2] + be[2])
            faces = [flow * (b[i] + be[i]) for i in (0, 1)]
            faces.append(w_e * ((be[1] - ratio * be[0]) - (b[1] - ratio * b[0])))
            lap, partial = first_pass(
                [f[0][n] for f in fields],
                [cap[side, i, k, 2:10, :] for i in range(FIELDS)],
                [cap[side, i, k, 0:8, :] for i in range(FIELDS)],
                [f[1][n] for f in fields],
                [f[2][n] for f in fields],
                cap_stat[side, 0, k, 1:9, :],
                cap_stat[side, 1, k, 1:9, :],
                cap_stat[side, 2, k, 1:9, :],
                cap_stat[side, 3, k, 1:9, :],
                cap_stat[side, 3, k, 0:8, :],
                cap_turn,
                [
                    lambda x, face=face: roll(jnp.where(lane == LANES - 1, face, x), 1)
                    for face in faces
                ],
            )
            for i in range(FIELDS):
                cap_lap[side, i, k, 1:9, :] = lap[i]
                if low <= k < high:
                    cap_part[side, i, k, 0:8, :] = partial[i]

    def cap_second(side, low, high):
        for i in range(FIELDS):
            blocks = [cap_lap[side, i, k, 1:9, :] for k in range(low - 1, high + 1)]
            east, west = arc_neighbours(blocks)
            for n, k in enumerate(range(low - 1, high + 1)):
                if low <= k < high:
                    cap[side, i, k, 1:9, :] = second_pass(
                        cap_part[side, i, k, 0:8, :],
                        blocks[n],
                        cap_lap[side, i, k, 2:10, :],
                        cap_lap[side, i, k, 0:8, :],
                        east[n],
                        west[n],
                        cap_stat[side, 0, k, 1:9, :],
                        cap_stat[side, 1, k, 1:9, :],
                    )

    @pl.when(is_top())
    def _():
        parts = [(j, side, w3_ref, base, n) for j, side, n, base in far_places(FAR_ROWS)]
        parts += [
            (j + REACH + 2, side, e3_ref, base, n)
            for j, side, n, base in far_places(FAR_ROWS[::-1])
        ]
        for side in (0, 1):
            parts.append((REACH - 1, side, rw_ref, 40 + CAP * side, 8))
            parts.append((REACH, side, (sb_ref, rb_ref)[side], 0, 8))
            parts.append((REACH + 1, side, re_ref, 40 + CAP * side, 8))
        for k, side, ref, base, n in parts:
            put_block(side, ARC - 1 - k if side else k, ref, base, n)
        bands.pad()
        for which in (0, 1):
            row = 8 + UPPER * which
            for i in range(FIELDS):
                state[i, row : row + UPPER, :] = upper_state[i, which]
            for i in range(5):
                stat[i, row : row + UPPER, :] = upper_stat[i, which]
        fill_ghosts(cap_stat, (1.0,), 0, ARC, 2)
        fill_ghosts(cap, PARITY, 0, ARC, 2)
        cap_weigh()
        for n in range(STEPS - 1):
            low, high = n + 1, ARC - 1 - n
            first_side = 1 if n == STEPS - 2 else 0

            def one(side, carry, low=low, high=high):
                cap_first(side, low, high)
                cap_second(side, low, high)
                return carry

            lax.fori_loop(first_side, 2, one, 0)
            fill_ghosts(cap, PARITY, low, high, 2 - first_side)
            for i in range(FIELDS):
                ghosts = [cap[0, i, k, 8:10, :] for k in (REACH - 1, REACH, REACH + 1)]
                for which, ghost in enumerate(shifted_ghosts(ghosts)):
                    row = 8 + UPPER * (which + 1) - HALO
                    state[i, row : row + 2, :] = ghost
            bands.step(bands.tiles)
        copies = []
        for i, out in enumerate((t_out, s_out, u_out, v_out)):
            row = 8 + UPPER - 2 * HALO
            west, east = state[i, row : row + 8, :], state[i, row + UPPER : row + UPPER + 8, :]
            rows_out[i] = jnp.where(lane < LANES // 2, roll(west, -HALO), roll(east, HALO))
            copies.append(
                pltpu.make_async_copy(
                    rows_out.at[i], out.at[0, pl.ds(height - HALO, HALO), :], sems.at[i]
                )
            )
        for copy in copies:
            copy.start()
        for copy in copies:
            copy.wait()


def body(lon_count, lat_count, t, s, u, v, m, opp):
    fields = (t, s, u, v, m)
    height = t.shape[1]
    vmem, anywhere = (
        pl.BlockSpec(memory_space=pltpu.VMEM),
        pl.BlockSpec(memory_space=pltpu.HBM),
    )
    f32, i32 = jnp.float32, jnp.int32

    def call(kernel, inputs, shapes, scratch=(), far=0, room=32 * 1024, flops=0):
        return pl.pallas_call(
            kernel,
            out_shape=[jax.ShapeDtypeStruct(shape, f32) for shape in shapes],
            in_specs=[anywhere] * far + [vmem] * (len(inputs) - far),
            out_specs=[vmem] * len(shapes),
            scratch_shapes=list(scratch),
            compiler_params=pltpu.CompilerParams(vmem_limit_bytes=(64 * 1024 - room) * 1024),
            cost_estimate=pl.CostEstimate(flops=flops, bytes_accessed=flops, transcendentals=0),
        )(*inputs)

    def place(lon, lat):
        return (lon % lon_count) * lat_count + lat

    lons, lats = range(lon_count), range(lat_count)
    last = lat_count - 1
    pairs_a = [(place(i, j), place(i, j ^ 1)) for i in lons for j in lats]
    pairs_b = [(place(i, j), place(i, ((j - 1) ^ 1) + 1)) for i in lons for j in lats[1:last]]
    pairs_b += [(place(i, last), place(-i, last)) for i in lons]

    def shift(x, by, rows):
        pairs = [(place(i, j), place(i + by, j)) for i in lons for j in rows]
        return lax.ppermute(x, ("lon", "lat"), pairs)

    (send_b,) = call(
        fold_rows_kernel,
        (*fields, opp.reshape(1, LANES)),
        [(CAP, LANES)],
        [pltpu.VMEM((16, LANES), i32), pltpu.SemaphoreType.DMA((6,))],
        far=6,
        room=64,
    )
    from_b = lax.ppermute(send_b, ("lon", "lat"), pairs_b)
    stack, send_a = call(
        load_kernel,
        (*fields, send_b),
        [(5, height, LANES), (CAP, LANES)],
        [pltpu.VMEM((height, LANES), i32), pltpu.SemaphoreType.DMA((5,))],
        far=5,
        room=384,
    )
    from_a = lax.ppermute(send_a, ("lon", "lat"), pairs_a)
    wide = 40 + 2 * CAP
    send_e, send_w = call(columns_kernel, (stack, send_b, from_a, from_b), [(wide, LANES)] * 2)
    from_w = shift(send_e, 1, lats)
    from_e = shift(send_w, -1, lats)
    send_far_e, send_far_w = call(
        far_kernel, (send_b, from_b, from_w, from_e), [(FAR, LANES)] * 2
    )
    far_w = shift(send_far_e, 3, [last])
    far_e = shift(send_far_w, -3, [last])

    def band_scratch(rows):
        return [pltpu.VMEM((n, 16 + 2 * rows, LANES), f32) for n in (FIELDS, FIELDS, FIELDS, 5)]

    *outs, upper_state, upper_stat = call(
        main_kernel,
        (stack, send_b, from_a, from_b, from_w, from_e),
        [t.shape] * 4 + [(FIELDS, 2, UPPER, LANES), (5, 2, UPPER, LANES)],
        band_scratch(height + 2 * HALO),
        flops=10**7,
    )
    return tuple(
        pl.pallas_call(
            cap_kernel,
            out_shape=[jax.ShapeDtypeStruct(t.shape, f32)] * 4,
            in_specs=[anywhere] * 4 + [vmem] * 8,
            out_specs=[anywhere] * 4,
            scratch_shapes=band_scratch(UPPER)
            + [
                pltpu.VMEM((2, FIELDS, ARC, 16, LANES), f32),
                pltpu.VMEM((2, FIELDS, ARC, 16, LANES), f32),
                pltpu.VMEM((2, FIELDS, ARC, 8, LANES), f32),
                pltpu.VMEM((2, 4, ARC, 16, LANES), f32),
                pltpu.VMEM((2, ARC, 8, LANES), i32),
                pltpu.VMEM((FIELDS, 8, LANES), f32),
                pltpu.SemaphoreType.DMA((FIELDS,)),
            ],
            input_output_aliases={i: i for i in range(4)},
            compiler_params=pltpu.CompilerParams(vmem_limit_bytes=32 * 1024 * 1024),
        )(*outs, upper_state, upper_stat, send_b, from_b, from_w, from_e, far_w, far_e)
    )


def solution(mesh):
    placed = P(None, "lat", "lon")
    return jax.shard_map(
        functools.partial(body, mesh.shape["lon"], mesh.shape["lat"]),
        mesh=mesh,
        in_specs=(placed,) * 5 + (P("lon"),),
        out_specs=(placed,) * 4,
        check_vma=False,
    )
```

```python
import functools

import jax
import jax.numpy as jnp
from jax import lax
from jax.experimental import pallas as pl
from jax.experimental.pallas import tpu as pltpu
from jax.sharding import PartitionSpec as P

STEPS = 4
TIME_STEP = 0.1
DIFFUSE = 0.15
EXPAND = 0.2
CONTRACT = 0.8
ROTATION = 0.5

HALO = 2 * STEPS
LANES = 128
FIELDS = 4
REACH = 4
ARC = 2 * REACH + 1
CAP = 48
PARITY = (1.0, 1.0, -1.0, -1.0)
GROUP = 14
FAR_ROWS = (2, 4, 6)
FAR = 128
UPPER = 24


def lane_index(rows=8):
    return lax.broadcasted_iota(jnp.int32, (rows, LANES), 1)


def roll(x, shift):
    shift = shift % LANES
    return x if shift == 0 else pltpu.roll(x, shift, 1)


def is_odd():
    return lax.rem(lax.axis_index("lat"), 2) == 1


def is_top():
    return lax.axis_index("lat") == lax.axis_size("lat") - 1


def fold_rows_kernel(t_ref, s_ref, u_ref, v_ref, m_ref, opp_ref, out, ints, sems):
    start = t_ref.shape[1] - HALO
    copies = [pltpu.make_async_copy(opp_ref, ints.at[pl.ds(8, 1), :], sems.at[5])]
    for i, ref in enumerate((t_ref, s_ref, u_ref, v_ref, m_ref)):
        target = out.at[pl.ds(8 * i, 8), :] if i < FIELDS else ints.at[pl.ds(0, 8), :]
        copies.append(
            pltpu.make_async_copy(ref.at[0, pl.ds(start, HALO), :], target, sems.at[i])
        )
    for copy in copies:
        copy.start()
    for copy in copies:
        copy.wait()
    out[32:40, :] = ints[0:8, :].astype(jnp.float32)
    out[40:48, :] = jnp.broadcast_to(ints[8:9, :].astype(jnp.float32), (8, LANES))


def load_kernel(t_ref, s_ref, u_ref, v_ref, m_ref, after, fields, e_ref, w_ref, ints, sems):
    copies = []
    for i, ref in enumerate((t_ref, s_ref, u_ref, v_ref, m_ref)):
        target = fields.at[i] if i < FIELDS else ints
        copies.append(pltpu.make_async_copy(ref.at[0], target, sems.at[i]))
    for copy in copies:
        copy.start()
    for copy in copies:
        copy.wait()
    fields[FIELDS] = ints[...].astype(jnp.float32)
    lane = lane_index()
    for i in range(5):
        east = jnp.zeros((8, LANES), jnp.float32)
        west = jnp.zeros((8, LANES), jnp.float32)
        for g in range(fields.shape[1] // 8):
            tile = fields[i, 8 * g : 8 * g + 8, :]
            here = (lane >= 8 * g) & (lane < 8 * g + 8)
            east = jnp.where(here, roll(tile, 8 * g - (LANES - HALO)), east)
            west = jnp.where(here, roll(tile, 8 * g), west)
        e_ref[i * 8 : i * 8 + 8, :] = east
        w_ref[i * 8 : i * 8 + 8, :] = west


def pair_kernel(e_in, w_in, sb_ref, rb_ref, e_ref, w_ref):
    for ref, columns in ((e_ref, e_in), (w_ref, w_in)):
        ref[0:40, :] = columns[...]

        @pl.when(is_top())
        def _(ref=ref):
            ref[40 : 40 + CAP, :] = sb_ref[...]
            ref[40 + CAP : 40 + 2 * CAP, :] = rb_ref[...]


def rows_kernel(fields, rw_ref, re_ref, after, a_ref, b_ref):
    odd = is_odd()
    lane = lane_index()
    height = fields.shape[1]
    north_lanes = height - HALO
    corners = [jnp.zeros((8, LANES), jnp.float32)] * 2
    for i in range(5):
        south, north = fields[i, 0:HALO, :], fields[i, height - HALO : height, :]
        a_ref[i * 8 : i * 8 + 8, :] = jnp.where(odd, south, north)
        b_ref[i * 8 : i * 8 + 8, :] = jnp.where(odd, north, south)
        for ref, at in ((rw_ref, 16 * i), (re_ref, 16 * i + 8)):
            columns = ref[i * 8 : i * 8 + 8, :]
            here = (lane >= at) & (lane < at + 8)
            corners = [
                jnp.where(here, roll(columns, at - start), corner)
                for start, corner in zip((0, north_lanes), corners)
            ]
    a_ref[40:48, :] = jnp.where(odd, corners[0], corners[1])
    b_ref[40:48, :] = jnp.where(odd, corners[1], corners[0])


def far_places(counts):
    base = 0
    for j, n in enumerate(counts):
        for side in (0, 1):
            yield j, side, n, base
            base += 5 * n + 1


def far_kernel(sb_ref, rb_ref, rw_ref, re_ref, e_ref, w_ref):
    @pl.when(is_top())
    def _():
        sources = (
            ((rw_ref, 40), (rw_ref, 40 + CAP)),
            ((sb_ref, 0), (rb_ref, 0)),
            ((re_ref, 40), (re_ref, 40 + CAP)),
        )
        for out, counts in ((e_ref, FAR_ROWS), (w_ref, FAR_ROWS[::-1])):
            for j, side, n, base in far_places(counts):
                ref, at = sources[j][side]
                for i in range(5):
                    out[base + i * n : base + i * n + n, :] = ref[
                        at + 8 * i + 8 - n : at + 8 * i + 8, :
                    ]
                out[base + 5 * n : base + 5 * n + 1, :] = ref[at + 40 : at + 41, :]
            out[FAR - 2 : FAR, :] = jnp.zeros((2, LANES), jnp.float32)


def first_pass(centre, north, south, east, west, sea, count, w_e, w_n, w_s, turn, roll_w):
    laps = [
        sea * (((east[i] + west[i]) + (north[i] + south[i])) - count * centre[i])
        for i in range(FIELDS)
    ]
    t, s, u, v = centre
    flow_e = w_e * (u + east[2])
    flow_n = w_n * (v + north[3])
    flow_s = w_s * (v + south[3])
    partial = []
    for i in (0, 1):
        c = centre[i]
        x = flow_e * (c + east[i])
        y = flow_n * (c + north[i]) - flow_s * (c + south[i])
        partial.append(c - (0.25 * TIME_STEP) * ((x - roll_w[i](x)) + y))
    ratio = EXPAND / CONTRACT
    slope = 0.25 * TIME_STEP * CONTRACT
    q = s - ratio * t
    q_e = east[1] - ratio * east[0]
    q_n = north[1] - ratio * north[0]
    q_s = south[1] - ratio * south[0]
    d = w_e * (q_e - q)
    partial.append(u + (turn * v - slope * (d + roll_w[2](d))))
    partial.append(v - (turn * u + slope * (w_n * (q_n - q) + w_s * (q - q_s))))
    return laps, partial


def second_pass(partial, lap, north, south, east, west, sea, count):
    mix = ((east + west) + (north + south)) - count * lap
    return sea * (partial - (TIME_STEP * DIFFUSE) * mix)


class Band:
    def __init__(self, state, laps, part, stat):
        self.state, self.laps, self.part, self.stat = state, laps, part, stat
        self.tiles = state.shape[1] // 8 - 2

    def pad(self):
        nothing = jnp.zeros((8, LANES), jnp.float32)
        for row in (0, 8 + 8 * self.tiles):
            for i in range(FIELDS):
                self.state[i, row : row + 8, :] = nothing
                self.laps[i, row : row + 8, :] = nothing
            for i in range(4):
                self.stat[i, row : row + 8, :] = nothing

    def each_tile(self, work, group):
        def trip(n, carry):
            start = pl.multiple_of(8 + 8 * group * n, 8)
            for j in range(group):
                work(start + 8 * j)
            return carry

        lax.fori_loop(0, self.tiles // group, trip, 0)

    def weigh(self, turning):
        def work(r):
            sea = self.stat[0, pl.ds(r, 8), :]
            north = self.stat[0, pl.ds(r + 1, 8), :]
            south = self.stat[0, pl.ds(r - 1, 8), :]
            east, west = roll(sea, -1), roll(sea, 1)
            self.stat[1, pl.ds(r, 8), :] = (east + west) + (north + south)
            self.stat[2, pl.ds(r, 8), :] = sea * east
            self.stat[3, pl.ds(r, 8), :] = sea * north
            self.stat[4, pl.ds(r, 8), :] = turning(r)
            for i in range(FIELDS):
                self.state[i, pl.ds(r, 8), :] = sea * self.state[i, pl.ds(r, 8), :]

        return work

    def first(self, r):
        def rows(ref, i, by=0):
            return ref[i, pl.ds(r + by, 8), :]

        centre = [rows(self.state, i) for i in range(FIELDS)]
        lap, partial = first_pass(
            centre,
            [rows(self.state, i, 1) for i in range(FIELDS)],
            [rows(self.state, i, -1) for i in range(FIELDS)],
            [roll(x, -1) for x in centre],
            [roll(x, 1) for x in centre],
            rows(self.stat, 0),
            rows(self.stat, 1),
            rows(self.stat, 2),
            rows(self.stat, 3),
            rows(self.stat, 3, -1),
            rows(self.stat, 4),
            (lambda x: roll(x, 1),) * 3,
        )
        for i in range(FIELDS):
            self.laps[i, pl.ds(r, 8), :] = lap[i]
            self.part[i, pl.ds(r, 8), :] = partial[i]

    def second(self, r):
        sea, count = self.stat[0, pl.ds(r, 8), :], self.stat[1, pl.ds(r, 8), :]
        for i in range(FIELDS):
            lap = self.laps[i, pl.ds(r, 8), :]
            self.state[i, pl.ds(r, 8), :] = second_pass(
                self.part[i, pl.ds(r, 8), :],
                lap,
                self.laps[i, pl.ds(r + 1, 8), :],
                self.laps[i, pl.ds(r - 1, 8), :],
                roll(lap, -1),
                roll(lap, 1),
                sea,
                count,
            )

    def step(self, group):
        self.each_tile(self.first, group)
        self.each_tile(self.second, group)


def shifted_ghosts(blocks):
    before, here, after = blocks
    lane = lane_index(here.shape[0])
    return (
        jnp.where(lane < HALO, roll(before, HALO), roll(here, HALO)),
        jnp.where(lane >= LANES - HALO, roll(after, -HALO), roll(here, -HALO)),
    )


def turning_of(row, total_rows):
    return (TIME_STEP * ROTATION) * (2.0 * (row + 0.5) / total_rows - 1.0)


def row_in_tile():
    return lax.broadcasted_iota(jnp.int32, (8, LANES), 0).astype(jnp.float32)


def main_kernel(
    fields,
    sb_ref,
    fold_ref,
    ra_ref,
    rb_ref,
    rw_ref,
    re_ref,
    t_out,
    s_out,
    u_out,
    v_out,
    upper_state,
    upper_stat,
    state,
    laps,
    part,
    stat,
):
    odd, top = is_odd(), is_top()
    lane = lane_index()
    height = fields.shape[1]
    total_rows = height * lax.axis_size("lat")
    tiles_n = height // 8 + 2
    band = 8 * tiles_n
    bands = Band(state, laps, part, stat)

    south_corner = jnp.where(odd, ra_ref[40:48, :], rb_ref[40:48, :])
    north_corner = jnp.where(odd, rb_ref[40:48, :], ra_ref[40:48, :])
    for i in range(5):
        ra, rb = ra_ref[i * 8 : i * 8 + 8, :], rb_ref[i * 8 : i * 8 + 8, :]
        from_w, from_e = rw_ref[i * 8 : i * 8 + 8, :], re_ref[i * 8 : i * 8 + 8, :]
        tiles = [(jnp.where(odd, ra, rb), south_corner, 16 * i, south_corner, 16 * i + 8)]
        for g in range(height // 8):
            tile = fields[i, 8 * g : 8 * g + 8, :]
            tiles.append((tile, from_w, 8 * g, from_e, 8 * g))
        tiles.append((jnp.where(odd, rb, ra), north_corner, 16 * i, north_corner, 16 * i + 8))
        ref, at = (state, i) if i < FIELDS else (stat, 0)
        for g, (tile, west, west_at, east, east_at) in enumerate(tiles):
            ref[at, 8 + 8 * g : 16 + 8 * g, :] = jnp.where(
                lane < HALO, roll(west, -west_at), roll(tile, HALO)
            )
            ref[at, 8 + band + 8 * g : 16 + band + 8 * g, :] = jnp.where(
                lane >= LANES - HALO, roll(east, LANES - HALO - east_at), roll(tile, -HALO)
            )
    bands.pad()

    @pl.when(top)
    def _():
        pairs = (
            (rw_ref, 40, rw_ref, 40 + CAP),
            (sb_ref, 0, fold_ref, 0),
            (re_ref, 40, re_ref, 40 + CAP),
        )
        for i in range(5):
            ghosts = []
            for own, own_at, facing, facing_at in pairs:
                index = lax.rem(own[own_at + 40 : own_at + 48, :].astype(jnp.int32), LANES)
                rows = facing[facing_at + 8 * i : facing_at + 8 * i + 8, :]
                ghosts.append(
                    (PARITY + (1.0,))[i]
                    * jnp.take_along_axis(rows, index, axis=1, mode="promise_in_bounds")
                )
            ref, at = (state, i) if i < FIELDS else (stat, 0)
            for which, ghost in enumerate(shifted_ghosts(ghosts)):
                row = 8 + band * (which + 1) - HALO
                ref[at, row : row + 1, :] = ghost[7:8, :]
                ref[at, row + 1 : row + 2, :] = ghost[6:7, :]

    base_row = (lax.axis_index("lat") * height - HALO).astype(jnp.float32)
    sub = row_in_tile()
    bands.each_tile(
        bands.weigh(
            lambda r: turning_of(
                base_row + lax.rem(r - 8, band).astype(jnp.float32) + sub, total_rows
            )
        ),
        GROUP,
    )

    def step(n, carry):
        bands.step(GROUP)

        @pl.when(top & (n == 0))
        def _():
            for which in (0, 1):
                row = 8 + band * (which + 1) - UPPER
                for i in range(FIELDS):
                    upper_state[i, which] = state[i, row : row + UPPER, :]
                for i in range(5):
                    upper_stat[i, which] = stat[i, row : row + UPPER, :]

        return carry

    lax.fori_loop(0, STEPS, step, 0)

    for i, out in enumerate((t_out, s_out, u_out, v_out)):
        for g in range(height // 8):
            r = 8 + HALO + 8 * g
            west, east = state[i, r : r + 8, :], state[i, r + band : r + band + 8, :]
            out[0, 8 * g : 8 * g + 8, :] = jnp.where(
                lane < LANES // 2, roll(west, -HALO), roll(east, HALO)
            )


def arc_neighbours(blocks):
    lane = lane_index()
    last = len(blocks) - 1
    e, w = [roll(x, -1) for x in blocks], [roll(x, 1) for x in blocks]
    east = [jnp.where(lane == LANES - 1, e[min(k + 1, last)], e[k]) for k in range(last + 1)]
    west = [jnp.where(lane == 0, w[max(k - 1, 0)], w[k]) for k in range(last + 1)]
    return east, west


def cap_kernel(
    t_in,
    s_in,
    u_in,
    v_in,
    upper_state,
    upper_stat,
    sb_ref,
    rb_ref,
    rw_ref,
    re_ref,
    w3_ref,
    e3_ref,
    t_out,
    s_out,
    u_out,
    v_out,
    state,
    laps,
    part,
    stat,
    cap,
    cap_lap,
    cap_part,
    cap_stat,
    cap_opp,
    rows_out,
    sems,
):
    lane = lane_index()
    height = t_out.shape[1]
    total_rows = height * lax.axis_size("lat")
    bands = Band(state, laps, part, stat)
    nothing = jnp.zeros((8, LANES), jnp.float32)
    cap_turn = turning_of(float(total_rows - HALO + 1) + row_in_tile(), total_rows)

    def fill_ghosts(ref, parities, low, high, sides):
        def one(side, carry):
            ghosts = {}
            for k in range(low, high):
                index = cap_opp[side, k]
                for i, parity in enumerate(parities):
                    rows = ref[1 - side, i, ARC - 1 - k, 0:8, :]
                    ghosts[k, i] = parity * jnp.take_along_axis(
                        rows, index, axis=1, mode="promise_in_bounds"
                    )
            for (k, i), ghost in ghosts.items():
                ref[side, i, k, 8:9, :] = ghost[7:8, :]
                ref[side, i, k, 9:10, :] = ghost[6:7, :]
            return carry

        lax.fori_loop(0, sides, one, 0)

    def put_block(side, place, ref, base, n):
        sea = ref[base + 4 * n : base + 5 * n, :]
        cap_stat[side, 0, place, 8 - n : 8, :] = sea
        cap_stat[side, 0, place, 10:16, :] = nothing[0:6]
        if n < 8:
            cap_stat[side, 0, place, 0 : 8 - n, :] = nothing[n:8]
        for i in range(FIELDS):
            cap[side, i, place, 8 - n : 8, :] = sea * ref[base + n * i : base + n * i + n, :]
            if n < 8:
                cap[side, i, place, 0 : 8 - n, :] = nothing[n:8]
            cap[side, i, place, 10:16, :] = nothing[0:6]
            cap_lap[side, i, place, 0:8, :] = nothing
            cap_lap[side, i, place, 8:16, :] = nothing
        opp = jnp.broadcast_to(ref[base + 5 * n : base + 5 * n + 1, :], (8, LANES))
        cap_opp[side, place] = lax.rem(opp.astype(jnp.int32), LANES)

    def cap_weigh():
        for side in (0, 1):
            for start in (0, 1):
                seas = [cap_stat[side, 0, k, start : start + 8, :] for k in range(ARC)]
                east, west = arc_neighbours(seas)
                for k in range(ARC):
                    north = cap_stat[side, 0, k, start + 1 : start + 9, :]
                    if start:
                        south = cap_stat[side, 0, k, start - 1 : start + 7, :]
                        cap_stat[side, 1, k, 1:9, :] = (east[k] + west[k]) + (north + south)
                    cap_stat[side, 2, k, start : start + 8, :] = seas[k] * east[k]
                    cap_stat[side, 3, k, start : start + 8, :] = seas[k] * north

    def cap_first(side, low, high):
        ratio = EXPAND / CONTRACT
        span = range(low - 1, high + 1)
        fields = []
        for i in range(FIELDS):
            blocks = [cap[side, i, k, 1:9, :] for k in span]
            fields.append((blocks, *arc_neighbours(blocks)))
        for n, k in enumerate(span):
            b, be = [f[0][n - 1] for f in fields], [f[1][n - 1] for f in fields]
            w_e = cap_stat[side, 2, max(k - 1, 0), 1:9, :]
            flow = w_e * (b[2] + be[2])
            faces = [flow * (b[i] + be[i]) for i in (0, 1)]
            faces.append(w_e * ((be[1] - ratio * be[0]) - (b[1] - ratio * b[0])))
            lap, partial = first_pass(
                [f[0][n] for f in fields],
                [cap[side, i, k, 2:10, :] for i in range(FIELDS)],
                [cap[side, i, k, 0:8, :] for i in range(FIELDS)],
                [f[1][n] for f in fields],
                [f[2][n] for f in fields],
                cap_stat[side, 0, k, 1:9, :],
                cap_stat[side, 1, k, 1:9, :],
                cap_stat[side, 2, k, 1:9, :],
                cap_stat[side, 3, k, 1:9, :],
                cap_stat[side, 3, k, 0:8, :],
                cap_turn,
                [
                    lambda x, face=face: roll(jnp.where(lane == LANES - 1, face, x), 1)
                    for face in faces
                ],
            )
            for i in range(FIELDS):
                cap_lap[side, i, k, 1:9, :] = lap[i]
                if low <= k < high:
                    cap_part[side, i, k, 0:8, :] = partial[i]

    def cap_second(side, low, high):
        for i in range(FIELDS):
            blocks = [cap_lap[side, i, k, 1:9, :] for k in range(low - 1, high + 1)]
            east, west = arc_neighbours(blocks)
            for n, k in enumerate(range(low - 1, high + 1)):
                if low <= k < high:
                    cap[side, i, k, 1:9, :] = second_pass(
                        cap_part[side, i, k, 0:8, :],
                        blocks[n],
                        cap_lap[side, i, k, 2:10, :],
                        cap_lap[side, i, k, 0:8, :],
                        east[n],
                        west[n],
                        cap_stat[side, 0, k, 1:9, :],
                        cap_stat[side, 1, k, 1:9, :],
                    )

    @pl.when(is_top())
    def _():
        parts = [(j, side, w3_ref, base, n) for j, side, n, base in far_places(FAR_ROWS)]
        parts += [
            (j + REACH + 2, side, e3_ref, base, n)
            for j, side, n, base in far_places(FAR_ROWS[::-1])
        ]
        for side in (0, 1):
            parts.append((REACH - 1, side, rw_ref, 40 + CAP * side, 8))
            parts.append((REACH, side, (sb_ref, rb_ref)[side], 0, 8))
            parts.append((REACH + 1, side, re_ref, 40 + CAP * side, 8))
        for k, side, ref, base, n in parts:
            put_block(side, ARC - 1 - k if side else k, ref, base, n)
        bands.pad()
        for which in (0, 1):
            row = 8 + UPPER * which
            for i in range(FIELDS):
                state[i, row : row + UPPER, :] = upper_state[i, which]
            for i in range(5):
                stat[i, row : row + UPPER, :] = upper_stat[i, which]
        fill_ghosts(cap_stat, (1.0,), 0, ARC, 2)
        fill_ghosts(cap, PARITY, 0, ARC, 2)
        cap_weigh()
        for n in range(STEPS - 1):
            low, high = n + 1, ARC - 1 - n
            first_side = 1 if n == STEPS - 2 else 0

            def one(side, carry, low=low, high=high):
                cap_first(side, low, high)
                cap_second(side, low, high)
                return carry

            lax.fori_loop(first_side, 2, one, 0)
            fill_ghosts(cap, PARITY, low, high, 2 - first_side)
            for i in range(FIELDS):
                ghosts = [cap[0, i, k, 8:10, :] for k in (REACH - 1, REACH, REACH + 1)]
                for which, ghost in enumerate(shifted_ghosts(ghosts)):
                    row = 8 + UPPER * (which + 1) - HALO
                    state[i, row : row + 2, :] = ghost
            bands.step(bands.tiles)
        copies = []
        for i, out in enumerate((t_out, s_out, u_out, v_out)):
            row = 8 + UPPER - 2 * HALO
            west, east = state[i, row : row + 8, :], state[i, row + UPPER : row + UPPER + 8, :]
            rows_out[i] = jnp.where(lane < LANES // 2, roll(west, -HALO), roll(east, HALO))
            copies.append(
                pltpu.make_async_copy(
                    rows_out.at[i], out.at[0, pl.ds(height - HALO, HALO), :], sems.at[i]
                )
            )
        for copy in copies:
            copy.start()
        for copy in copies:
            copy.wait()


def body(lon_count, lat_count, t, s, u, v, m, opp):
    fields = (t, s, u, v, m)
    height = t.shape[1]
    vmem, anywhere = (
        pl.BlockSpec(memory_space=pltpu.VMEM),
        pl.BlockSpec(memory_space=pltpu.HBM),
    )
    f32, i32 = jnp.float32, jnp.int32

    def call(kernel, inputs, shapes, scratch=(), far=0, flops=0):
        inputs = [
            pltpu.with_memory_space_constraint(x, pltpu.HBM) if i < far else x
            for i, x in enumerate(inputs)
        ]
        return pl.pallas_call(
            kernel,
            out_shape=[jax.ShapeDtypeStruct(shape, f32) for shape in shapes],
            in_specs=[anywhere] * far + [vmem] * (len(inputs) - far),
            out_specs=[vmem] * len(shapes),
            scratch_shapes=list(scratch),
            compiler_params=pltpu.CompilerParams(vmem_limit_bytes=32 * 1024 * 1024),
            cost_estimate=pl.CostEstimate(flops=flops, bytes_accessed=flops, transcendentals=0),
        )(*inputs)

    def place(lon, lat):
        return (lon % lon_count) * lat_count + lat

    lons, lats = range(lon_count), range(lat_count)
    last = lat_count - 1
    pairs_a = [(place(i, j), place(i, j ^ 1)) for i in lons for j in lats]
    pairs_b = [(place(i, j), place(i, ((j - 1) ^ 1) + 1)) for i in lons for j in lats[1:last]]
    pairs_fold = [(place(i, last), place(-i, last)) for i in lons]

    def shift(x, by, rows):
        pairs = [(place(i, j), place(i + by, j)) for i in lons for j in rows]
        return lax.ppermute(x, ("lon", "lat"), pairs)

    def along_lat(x, pairs):
        return lax.ppermute(x, ("lon", "lat"), pairs)

    (top_rows,) = call(
        fold_rows_kernel,
        (*fields, opp.reshape(1, LANES)),
        [(CAP, LANES)],
        [pltpu.VMEM((16, LANES), i32), pltpu.SemaphoreType.DMA((6,))],
        far=6,
    )
    from_fold = along_lat(top_rows, pairs_fold)
    stack, columns_e, columns_w = call(
        load_kernel,
        (*fields, top_rows),
        [(5, height, LANES), (40, LANES), (40, LANES)],
        [pltpu.VMEM((height, LANES), i32), pltpu.SemaphoreType.DMA((5,))],
        far=5,
    )
    send_e, send_w = call(
        pair_kernel, (columns_e, columns_w, top_rows, from_fold), [(40 + 2 * CAP, LANES)] * 2
    )
    from_w = shift(send_e, 1, lats)
    from_e = shift(send_w, -1, lats)
    send_far_e, send_far_w = call(
        far_kernel, (top_rows, from_fold, from_w, from_e), [(FAR, LANES)] * 2
    )
    far_w = shift(send_far_e, 3, [last])
    far_e = shift(send_far_w, -3, [last])
    send_a, send_b = call(
        rows_kernel, (stack, from_w, from_e, send_far_e), [(CAP, LANES)] * 2
    )
    from_a = along_lat(send_a, pairs_a)
    from_b = along_lat(send_b, pairs_b)

    def band_scratch(rows):
        return [pltpu.VMEM((n, 16 + 2 * rows, LANES), f32) for n in (FIELDS, FIELDS, FIELDS, 5)]

    *outs, upper_state, upper_stat = call(
        main_kernel,
        (stack, top_rows, from_fold, from_a, from_b, from_w, from_e),
        [t.shape] * 4 + [(FIELDS, 2, UPPER, LANES), (5, 2, UPPER, LANES)],
        band_scratch(height + 2 * HALO),
        flops=10**7,
    )
    return tuple(
        pl.pallas_call(
            cap_kernel,
            out_shape=[jax.ShapeDtypeStruct(t.shape, f32)] * 4,
            in_specs=[anywhere] * 4 + [vmem] * 8,
            out_specs=[anywhere] * 4,
            scratch_shapes=band_scratch(UPPER)
            + [
                pltpu.VMEM((2, FIELDS, ARC, 16, LANES), f32),
                pltpu.VMEM((2, FIELDS, ARC, 16, LANES), f32),
                pltpu.VMEM((2, FIELDS, ARC, 8, LANES), f32),
                pltpu.VMEM((2, 4, ARC, 16, LANES), f32),
                pltpu.VMEM((2, ARC, 8, LANES), i32),
                pltpu.VMEM((FIELDS, 8, LANES), f32),
                pltpu.SemaphoreType.DMA((FIELDS,)),
            ],
            input_output_aliases={i: i for i in range(4)},
            compiler_params=pltpu.CompilerParams(vmem_limit_bytes=32 * 1024 * 1024),
        )(*outs, upper_state, upper_stat, top_rows, from_fold, from_w, from_e, far_w, far_e)
    )


def solution(mesh):
    placed = P(None, "lat", "lon")
    return jax.shard_map(
        functools.partial(body, mesh.shape["lon"], mesh.shape["lat"]),
        mesh=mesh,
        in_specs=(placed,) * 5 + (P("lon"),),
        out_specs=(placed,) * 4,
        check_vma=False,
    )
```

```python
import functools

import jax
import jax.numpy as jnp
from jax import lax
from jax.experimental import pallas as pl
from jax.experimental.pallas import tpu as pltpu
from jax.sharding import PartitionSpec as P

STEPS = 4
TIME_STEP = 0.1
DIFFUSE = 0.15
EXPAND = 0.2
CONTRACT = 0.8
ROTATION = 0.5

HALO = 2 * STEPS
LANES = 128
FIELDS = 4
REACH = 4
ARC = 2 * REACH + 1
CAP = 48
PARITY = (1.0, 1.0, -1.0, -1.0)
GROUP = 14
FAR_ROWS = (2, 4, 6)
FAR = 128
UPPER = 24


def lane_index(rows=8):
    return lax.broadcasted_iota(jnp.int32, (rows, LANES), 1)


def roll(x, shift):
    shift = shift % LANES
    return x if shift == 0 else pltpu.roll(x, shift, 1)


def is_odd():
    return lax.rem(lax.axis_index("lat"), 2) == 1


def is_top():
    return lax.axis_index("lat") == lax.axis_size("lat") - 1


def is_odd_lon():
    return lax.rem(lax.axis_index("lon"), 2) == 1


class Either:
    def __init__(self, flag, yes, no):
        self.flag, self.yes, self.no = flag, yes, no

    def __getitem__(self, index):
        return jnp.where(self.flag, self.yes[index], self.no[index])


def first_rows_kernel(t_ref, s_ref, u_ref, v_ref, m_ref, opp_ref, out, ints, sems):
    start = pl.multiple_of(jnp.where(is_odd(), t_ref.shape[1] - HALO, 0), 8)
    copies = [pltpu.make_async_copy(opp_ref, ints.at[pl.ds(8, 1), :], sems.at[5])]
    for i, ref in enumerate((t_ref, s_ref, u_ref, v_ref, m_ref)):
        target = out.at[pl.ds(8 * i, 8), :] if i < FIELDS else ints.at[pl.ds(0, 8), :]
        copies.append(
            pltpu.make_async_copy(ref.at[0, pl.ds(start, HALO), :], target, sems.at[i])
        )
    for copy in copies:
        copy.start()
    for copy in copies:
        copy.wait()
    out[32:40, :] = ints[0:8, :].astype(jnp.float32)
    out[40:48, :] = jnp.broadcast_to(ints[8:9, :].astype(jnp.float32), (8, LANES))


def add_columns(e, w, tile, g):
    lane = lane_index()
    here = (lane >= 8 * g) & (lane < 8 * g + 8)
    e = jnp.where(here, roll(tile, 8 * g - (LANES - HALO)), e)
    return e, jnp.where(here, roll(tile, 8 * g), w)


def load_kernel(t_ref, s_ref, u_ref, v_ref, m_ref, after, fields, a_ref, e_ref, w_ref, ints, sems):
    height = fields.shape[1]
    copies = []
    for i, ref in enumerate((t_ref, s_ref, u_ref, v_ref, m_ref)):
        target = fields.at[i] if i < FIELDS else ints
        copies.append(pltpu.make_async_copy(ref.at[0], target, sems.at[i]))
    for copy in copies:
        copy.start()
    for copy in copies:
        copy.wait()
    fields[FIELDS] = ints[...].astype(jnp.float32)
    odd = is_odd()
    for i in range(5):
        south, north = fields[i, 0:HALO, :], fields[i, height - HALO : height, :]
        a_ref[i * 8 : i * 8 + 8, :] = jnp.where(odd, south, north)
        e = w = jnp.zeros((8, LANES), jnp.float32)
        for g in range(height // 8):
            e, w = add_columns(e, w, fields[i, 8 * g : 8 * g + 8, :], g + 1)
        e_ref[i * 8 : i * 8 + 8, :] = e
        w_ref[i * 8 : i * 8 + 8, :] = w


def pair_kernel(height, e_in, w_in, sb_ref, ra_ref, rb_ref, e_ref, w_ref):
    odd = is_odd()
    for i in range(5):
        at = slice(i * 8, i * 8 + 8)
        ra, rb = ra_ref[at, :], rb_ref[at, :]
        e, w = add_columns(e_in[at, :], w_in[at, :], jnp.where(odd, ra, rb), 0)
        e, w = add_columns(e, w, jnp.where(odd, rb, ra), height // 8 + 1)
        e_ref[at, :], w_ref[at, :] = e, w

    @pl.when(is_top())
    def _():
        for ref in (e_ref, w_ref):
            ref[40 : 40 + CAP, :] = sb_ref[...]
            ref[40 + CAP : 40 + 2 * CAP, :] = rb_ref[...]


def far_places(counts):
    base = 0
    for j, n in enumerate(counts):
        for side in (0, 1):
            yield j, side, n, base
            base += 5 * n + 1


def far_kernel(sb_ref, rb_ref, rw_ref, re_ref, first, second):
    @pl.when(is_top())
    def _():
        far_flag = jnp.logical_not(is_odd_lon())
        sources = (
            ((rw_ref, 40), (rw_ref, 40 + CAP)),
            ((sb_ref, 0), (rb_ref, 0)),
            ((re_ref, 40), (re_ref, 40 + CAP)),
        )

        def fill(out, counts):
            for j, side, n, base in far_places(counts):
                ref, at = sources[j][side]
                for i in range(5):
                    out[base + i * n : base + i * n + n, :] = ref[
                        at + 8 * i + 8 - n : at + 8 * i + 8, :
                    ]
                out[base + 5 * n : base + 5 * n + 1, :] = ref[at + 40 : at + 41, :]
            out[FAR - 2 : FAR, :] = jnp.zeros((2, LANES), jnp.float32)

        @pl.when(far_flag)
        def _():
            fill(first, FAR_ROWS)
            fill(second, FAR_ROWS[::-1])

        @pl.when(jnp.logical_not(far_flag))
        def _():
            fill(first, FAR_ROWS[::-1])
            fill(second, FAR_ROWS)


def first_pass(centre, north, south, east, west, sea, count, w_e, w_n, w_s, turn, roll_w):
    laps = [
        sea * (((east[i] + west[i]) + (north[i] + south[i])) - count * centre[i])
        for i in range(FIELDS)
    ]
    t, s, u, v = centre
    flow_e = w_e * (u + east[2])
    flow_n = w_n * (v + north[3])
    flow_s = w_s * (v + south[3])
    partial = []
    for i in (0, 1):
        c = centre[i]
        x = flow_e * (c + east[i])
        y = flow_n * (c + north[i]) - flow_s * (c + south[i])
        partial.append(c - (0.25 * TIME_STEP) * ((x - roll_w[i](x)) + y))
    ratio = EXPAND / CONTRACT
    slope = 0.25 * TIME_STEP * CONTRACT
    q = s - ratio * t
    q_e = east[1] - ratio * east[0]
    q_n = north[1] - ratio * north[0]
    q_s = south[1] - ratio * south[0]
    d = w_e * (q_e - q)
    partial.append(u + (turn * v - slope * (d + roll_w[2](d))))
    partial.append(v - (turn * u + slope * (w_n * (q_n - q) + w_s * (q - q_s))))
    return laps, partial


def second_pass(partial, lap, north, south, east, west, sea, count):
    mix = ((east + west) + (north + south)) - count * lap
    return sea * (partial - (TIME_STEP * DIFFUSE) * mix)


class Band:
    def __init__(self, state, laps, part, stat):
        self.state, self.laps, self.part, self.stat = state, laps, part, stat
        self.tiles = state.shape[1] // 8 - 2

    def pad(self):
        nothing = jnp.zeros((8, LANES), jnp.float32)
        for row in (0, 8 + 8 * self.tiles):
            for i in range(FIELDS):
                self.state[i, row : row + 8, :] = nothing
                self.laps[i, row : row + 8, :] = nothing
            for i in range(4):
                self.stat[i, row : row + 8, :] = nothing

    def each_tile(self, work, group):
        def trip(n, carry):
            start = pl.multiple_of(8 + 8 * group * n, 8)
            for j in range(group):
                work(start + 8 * j)
            return carry

        lax.fori_loop(0, self.tiles // group, trip, 0)

    def weigh(self, turning):
        def work(r):
            sea = self.stat[0, pl.ds(r, 8), :]
            north = self.stat[0, pl.ds(r + 1, 8), :]
            south = self.stat[0, pl.ds(r - 1, 8), :]
            east, west = roll(sea, -1), roll(sea, 1)
            self.stat[1, pl.ds(r, 8), :] = (east + west) + (north + south)
            self.stat[2, pl.ds(r, 8), :] = sea * east
            self.stat[3, pl.ds(r, 8), :] = sea * north
            self.stat[4, pl.ds(r, 8), :] = turning(r)
            for i in range(FIELDS):
                self.state[i, pl.ds(r, 8), :] = sea * self.state[i, pl.ds(r, 8), :]

        return work

    def first(self, r):
        def rows(ref, i, by=0):
            return ref[i, pl.ds(r + by, 8), :]

        centre = [rows(self.state, i) for i in range(FIELDS)]
        lap, partial = first_pass(
            centre,
            [rows(self.state, i, 1) for i in range(FIELDS)],
            [rows(self.state, i, -1) for i in range(FIELDS)],
            [roll(x, -1) for x in centre],
            [roll(x, 1) for x in centre],
            rows(self.stat, 0),
            rows(self.stat, 1),
            rows(self.stat, 2),
            rows(self.stat, 3),
            rows(self.stat, 3, -1),
            rows(self.stat, 4),
            (lambda x: roll(x, 1),) * 3,
        )
        for i in range(FIELDS):
            self.laps[i, pl.ds(r, 8), :] = lap[i]
            self.part[i, pl.ds(r, 8), :] = partial[i]

    def second(self, r):
        sea, count = self.stat[0, pl.ds(r, 8), :], self.stat[1, pl.ds(r, 8), :]
        for i in range(FIELDS):
            lap = self.laps[i, pl.ds(r, 8), :]
            self.state[i, pl.ds(r, 8), :] = second_pass(
                self.part[i, pl.ds(r, 8), :],
                lap,
                self.laps[i, pl.ds(r + 1, 8), :],
                self.laps[i, pl.ds(r - 1, 8), :],
                roll(lap, -1),
                roll(lap, 1),
                sea,
                count,
            )

    def step(self, group):
        self.each_tile(self.first, group)
        self.each_tile(self.second, group)


def shifted_ghosts(blocks):
    before, here, after = blocks
    lane = lane_index(here.shape[0])
    return (
        jnp.where(lane < HALO, roll(before, HALO), roll(here, HALO)),
        jnp.where(lane >= LANES - HALO, roll(after, -HALO), roll(here, -HALO)),
    )


def turning_of(row, total_rows):
    return (TIME_STEP * ROTATION) * (2.0 * (row + 0.5) / total_rows - 1.0)


def row_in_tile():
    return lax.broadcasted_iota(jnp.int32, (8, LANES), 0).astype(jnp.float32)


def main_kernel(
    fields,
    sb_ref,
    ra_ref,
    rb_ref,
    rw_ref,
    re_ref,
    t_out,
    s_out,
    u_out,
    v_out,
    upper_state,
    upper_stat,
    state,
    laps,
    part,
    stat,
):
    odd, top = is_odd(), is_top()
    lane = lane_index()
    height = fields.shape[1]
    total_rows = height * lax.axis_size("lat")
    tiles_n = height // 8 + 2
    band = 8 * tiles_n
    bands = Band(state, laps, part, stat)

    for i in range(5):
        at = slice(i * 8, i * 8 + 8)
        ra, rb, from_w, from_e = ra_ref[at, :], rb_ref[at, :], rw_ref[at, :], re_ref[at, :]
        tiles = [jnp.where(odd, ra, rb)]
        tiles += [fields[i, 8 * g : 8 * g + 8, :] for g in range(height // 8)]
        tiles += [jnp.where(odd, rb, ra)]
        ref, at = (state, i) if i < FIELDS else (stat, 0)
        for g, tile in enumerate(tiles):
            ref[at, 8 + 8 * g : 16 + 8 * g, :] = jnp.where(
                lane < HALO, roll(from_w, -8 * g), roll(tile, HALO)
            )
            ref[at, 8 + band + 8 * g : 16 + band + 8 * g, :] = jnp.where(
                lane >= LANES - HALO, roll(from_e, LANES - HALO - 8 * g), roll(tile, -HALO)
            )
    bands.pad()

    @pl.when(top)
    def _():
        pairs = (
            (rw_ref, 40, rw_ref, 40 + CAP),
            (sb_ref, 0, rb_ref, 0),
            (re_ref, 40, re_ref, 40 + CAP),
        )
        for i in range(5):
            ghosts = []
            for own, own_at, facing, facing_at in pairs:
                index = lax.rem(own[own_at + 40 : own_at + 48, :].astype(jnp.int32), LANES)
                rows = facing[facing_at + 8 * i : facing_at + 8 * i + 8, :]
                ghosts.append(
                    (PARITY + (1.0,))[i]
                    * jnp.take_along_axis(rows, index, axis=1, mode="promise_in_bounds")
                )
            ref, at = (state, i) if i < FIELDS else (stat, 0)
            for which, ghost in enumerate(shifted_ghosts(ghosts)):
                row = 8 + band * (which + 1) - HALO
                ref[at, row : row + 1, :] = ghost[7:8, :]
                ref[at, row + 1 : row + 2, :] = ghost[6:7, :]

    base_row = (lax.axis_index("lat") * height - HALO).astype(jnp.float32)
    sub = row_in_tile()
    bands.each_tile(
        bands.weigh(
            lambda r: turning_of(
                base_row + lax.rem(r - 8, band).astype(jnp.float32) + sub, total_rows
            )
        ),
        GROUP,
    )

    def step(n, carry):
        bands.step(GROUP)

        @pl.when(top & (n == 0))
        def _():
            for which in (0, 1):
                row = 8 + band * (which + 1) - UPPER
                for i in range(FIELDS):
                    upper_state[i, which] = state[i, row : row + UPPER, :]
                for i in range(5):
                    upper_stat[i, which] = stat[i, row : row + UPPER, :]

        return carry

    lax.fori_loop(0, STEPS, step, 0)

    for i, out in enumerate((t_out, s_out, u_out, v_out)):
        for g in range(height // 8):
            r = 8 + HALO + 8 * g
            west, east = state[i, r : r + 8, :], state[i, r + band : r + band + 8, :]
            out[0, 8 * g : 8 * g + 8, :] = jnp.where(
                lane < LANES // 2, roll(west, -HALO), roll(east, HALO)
            )


def arc_neighbours(blocks):
    lane = lane_index()
    last = len(blocks) - 1
    e, w = [roll(x, -1) for x in blocks], [roll(x, 1) for x in blocks]
    east = [jnp.where(lane == LANES - 1, e[min(k + 1, last)], e[k]) for k in range(last + 1)]
    west = [jnp.where(lane == 0, w[max(k - 1, 0)], w[k]) for k in range(last + 1)]
    return east, west


def cap_kernel(
    t_in,
    s_in,
    u_in,
    v_in,
    upper_state,
    upper_stat,
    sb_ref,
    rb_ref,
    rw_ref,
    re_ref,
    first_far,
    second_far,
    t_out,
    s_out,
    u_out,
    v_out,
    state,
    laps,
    part,
    stat,
    cap,
    cap_lap,
    cap_part,
    cap_stat,
    cap_opp,
    rows_out,
    sems,
):
    far_flag = jnp.logical_not(is_odd_lon())
    w3_ref = Either(far_flag, second_far, first_far)
    e3_ref = Either(far_flag, first_far, second_far)
    lane = lane_index()
    height = t_out.shape[1]
    total_rows = height * lax.axis_size("lat")
    bands = Band(state, laps, part, stat)
    nothing = jnp.zeros((8, LANES), jnp.float32)
    cap_turn = turning_of(float(total_rows - HALO + 1) + row_in_tile(), total_rows)

    def fill_ghosts(ref, parities, low, high, sides):
        def one(side, carry):
            ghosts = {}
            for k in range(low, high):
                index = cap_opp[side, k]
                for i, parity in enumerate(parities):
                    rows = ref[1 - side, i, ARC - 1 - k, 0:8, :]
                    ghosts[k, i] = parity * jnp.take_along_axis(
                        rows, index, axis=1, mode="promise_in_bounds"
                    )
            for (k, i), ghost in ghosts.items():
                ref[side, i, k, 8:9, :] = ghost[7:8, :]
                ref[side, i, k, 9:10, :] = ghost[6:7, :]
            return carry

        lax.fori_loop(0, sides, one, 0)

    def put_block(side, place, ref, base, n):
        sea = ref[base + 4 * n : base + 5 * n, :]
        cap_stat[side, 0, place, 8 - n : 8, :] = sea
        cap_stat[side, 0, place, 10:16, :] = nothing[0:6]
        if n < 8:
            cap_stat[side, 0, place, 0 : 8 - n, :] = nothing[n:8]
        for i in range(FIELDS):
            cap[side, i, place, 8 - n : 8, :] = sea * ref[base + n * i : base + n * i + n, :]
            if n < 8:
                cap[side, i, place, 0 : 8 - n, :] = nothing[n:8]
            cap[side, i, place, 10:16, :] = nothing[0:6]
            cap_lap[side, i, place, 0:8, :] = nothing
            cap_lap[side, i, place, 8:16, :] = nothing
        opp = jnp.broadcast_to(ref[base + 5 * n : base + 5 * n + 1, :], (8, LANES))
        cap_opp[side, place] = lax.rem(opp.astype(jnp.int32), LANES)

    def cap_weigh():
        for side in (0, 1):
            for start in (0, 1):
                seas = [cap_stat[side, 0, k, start : start + 8, :] for k in range(ARC)]
                east, west = arc_neighbours(seas)
                for k in range(ARC):
                    north = cap_stat[side, 0, k, start + 1 : start + 9, :]
                    if start:
                        south = cap_stat[side, 0, k, start - 1 : start + 7, :]
                        cap_stat[side, 1, k, 1:9, :] = (east[k] + west[k]) + (north + south)
                    cap_stat[side, 2, k, start : start + 8, :] = seas[k] * east[k]
                    cap_stat[side, 3, k, start : start + 8, :] = seas[k] * north

    def cap_first(side, low, high):
        ratio = EXPAND / CONTRACT
        span = range(low - 1, high + 1)
        fields = []
        for i in range(FIELDS):
            blocks = [cap[side, i, k, 1:9, :] for k in span]
            fields.append((blocks, *arc_neighbours(blocks)))
        for n, k in enumerate(span):
            b, be = [f[0][n - 1] for f in fields], [f[1][n - 1] for f in fields]
            w_e = cap_stat[side, 2, max(k - 1, 0), 1:9, :]
            flow = w_e * (b[2] + be[2])
            faces = [flow * (b[i] + be[i]) for i in (0, 1)]
            faces.append(w_e * ((be[1] - ratio * be[0]) - (b[1] - ratio * b[0])))
            lap, partial = first_pass(
                [f[0][n] for f in fields],
                [cap[side, i, k, 2:10, :] for i in range(FIELDS)],
                [cap[side, i, k, 0:8, :] for i in range(FIELDS)],
                [f[1][n] for f in fields],
                [f[2][n] for f in fields],
                cap_stat[side, 0, k, 1:9, :],
                cap_stat[side, 1, k, 1:9, :],
                cap_stat[side, 2, k, 1:9, :],
                cap_stat[side, 3, k, 1:9, :],
                cap_stat[side, 3, k, 0:8, :],
                cap_turn,
                [
                    lambda x, face=face: roll(jnp.where(lane == LANES - 1, face, x), 1)
                    for face in faces
                ],
            )
            for i in range(FIELDS):
                cap_lap[side, i, k, 1:9, :] = lap[i]
                if low <= k < high:
                    cap_part[side, i, k, 0:8, :] = partial[i]

    def cap_second(side, low, high):
        for i in range(FIELDS):
            blocks = [cap_lap[side, i, k, 1:9, :] for k in range(low - 1, high + 1)]
            east, west = arc_neighbours(blocks)
            for n, k in enumerate(range(low - 1, high + 1)):
                if low <= k < high:
                    cap[side, i, k, 1:9, :] = second_pass(
                        cap_part[side, i, k, 0:8, :],
                        blocks[n],
                        cap_lap[side, i, k, 2:10, :],
                        cap_lap[side, i, k, 0:8, :],
                        east[n],
                        west[n],
                        cap_stat[side, 0, k, 1:9, :],
                        cap_stat[side, 1, k, 1:9, :],
                    )

    @pl.when(is_top())
    def _():
        parts = [(j, side, w3_ref, base, n) for j, side, n, base in far_places(FAR_ROWS)]
        parts += [
            (j + REACH + 2, side, e3_ref, base, n)
            for j, side, n, base in far_places(FAR_ROWS[::-1])
        ]
        for side in (0, 1):
            parts.append((REACH - 1, side, rw_ref, 40 + CAP * side, 8))
            parts.append((REACH, side, (sb_ref, rb_ref)[side], 0, 8))
            parts.append((REACH + 1, side, re_ref, 40 + CAP * side, 8))
        for k, side, ref, base, n in parts:
            put_block(side, ARC - 1 - k if side else k, ref, base, n)
        bands.pad()
        for which in (0, 1):
            row = 8 + UPPER * which
            for i in range(FIELDS):
                state[i, row : row + UPPER, :] = upper_state[i, which]
            for i in range(5):
                stat[i, row : row + UPPER, :] = upper_stat[i, which]
        fill_ghosts(cap_stat, (1.0,), 0, ARC, 2)
        fill_ghosts(cap, PARITY, 0, ARC, 2)
        cap_weigh()
        for n in range(STEPS - 1):
            low, high = n + 1, ARC - 1 - n
            first_side = 1 if n == STEPS - 2 else 0

            def one(side, carry, low=low, high=high):
                cap_first(side, low, high)
                cap_second(side, low, high)
                return carry

            lax.fori_loop(first_side, 2, one, 0)
            fill_ghosts(cap, PARITY, low, high, 2 - first_side)
            for i in range(FIELDS):
                ghosts = [cap[0, i, k, 8:10, :] for k in (REACH - 1, REACH, REACH + 1)]
                for which, ghost in enumerate(shifted_ghosts(ghosts)):
                    row = 8 + UPPER * (which + 1) - HALO
                    state[i, row : row + 2, :] = ghost
            bands.step(bands.tiles)
        copies = []
        for i, out in enumerate((t_out, s_out, u_out, v_out)):
            row = 8 + UPPER - 2 * HALO
            west, east = state[i, row : row + 8, :], state[i, row + UPPER : row + UPPER + 8, :]
            rows_out[i] = jnp.where(lane < LANES // 2, roll(west, -HALO), roll(east, HALO))
            copies.append(
                pltpu.make_async_copy(
                    rows_out.at[i], out.at[0, pl.ds(height - HALO, HALO), :], sems.at[i]
                )
            )
        for copy in copies:
            copy.start()
        for copy in copies:
            copy.wait()


def body(lon_count, lat_count, t, s, u, v, m, opp):
    fields = (t, s, u, v, m)
    height = t.shape[1]
    vmem, anywhere = (
        pl.BlockSpec(memory_space=pltpu.VMEM),
        pl.BlockSpec(memory_space=pltpu.HBM),
    )
    f32, i32 = jnp.float32, jnp.int32

    def call(kernel, inputs, shapes, scratch=(), far=0, flops=0):
        inputs = [
            pltpu.with_memory_space_constraint(x, pltpu.HBM) if i < far else x
            for i, x in enumerate(inputs)
        ]
        return pl.pallas_call(
            kernel,
            out_shape=[jax.ShapeDtypeStruct(shape, f32) for shape in shapes],
            in_specs=[anywhere] * far + [vmem] * (len(inputs) - far),
            out_specs=[vmem] * len(shapes),
            scratch_shapes=list(scratch),
            compiler_params=pltpu.CompilerParams(vmem_limit_bytes=32 * 1024 * 1024),
            cost_estimate=pl.CostEstimate(flops=flops, bytes_accessed=flops, transcendentals=0),
        )(*inputs)

    def place(lon, lat):
        return (lon % lon_count) * lat_count + lat

    lons, lats = range(lon_count), range(lat_count)
    last = lat_count - 1
    pairs_a = [(place(i, j), place(i, j ^ 1)) for i in lons for j in lats]
    pairs_b = [(place(i, j), place(i, ((j - 1) ^ 1) + 1)) for i in lons for j in lats[1:last]]
    pairs_b += [(place(i, last), place(-i, last)) for i in lons]

    def swap(x, by, rest, rows):
        pairs = []
        for i in lons:
            other = i + by if i % 2 == rest else i - by
            pairs += [(place(i, j), place(other, j)) for j in rows]
        return exchange(x, pairs)

    def shift(x, by):
        return exchange(x, [(place(i, j), place(i + by, j)) for i in lons for j in lats])

    def exchange(x, pairs):
        return lax.ppermute(x, ("lon", "lat"), pairs)

    (send_b,) = call(
        first_rows_kernel,
        (*fields, opp.reshape(1, LANES)),
        [(CAP, LANES)],
        [pltpu.VMEM((16, LANES), i32), pltpu.SemaphoreType.DMA((6,))],
        far=6,
    )
    from_b = exchange(send_b, pairs_b)
    stack, send_a, columns_e, columns_w = call(
        load_kernel,
        (*fields, send_b),
        [(5, height, LANES), (40, LANES), (40, LANES), (40, LANES)],
        [pltpu.VMEM((height, LANES), i32), pltpu.SemaphoreType.DMA((5,))],
        far=5,
    )
    from_a = exchange(send_a, pairs_a)
    send_e, send_w = call(
        functools.partial(pair_kernel, height),
        (columns_e, columns_w, send_b, from_a, from_b),
        [(40 + 2 * CAP, LANES)] * 2,
    )
    from_w = shift(send_e, 1)
    from_e = shift(send_w, -1)
    far_send_1, far_send_2 = call(
        far_kernel, (send_b, from_b, from_w, from_e), [(FAR, LANES)] * 2
    )
    far_1 = swap(far_send_1, 3, 0, [last])
    far_2 = swap(far_send_2, 3, 1, [last])

    def band_scratch(rows):
        return [pltpu.VMEM((n, 16 + 2 * rows, LANES), f32) for n in (FIELDS, FIELDS, FIELDS, 5)]

    *outs, upper_state, upper_stat = call(
        main_kernel,
        (stack, send_b, from_a, from_b, from_w, from_e),
        [t.shape] * 4 + [(FIELDS, 2, UPPER, LANES), (5, 2, UPPER, LANES)],
        band_scratch(height + 2 * HALO),
        flops=10**7,
    )
    return tuple(
        pl.pallas_call(
            cap_kernel,
            out_shape=[jax.ShapeDtypeStruct(t.shape, f32)] * 4,
            in_specs=[anywhere] * 4 + [vmem] * 8,
            out_specs=[anywhere] * 4,
            scratch_shapes=band_scratch(UPPER)
            + [
                pltpu.VMEM((2, FIELDS, ARC, 16, LANES), f32),
                pltpu.VMEM((2, FIELDS, ARC, 16, LANES), f32),
                pltpu.VMEM((2, FIELDS, ARC, 8, LANES), f32),
                pltpu.VMEM((2, 4, ARC, 16, LANES), f32),
                pltpu.VMEM((2, ARC, 8, LANES), i32),
                pltpu.VMEM((FIELDS, 8, LANES), f32),
                pltpu.SemaphoreType.DMA((FIELDS,)),
            ],
            input_output_aliases={i: i for i in range(4)},
            compiler_params=pltpu.CompilerParams(vmem_limit_bytes=32 * 1024 * 1024),
        )(*outs, upper_state, upper_stat, send_b, from_b, from_w, from_e, far_1, far_2)
    )


def solution(mesh):
    placed = P(None, "lat", "lon")
    return jax.shard_map(
        functools.partial(body, mesh.shape["lon"], mesh.shape["lat"]),
        mesh=mesh,
        in_specs=(placed,) * 5 + (P("lon"),),
        out_specs=(placed,) * 4,
        check_vma=False,
    )
```

```python
import functools

import jax
import jax.numpy as jnp
from jax import lax
from jax.experimental import pallas as pl
from jax.experimental.pallas import tpu as pltpu
from jax.sharding import PartitionSpec as P

STEPS = 4
TIME_STEP = 0.1
DIFFUSE = 0.15
EXPAND = 0.2
CONTRACT = 0.8
ROTATION = 0.5

HALO = 2 * STEPS
LANES = 128
FIELDS = 4
REACH = 4
ARC = 2 * REACH + 1
CAP = 48
PARITY = (1.0, 1.0, -1.0, -1.0)
STATS = 6
STRIP = 8
STRIP_STEP = 6
FAR_ROWS = (2, 4, 6)
FAR = 128
UPPER = 24


def lane_index(rows=8):
    return lax.broadcasted_iota(jnp.int32, (rows, LANES), 1)


def roll(x, shift):
    shift = shift % LANES
    return x if shift == 0 else pltpu.roll(x, shift, 1)


def is_odd():
    return lax.rem(lax.axis_index("lat"), 2) == 1


def is_top():
    return lax.axis_index("lat") == lax.axis_size("lat") - 1


def is_early():
    return lax.axis_index("lon") < lax.axis_size("lon") // 4


def is_odd_lon():
    return lax.rem(lax.axis_index("lon"), 2) == 1


class Either:
    def __init__(self, flag, yes, no):
        self.flag, self.yes, self.no = flag, yes, no

    def __getitem__(self, index):
        return jnp.where(self.flag, self.yes[index], self.no[index])


def near_refs(first, second):
    odd_lon = is_odd_lon()
    return Either(odd_lon, second, first), Either(odd_lon, first, second)


def first_rows_kernel(t_ref, s_ref, u_ref, v_ref, m_ref, opp_ref, after, out, ints, sems):
    start = pl.multiple_of(jnp.where(is_odd(), t_ref.shape[1] - HALO, 0), 8)
    copies = [pltpu.make_async_copy(opp_ref, ints.at[pl.ds(8, 1), :], sems.at[5])]
    for i, ref in enumerate((t_ref, s_ref, u_ref, v_ref, m_ref)):
        target = out.at[pl.ds(8 * i, 8), :] if i < FIELDS else ints.at[pl.ds(0, 8), :]
        copies.append(
            pltpu.make_async_copy(ref.at[0, pl.ds(start, HALO), :], target, sems.at[i])
        )
    for copy in copies:
        copy.start()
    for copy in copies:
        copy.wait()
    out[32:40, :] = ints[0:8, :].astype(jnp.float32)
    out[40:48, :] = jnp.broadcast_to(ints[8:9, :].astype(jnp.float32), (8, LANES))


def add_columns(e, w, tile, g):
    lane = lane_index()
    slots = ([g] if g < STRIP else []) + ([g - STRIP_STEP + STRIP] if g >= STRIP_STEP else [])
    for slot in slots:
        here = (lane >= 8 * slot) & (lane < 8 * slot + 8)
        e = jnp.where(here, roll(tile, 8 * slot - (LANES - HALO)), e)
        w = jnp.where(here, roll(tile, 8 * slot), w)
    return e, w


def pair_kernel(height, e_in, w_in, sb_ref, ra_ref, rb_ref, first, second):
    odd, odd_lon = is_odd(), is_odd_lon()
    for i in range(5):
        at = slice(i * 8, i * 8 + 8)
        ra, rb = ra_ref[at, :], rb_ref[at, :]
        e, w = add_columns(e_in[at, :], w_in[at, :], jnp.where(odd, ra, rb), 0)
        e, w = add_columns(e, w, jnp.where(odd, rb, ra), height // 8 + 1)
        first[at, :] = jnp.where(odd_lon, e, w)
        second[at, :] = jnp.where(odd_lon, w, e)

    @pl.when(is_top())
    def _():
        for ref in (first, second):
            ref[40 : 40 + CAP, :] = sb_ref[...]
            ref[40 + CAP : 40 + 2 * CAP, :] = rb_ref[...]


def far_places(counts):
    base = 0
    for j, n in enumerate(counts):
        for side in (0, 1):
            yield j, side, n, base
            base += 5 * n + 1


def far_kernel(sb_ref, rb_ref, first_in, second_in, first, second):
    @pl.when(is_top())
    def _():
        far_flag = jnp.logical_not(is_odd_lon())
        rw_ref, re_ref = near_refs(first_in, second_in)
        sources = (
            ((rw_ref, 40), (rw_ref, 40 + CAP)),
            ((sb_ref, 0), (rb_ref, 0)),
            ((re_ref, 40), (re_ref, 40 + CAP)),
        )

        def fill(out, counts):
            for j, side, n, base in far_places(counts):
                ref, at = sources[j][side]
                for i in range(5):
                    out[base + i * n : base + i * n + n, :] = ref[
                        at + 8 * i + 8 - n : at + 8 * i + 8, :
                    ]
                out[base + 5 * n : base + 5 * n + 1, :] = ref[at + 40 : at + 41, :]
            out[FAR - 2 : FAR, :] = jnp.zeros((2, LANES), jnp.float32)

        @pl.when(far_flag)
        def _():
            fill(first, FAR_ROWS)
            fill(second, FAR_ROWS[::-1])

        @pl.when(jnp.logical_not(far_flag))
        def _():
            fill(first, FAR_ROWS[::-1])
            fill(second, FAR_ROWS)


def first_pass(centre, north, south, east, west, stat, w_s):
    sea, count, w_e, w_n, turn = stat
    laps = [
        sea * (((east[i] + west[i]) + (north[i] + south[i])) - count * centre[i])
        for i in range(FIELDS)
    ]
    t, s, u, v = centre
    flow_e = (0.25 * TIME_STEP) * w_e * (u + east[2])
    flow_n = (0.25 * TIME_STEP) * w_n * (v + north[3])
    flow_s = (0.25 * TIME_STEP) * w_s * (v + south[3])
    partial, flux = [], []
    for i in (0, 1):
        c = centre[i]
        flux.append(flow_e * (c + east[i]))
        partial.append(c - (flow_n * (c + north[i]) - flow_s * (c + south[i])))
    ratio = EXPAND / CONTRACT
    slope = 0.25 * TIME_STEP * CONTRACT
    q = s - ratio * t
    q_e = east[1] - ratio * east[0]
    q_n = north[1] - ratio * north[0]
    q_s = south[1] - ratio * south[0]
    flux.append(slope * w_e * (q_e - q))
    partial.append(u + turn * v)
    partial.append(v - (turn * u + slope * (w_n * (q_n - q) + w_s * (q - q_s))))
    return laps, partial, flux


def face_terms(i, lap, east, w_e, flux):
    mix = (TIME_STEP * DIFFUSE) * w_e * (east - lap)
    if i < 2:
        return flux + mix, flux + mix
    if i == 2:
        return flux + mix, mix - flux
    return mix, mix


def second_pass(partial, loss, gain, lap, north, south, sea, count_ns):
    mix = (TIME_STEP * DIFFUSE) * ((north + south) - count_ns * lap)
    return sea * (partial - ((loss - gain) + mix))


class Band:
    def __init__(self, state, laps, part, flux, stat):
        self.state, self.laps, self.part, self.flux, self.stat = state, laps, part, flux, stat
        self.rows = range(8, state.shape[1] - 8, 8)

    def pad(self):
        nothing = jnp.zeros((8, LANES), jnp.float32)
        for row in (0, self.rows[-1] + 8):
            for i in range(FIELDS):
                self.state[i, row : row + 8, :] = nothing
                self.laps[i, row : row + 8, :] = nothing
            for i in range(STATS):
                self.stat[i, row : row + 8, :] = nothing

    def weigh(self, turning):
        for r in self.rows:
            at = slice(r, r + 8)
            sea = self.stat[0, at, :]
            north, south = self.stat[0, r + 1 : r + 9, :], self.stat[0, r - 1 : r + 7, :]
            east, west = roll(sea, -1), roll(sea, 1)
            self.stat[1, at, :] = (east + west) + (north + south)
            self.stat[2, at, :] = sea * east
            self.stat[3, at, :] = sea * north
            self.stat[4, at, :] = turning(r)
            self.stat[5, at, :] = north + south
            for i in range(FIELDS):
                self.state[i, at, :] = sea * self.state[i, at, :]

    def step(self):
        for r in self.rows:
            at, up, down = slice(r, r + 8), slice(r + 1, r + 9), slice(r - 1, r + 7)
            centre = [self.state[i, at, :] for i in range(FIELDS)]
            lap, partial, flux = first_pass(
                centre,
                [self.state[i, up, :] for i in range(FIELDS)],
                [self.state[i, down, :] for i in range(FIELDS)],
                [roll(x, -1) for x in centre],
                [roll(x, 1) for x in centre],
                [self.stat[i, at, :] for i in range(5)],
                self.stat[3, down, :],
            )
            for i in range(FIELDS):
                self.laps[i, at, :] = lap[i]
                self.part[i, at, :] = partial[i]
                if i < 3:
                    self.flux[i, at, :] = flux[i]
        for r in self.rows:
            at, up, down = slice(r, r + 8), slice(r + 1, r + 9), slice(r - 1, r + 7)
            sea, w_e, count_ns = (self.stat[i, at, :] for i in (0, 2, 5))
            for i in range(FIELDS):
                lap = self.laps[i, at, :]
                flux = self.flux[i, at, :] if i < 3 else None
                loss, gain = face_terms(i, lap, roll(lap, -1), w_e, flux)
                self.state[i, at, :] = second_pass(
                    self.part[i, at, :],
                    loss,
                    roll(gain, 1),
                    lap,
                    self.laps[i, up, :],
                    self.laps[i, down, :],
                    sea,
                    count_ns,
                )


def strip_own(low, high):
    lane = lane_index()
    second = lane >= 64
    west = jnp.where(second, roll(high, 72), roll(low, 8))
    east = jnp.where(second, roll(high, 112), roll(low, 48))
    return jnp.where(lax.rem(lane, 64) < 32, west, east)


def prepare(refs, fields, a_ref, e_ref, w_ref, inner, strip, ints, state, laps, part, flux, stat, sems):
    height = fields.shape[1]
    total_rows = height * lax.axis_size("lat")
    copies = []
    for i, ref in enumerate(refs):
        target = fields.at[i] if i < FIELDS else ints
        copies.append(pltpu.make_async_copy(ref.at[0], target, sems.at[i]))
    for copy in copies:
        copy.start()
    for copy in copies:
        copy.wait()
    fields[FIELDS] = ints[...].astype(jnp.float32)
    odd = is_odd()
    bands = Band(state, laps, part, flux, stat)
    bands.pad()
    for i in range(5):
        tiles = [fields[i, 8 * g : 8 * g + 8, :] for g in range(height // 8)]
        a_ref[i * 8 : i * 8 + 8, :] = jnp.where(odd, tiles[0], tiles[-1])
        e = w = jnp.zeros((8, LANES), jnp.float32)
        ref, at = (state, i) if i < FIELDS else (stat, 0)
        for g, tile in enumerate(tiles):
            e, w = add_columns(e, w, tile, g + 1)
            ref[at, 8 + 8 * g : 16 + 8 * g, :] = tile
        e_ref[i * 8 : i * 8 + 8, :] = e
        w_ref[i * 8 : i * 8 + 8, :] = w
        for n in range(STRIP):
            low, high = tiles[max(n - 1, 0)], tiles[min(n + STRIP_STEP - 1, len(tiles) - 1)]
            strip[i, 8 * n : 8 * n + 8, :] = strip_own(low, high)
    base_row = (lax.axis_index("lat") * height).astype(jnp.float32)
    sub = row_in_tile()
    bands.weigh(lambda r: turning_of(base_row + float(r - 8) + sub, total_rows))

    def step(n, carry):
        bands.step()
        return carry

    lax.fori_loop(0, STEPS, step, 0)
    for i in range(FIELDS):
        for g in range(height // 8):
            inner[i, 8 * g : 8 * g + 8, :] = state[i, 8 + 8 * g : 16 + 8 * g, :]


def early_kernel(*refs):
    @pl.when(is_early())
    def _():
        prepare(refs[:5], *refs[5:])


def late_kernel(*refs):
    early = is_early()

    @pl.when(early)
    def _():
        for source, target in zip(refs[6:12], refs[12:18]):
            target[...] = source[...]

    @pl.when(jnp.logical_not(early))
    def _():
        prepare(refs[:5], *refs[12:])


def strip_ghosts(blocks, old):
    before, here, after = blocks
    lane = lane_index(here.shape[0])
    new = jnp.where(lane < 96, roll(here, 72), roll(here, 112))
    new = jnp.where(lane < 72, roll(before, 64 - (LANES - HALO)), new)
    new = jnp.where(lane >= 112, roll(after, 112), new)
    return jnp.where(lane < 64, old, new)


def join_columns(centre, strip, second):
    lane = lane_index()
    start = 64 if second else 0
    west, east = roll(strip, -start - HALO), roll(strip, LANES - HALO - start - 40)
    return jnp.where(lane < HALO, west, jnp.where(lane >= LANES - HALO, east, centre))


def turning_of(row, total_rows):
    return (TIME_STEP * ROTATION) * (2.0 * (row + 0.5) / total_rows - 1.0)


def row_in_tile():
    return lax.broadcasted_iota(jnp.int32, (8, LANES), 0).astype(jnp.float32)


def frame_kernel(
    fields,
    strip,
    inner,
    sb_ref,
    ra_ref,
    rb_ref,
    first_in,
    second_in,
    t_out,
    s_out,
    u_out,
    v_out,
    upper_state,
    upper_stat,
    state,
    laps,
    part,
    flux,
    stat,
):
    rw_ref, re_ref = near_refs(first_in, second_in)
    odd, top = is_odd(), is_top()
    lane = lane_index()
    height = fields.shape[1]
    total_rows = height * lax.axis_size("lat")
    north_row, strip_row = 8 + UPPER, 8 + 2 * UPPER
    bands = Band(state, laps, part, flux, stat)
    bands.pad()
    side = lax.rem(lane, 64)

    for i in range(5):
        at = slice(i * 8, i * 8 + 8)
        ra, rb, from_w, from_e = ra_ref[at, :], rb_ref[at, :], rw_ref[at, :], re_ref[at, :]
        south, north = jnp.where(odd, ra, rb), jnp.where(odd, rb, ra)
        ref, at = (state, i) if i < FIELDS else (stat, 0)
        ref[at, 8:16, :] = south
        ref[at, 16 : 8 + UPPER, :] = fields[i, 0 : UPPER - 8, :]
        ref[at, north_row : north_row + UPPER - 8, :] = fields[i, height - UPPER + 8 : height, :]
        ref[at, north_row + UPPER - 8 : strip_row, :] = north
        for n in range(STRIP):
            own = strip[i, 8 * n : 8 * n + 8, :]
            if n == 0:
                own = jnp.where(lane < 64, strip_own(south, south), own)
            if n == STRIP - 1:
                own = jnp.where(lane >= 64, strip_own(north, north), own)
            own = jnp.where(side < HALO, roll(from_w, -8 * n), own)
            own = jnp.where(side >= 48, roll(from_e, 48 - 8 * n), own)
            ref[at, strip_row + 8 * n : strip_row + 8 * n + 8, :] = own

    @pl.when(top)
    def _():
        pairs = (
            (rw_ref, 40, rw_ref, 40 + CAP),
            (sb_ref, 0, rb_ref, 0),
            (re_ref, 40, re_ref, 40 + CAP),
        )
        for i in range(5):
            ghosts = []
            for own, own_at, facing, facing_at in pairs:
                index = lax.rem(own[own_at + 40 : own_at + 48, :].astype(jnp.int32), LANES)
                rows = facing[facing_at + 8 * i : facing_at + 8 * i + 8, :]
                ghosts.append(
                    (PARITY + (1.0,))[i]
                    * jnp.take_along_axis(rows, index, axis=1, mode="promise_in_bounds")
                )
            ref, at = (state, i) if i < FIELDS else (stat, 0)
            row = north_row + UPPER - HALO
            ref[at, row : row + 1, :] = ghosts[1][7:8, :]
            ref[at, row + 1 : row + 2, :] = ghosts[1][6:7, :]
            for n in (0, 1):
                row = strip_row + 8 * STRIP - HALO + n
                ref[at, row : row + 1, :] = strip_ghosts(
                    [ghost[7 - n : 8 - n, :] for ghost in ghosts], ref[at, row : row + 1, :]
                )

    base_row = (lax.axis_index("lat") * height - HALO).astype(jnp.float32)
    sub = row_in_tile()
    second = jnp.where(lane >= 64, 8.0 * STRIP_STEP, 0.0)

    def turning(r):
        if r < north_row:
            row = base_row + float(r - 8) + sub
        elif r < strip_row:
            row = base_row + float(height + 2 * HALO - UPPER + r - north_row) + sub
        else:
            row = base_row + float(r - strip_row) + sub + second
        return turning_of(row, total_rows)

    bands.weigh(turning)

    def step(n, carry):
        bands.step()

        @pl.when(top & (n == 0))
        def _():
            for which, row in enumerate((north_row, strip_row + 8 * STRIP - UPPER)):
                for i in range(FIELDS):
                    upper_state[i, which] = state[i, row : row + UPPER, :]
                for i in range(STATS):
                    upper_stat[i, which] = stat[i, row : row + UPPER, :]

        return carry

    lax.fori_loop(0, STEPS, step, 0)

    tiles_n = height // 8
    for i, out in enumerate((t_out, s_out, u_out, v_out)):
        for g in range(tiles_n):
            if g == 0:
                centre = state[i, 16:24, :]
            elif g == tiles_n - 1:
                centre = state[i, north_row + 8 : north_row + 16, :]
            else:
                centre = inner[i, 8 * g : 8 * g + 8, :]
            late = g + 1 > STRIP_STEP
            row = strip_row + 8 * (g + 1 - (STRIP_STEP if late else 0))
            out[0, 8 * g : 8 * g + 8, :] = join_columns(centre, state[i, row : row + 8, :], late)


def arc_east(blocks):
    lane, last = lane_index(), len(blocks) - 1
    e = [roll(x, -1) for x in blocks]
    return [jnp.where(lane == LANES - 1, e[min(k + 1, last)], e[k]) for k in range(last + 1)]


def arc_west(blocks):
    lane = lane_index()
    w = [roll(x, 1) for x in blocks]
    return [jnp.where(lane == 0, w[max(k - 1, 0)], w[k]) for k in range(len(blocks))]


def cap_kernel(
    t_in,
    s_in,
    u_in,
    v_in,
    upper_state,
    upper_stat,
    sb_ref,
    rb_ref,
    first_in,
    second_in,
    first_far,
    second_far,
    t_out,
    s_out,
    u_out,
    v_out,
    state,
    laps,
    part,
    flux,
    stat,
    cap,
    cap_lap,
    cap_part,
    cap_flux,
    cap_stat,
    cap_opp,
    rows_out,
    sems,
):
    rw_ref, re_ref = near_refs(first_in, second_in)
    far_flag = jnp.logical_not(is_odd_lon())
    w3_ref = Either(far_flag, second_far, first_far)
    e3_ref = Either(far_flag, first_far, second_far)
    lane = lane_index()
    height = t_out.shape[1]
    total_rows = height * lax.axis_size("lat")
    bands = Band(state, laps, part, flux, stat)
    nothing = jnp.zeros((8, LANES), jnp.float32)
    cap_turn = turning_of(float(total_rows - HALO + 1) + row_in_tile(), total_rows)

    def fill_ghosts(ref, parities, low, high, sides):
        for side in range(sides):
            ghosts = {}
            for k in range(low, high):
                index = cap_opp[side, k]
                for i, parity in enumerate(parities):
                    rows = ref[1 - side, i, ARC - 1 - k, 0:8, :]
                    ghosts[k, i] = parity * jnp.take_along_axis(
                        rows, index, axis=1, mode="promise_in_bounds"
                    )
            for (k, i), ghost in ghosts.items():
                ref[side, i, k, 8:9, :] = ghost[7:8, :]
                ref[side, i, k, 9:10, :] = ghost[6:7, :]

    def put_block(side, place, ref, base, n):
        sea = ref[base + 4 * n : base + 5 * n, :]
        cap_stat[side, 0, place, 8 - n : 8, :] = sea
        cap_stat[side, 0, place, 10:16, :] = nothing[0:6]
        if n < 8:
            cap_stat[side, 0, place, 0 : 8 - n, :] = nothing[n:8]
        for i in range(FIELDS):
            cap[side, i, place, 8 - n : 8, :] = sea * ref[base + n * i : base + n * i + n, :]
            if n < 8:
                cap[side, i, place, 0 : 8 - n, :] = nothing[n:8]
            cap[side, i, place, 10:16, :] = nothing[0:6]
            cap_lap[side, i, place, 0:8, :] = nothing
            cap_lap[side, i, place, 8:16, :] = nothing
        opp = jnp.broadcast_to(ref[base + 5 * n : base + 5 * n + 1, :], (8, LANES))
        cap_opp[side, place] = lax.rem(opp.astype(jnp.int32), LANES)

    def cap_weigh():
        for side in (0, 1):
            for start in (0, 1):
                seas = [cap_stat[side, 0, k, start : start + 8, :] for k in range(ARC)]
                east, west = arc_east(seas), arc_west(seas)
                for k in range(ARC):
                    north = cap_stat[side, 0, k, start + 1 : start + 9, :]
                    if start:
                        south = cap_stat[side, 0, k, start - 1 : start + 7, :]
                        cap_stat[side, 1, k, 1:9, :] = (east[k] + west[k]) + (north + south)
                        cap_stat[side, 4, k, 1:9, :] = north + south
                    cap_stat[side, 2, k, start : start + 8, :] = seas[k] * east[k]
                    cap_stat[side, 3, k, start : start + 8, :] = seas[k] * north

    def cap_first(side, low, high):
        span = range(low - 1, high + 1)
        fields = [[cap[side, i, k, 1:9, :] for k in span] for i in range(FIELDS)]
        east, west = [arc_east(f) for f in fields], [arc_west(f) for f in fields]
        for n, k in enumerate(span):
            lap, partial, fluxes = first_pass(
                [f[n] for f in fields],
                [cap[side, i, k, 2:10, :] for i in range(FIELDS)],
                [cap[side, i, k, 0:8, :] for i in range(FIELDS)],
                [f[n] for f in east],
                [f[n] for f in west],
                [cap_stat[side, i, k, 1:9, :] for i in range(4)] + [cap_turn],
                cap_stat[side, 3, k, 0:8, :],
            )
            for i in range(FIELDS):
                cap_lap[side, i, k, 1:9, :] = lap[i]
                if i < 3:
                    cap_flux[side, i, k, 0:8, :] = fluxes[i]
                if low <= k < high:
                    cap_part[side, i, k, 0:8, :] = partial[i]

    def cap_second(side, low, high):
        span = range(low - 1, high + 1)
        for i in range(FIELDS):
            blocks = [cap_lap[side, i, k, 1:9, :] for k in span]
            terms = [
                face_terms(
                    i,
                    blocks[n],
                    east,
                    cap_stat[side, 2, span[n], 1:9, :],
                    cap_flux[side, i, span[n], 0:8, :] if i < 3 else None,
                )
                for n, east in enumerate(arc_east(blocks))
            ]
            gains = arc_west([gain for _, gain in terms])
            for n, k in enumerate(span):
                if low <= k < high:
                    cap[side, i, k, 1:9, :] = second_pass(
                        cap_part[side, i, k, 0:8, :],
                        terms[n][0],
                        gains[n],
                        blocks[n],
                        cap_lap[side, i, k, 2:10, :],
                        cap_lap[side, i, k, 0:8, :],
                        cap_stat[side, 0, k, 1:9, :],
                        cap_stat[side, 4, k, 1:9, :],
                    )

    @pl.when(is_top())
    def _():
        parts = [(j, side, w3_ref, base, n) for j, side, n, base in far_places(FAR_ROWS)]
        parts += [
            (j + REACH + 2, side, e3_ref, base, n)
            for j, side, n, base in far_places(FAR_ROWS[::-1])
        ]
        for side in (0, 1):
            parts.append((REACH - 1, side, rw_ref, 40 + CAP * side, 8))
            parts.append((REACH, side, (sb_ref, rb_ref)[side], 0, 8))
            parts.append((REACH + 1, side, re_ref, 40 + CAP * side, 8))
        for k, side, ref, base, n in parts:
            put_block(side, ARC - 1 - k if side else k, ref, base, n)
        bands.pad()
        for which in (0, 1):
            row = 8 + UPPER * which
            for i in range(FIELDS):
                state[i, row : row + UPPER, :] = upper_state[i, which]
            for i in range(STATS):
                stat[i, row : row + UPPER, :] = upper_stat[i, which]
        fill_ghosts(cap_stat, (1.0,), 0, ARC, 2)
        fill_ghosts(cap, PARITY, 0, ARC, 2)
        cap_weigh()
        for n in range(STEPS - 1):
            low, high = n + 1, ARC - 1 - n
            first_side = 1 if n == STEPS - 2 else 0

            def one(side, carry, low=low, high=high):
                cap_first(side, low, high)
                cap_second(side, low, high)
                return carry

            lax.fori_loop(first_side, 2, one, 0)
            fill_ghosts(cap, PARITY, low, high, 2 - first_side)
            for i in range(FIELDS):
                ghosts = [cap[0, i, k, 8:10, :] for k in (REACH - 1, REACH, REACH + 1)]
                row = 8 + UPPER - HALO
                state[i, row : row + 2, :] = ghosts[1]
                row += UPPER
                state[i, row : row + 2, :] = strip_ghosts(ghosts, state[i, row : row + 2, :])
            bands.step()
        copies = []
        for i, out in enumerate((t_out, s_out, u_out, v_out)):
            row = 8 + UPPER - 2 * HALO
            rows_out[i] = join_columns(
                state[i, row : row + 8, :], state[i, row + UPPER : row + UPPER + 8, :], True
            )
            copies.append(
                pltpu.make_async_copy(
                    rows_out.at[i], out.at[0, pl.ds(height - HALO, HALO), :], sems.at[i]
                )
            )
        for copy in copies:
            copy.start()
        for copy in copies:
            copy.wait()


def body(lon_count, lat_count, t, s, u, v, m, opp):
    fields = (t, s, u, v, m)
    height = t.shape[1]
    vmem, anywhere = (
        pl.BlockSpec(memory_space=pltpu.VMEM),
        pl.BlockSpec(memory_space=pltpu.HBM),
    )
    f32, i32 = jnp.float32, jnp.int32

    def call(kernel, inputs, shapes, scratch=(), far=0, flops=0):
        inputs = [
            pltpu.with_memory_space_constraint(x, pltpu.HBM) if i < far else x
            for i, x in enumerate(inputs)
        ]
        return pl.pallas_call(
            kernel,
            out_shape=[jax.ShapeDtypeStruct(shape, f32) for shape in shapes],
            in_specs=[anywhere] * far + [vmem] * (len(inputs) - far),
            out_specs=[vmem] * len(shapes),
            scratch_shapes=list(scratch),
            compiler_params=pltpu.CompilerParams(vmem_limit_bytes=32 * 1024 * 1024),
            cost_estimate=pl.CostEstimate(flops=flops, bytes_accessed=flops, transcendentals=0),
        )(*inputs)

    def place(lon, lat):
        return (lon % lon_count) * lat_count + lat

    lons, lats = range(lon_count), range(lat_count)
    last = lat_count - 1
    pairs_a = [(place(i, j), place(i, j ^ 1)) for i in lons for j in lats]
    pairs_b = [(place(i, j), place(i, ((j - 1) ^ 1) + 1)) for i in lons for j in lats[1:last]]
    pairs_b += [(place(i, last), place(-i, last)) for i in lons]

    def swap(x, by, rest, rows):
        pairs = []
        for i in lons:
            other = i + by if i % 2 == rest else i - by
            pairs += [(place(i, j), place(other, j)) for j in rows]
        return exchange(x, pairs)

    def exchange(x, pairs):
        return lax.ppermute(x, ("lon", "lat"), pairs)

    def band_scratch(rows):
        return [
            pltpu.VMEM((n, 16 + rows, LANES), f32) for n in (FIELDS, FIELDS, FIELDS, 3, STATS)
        ]

    prepared = [(5, height, LANES), (40, LANES), (40, LANES), (40, LANES)]
    prepared += [(FIELDS, height, LANES), (5, 8 * STRIP, LANES)]
    scratch = [pltpu.VMEM((height, LANES), i32), *band_scratch(height), pltpu.SemaphoreType.DMA((5,))]
    own = call(early_kernel, fields, prepared, scratch, far=5, flops=10**7)
    (send_b,) = call(
        first_rows_kernel,
        (*fields, opp.reshape(1, LANES), own[1]),
        [(CAP, LANES)],
        [pltpu.VMEM((16, LANES), i32), pltpu.SemaphoreType.DMA((6,))],
        far=6,
    )
    from_b = exchange(send_b, pairs_b)
    stack, send_a, columns_e, columns_w, inner, strip = call(
        late_kernel, (*fields, send_b, *own), prepared, scratch, far=5, flops=10**7
    )
    from_a = exchange(send_a, pairs_a)
    send_1, send_2 = call(
        functools.partial(pair_kernel, height),
        (columns_e, columns_w, send_b, from_a, from_b),
        [(40 + 2 * CAP, LANES)] * 2,
    )
    near_1 = swap(send_1, 1, 1, lats)
    near_2 = swap(send_2, 1, 0, lats)
    far_send_1, far_send_2 = call(
        far_kernel, (send_b, from_b, near_1, near_2), [(FAR, LANES)] * 2
    )
    far_1 = swap(far_send_1, 3, 0, [last])
    far_2 = swap(far_send_2, 3, 1, [last])

    *outs, upper_state, upper_stat = call(
        frame_kernel,
        (stack, strip, inner, send_b, from_a, from_b, near_1, near_2),
        [t.shape] * 4 + [(FIELDS, 2, UPPER, LANES), (STATS, 2, UPPER, LANES)],
        band_scratch(2 * UPPER + 8 * STRIP),
        flops=10**7,
    )
    return tuple(
        pl.pallas_call(
            cap_kernel,
            out_shape=[jax.ShapeDtypeStruct(t.shape, f32)] * 4,
            in_specs=[anywhere] * 4 + [vmem] * 8,
            out_specs=[anywhere] * 4,
            scratch_shapes=band_scratch(2 * UPPER)
            + [
                pltpu.VMEM((2, FIELDS, ARC, 16, LANES), f32),
                pltpu.VMEM((2, FIELDS, ARC, 16, LANES), f32),
                pltpu.VMEM((2, FIELDS, ARC, 8, LANES), f32),
                pltpu.VMEM((2, 3, ARC, 8, LANES), f32),
                pltpu.VMEM((2, 5, ARC, 16, LANES), f32),
                pltpu.VMEM((2, ARC, 8, LANES), i32),
                pltpu.VMEM((FIELDS, 8, LANES), f32),
                pltpu.SemaphoreType.DMA((FIELDS,)),
            ],
            input_output_aliases={i: i for i in range(4)},
            compiler_params=pltpu.CompilerParams(vmem_limit_bytes=32 * 1024 * 1024),
        )(*outs, upper_state, upper_stat, send_b, from_b, near_1, near_2, far_1, far_2)
    )


def solution(mesh):
    placed = P(None, "lat", "lon")
    return jax.shard_map(
        functools.partial(body, mesh.shape["lon"], mesh.shape["lat"]),
        mesh=mesh,
        in_specs=(placed,) * 5 + (P("lon"),),
        out_specs=(placed,) * 4,
        check_vma=False,
    )
```

```python
import functools

import jax
import jax.numpy as jnp
from jax import lax
from jax.experimental import pallas as pl
from jax.experimental.pallas import tpu as pltpu
from jax.sharding import PartitionSpec as P

STEPS = 4
TIME_STEP = 0.1
DIFFUSE = 0.15
EXPAND = 0.2
CONTRACT = 0.8
ROTATION = 0.5

HALO = 2 * STEPS
LANES = 128
FIELDS = 4
REACH = 4
ARC = 2 * REACH + 1
CAP = 48
PARITY = (1.0, 1.0, -1.0, -1.0)
STATS = 6
STRIP = 8
STRIP_STEP = 6
FAR_ROWS = (2, 4, 6)
FAR = 128
UPPER = 24


def lane_index(rows=8):
    return lax.broadcasted_iota(jnp.int32, (rows, LANES), 1)


def roll(x, shift):
    shift = shift % LANES
    return x if shift == 0 else pltpu.roll(x, shift, 1)


def is_odd():
    return lax.rem(lax.axis_index("lat"), 2) == 1


def is_top():
    return lax.axis_index("lat") == lax.axis_size("lat") - 1


def is_early():
    return lax.axis_index("lon") < lax.axis_size("lon") // 4


def is_odd_lon():
    return lax.rem(lax.axis_index("lon"), 2) == 1


class Either:
    def __init__(self, flag, yes, no):
        self.flag, self.yes, self.no = flag, yes, no

    def __getitem__(self, index):
        return jnp.where(self.flag, self.yes[index], self.no[index])


def near_refs(first, second):
    odd_lon = is_odd_lon()
    return Either(odd_lon, second, first), Either(odd_lon, first, second)


def first_rows_kernel(t_ref, s_ref, u_ref, v_ref, m_ref, opp_ref, after, out, ints, sems):
    start = pl.multiple_of(jnp.where(is_odd(), t_ref.shape[1] - HALO, 0), 8)
    copies = [pltpu.make_async_copy(opp_ref, ints.at[pl.ds(8, 1), :], sems.at[5])]
    for i, ref in enumerate((t_ref, s_ref, u_ref, v_ref, m_ref)):
        target = out.at[pl.ds(8 * i, 8), :] if i < FIELDS else ints.at[pl.ds(0, 8), :]
        copies.append(
            pltpu.make_async_copy(ref.at[0, pl.ds(start, HALO), :], target, sems.at[i])
        )
    for copy in copies:
        copy.start()
    for copy in copies:
        copy.wait()
    out[32:40, :] = ints[0:8, :].astype(jnp.float32)
    out[40:48, :] = jnp.broadcast_to(ints[8:9, :].astype(jnp.float32), (8, LANES))


def add_columns(e, w, tile, g):
    lane = lane_index()
    slots = ([g] if g < STRIP else []) + ([g - STRIP_STEP + STRIP] if g >= STRIP_STEP else [])
    for slot in slots:
        here = (lane >= 8 * slot) & (lane < 8 * slot + 8)
        e = jnp.where(here, roll(tile, 8 * slot - (LANES - HALO)), e)
        w = jnp.where(here, roll(tile, 8 * slot), w)
    return e, w


def pair_kernel(height, e_in, w_in, sb_ref, ra_ref, rb_ref, first, second):
    odd, odd_lon = is_odd(), is_odd_lon()
    for i in range(5):
        at = slice(i * 8, i * 8 + 8)
        ra, rb = ra_ref[at, :], rb_ref[at, :]
        e, w = add_columns(e_in[at, :], w_in[at, :], jnp.where(odd, ra, rb), 0)
        e, w = add_columns(e, w, jnp.where(odd, rb, ra), height // 8 + 1)
        first[at, :] = jnp.where(odd_lon, e, w)
        second[at, :] = jnp.where(odd_lon, w, e)

    @pl.when(is_top())
    def _():
        for ref in (first, second):
            ref[40 : 40 + CAP, :] = sb_ref[...]
            ref[40 + CAP : 40 + 2 * CAP, :] = rb_ref[...]


def far_places(counts):
    base = 0
    for j, n in enumerate(counts):
        for side in (0, 1):
            yield j, side, n, base
            base += 5 * n + 1


def far_kernel(sb_ref, rb_ref, first_in, second_in, first, second):
    @pl.when(is_top())
    def _():
        far_flag = jnp.logical_not(is_odd_lon())
        rw_ref, re_ref = near_refs(first_in, second_in)
        sources = (
            ((rw_ref, 40), (rw_ref, 40 + CAP)),
            ((sb_ref, 0), (rb_ref, 0)),
            ((re_ref, 40), (re_ref, 40 + CAP)),
        )

        def fill(out, counts):
            for j, side, n, base in far_places(counts):
                ref, at = sources[j][side]
                for i in range(5):
                    out[base + i * n : base + i * n + n, :] = ref[
                        at + 8 * i + 8 - n : at + 8 * i + 8, :
                    ]
                out[base + 5 * n : base + 5 * n + 1, :] = ref[at + 40 : at + 41, :]
            out[FAR - 2 : FAR, :] = jnp.zeros((2, LANES), jnp.float32)

        @pl.when(far_flag)
        def _():
            fill(first, FAR_ROWS)
            fill(second, FAR_ROWS[::-1])

        @pl.when(jnp.logical_not(far_flag))
        def _():
            fill(first, FAR_ROWS[::-1])
            fill(second, FAR_ROWS)


def first_pass(centre, north, south, east, west, stat, w_s):
    sea, count, w_e, w_n, turn = stat
    laps = [
        sea * (((east[i] + west[i]) + (north[i] + south[i])) - count * centre[i])
        for i in range(FIELDS)
    ]
    t, s, u, v = centre
    flow_e = (0.25 * TIME_STEP) * w_e * (u + east[2])
    flow_n = (0.25 * TIME_STEP) * w_n * (v + north[3])
    flow_s = (0.25 * TIME_STEP) * w_s * (v + south[3])
    partial, flux = [], []
    for i in (0, 1):
        c = centre[i]
        flux.append(flow_e * (c + east[i]))
        partial.append(c - (flow_n * (c + north[i]) - flow_s * (c + south[i])))
    ratio = EXPAND / CONTRACT
    slope = 0.25 * TIME_STEP * CONTRACT
    q = s - ratio * t
    q_e = east[1] - ratio * east[0]
    q_n = north[1] - ratio * north[0]
    q_s = south[1] - ratio * south[0]
    flux.append(slope * w_e * (q_e - q))
    partial.append(u + turn * v)
    partial.append(v - (turn * u + slope * (w_n * (q_n - q) + w_s * (q - q_s))))
    return laps, partial, flux


def face_terms(i, lap, east, w_e, flux):
    mix = (TIME_STEP * DIFFUSE) * w_e * (east - lap)
    if i < 2:
        return flux + mix, flux + mix
    if i == 2:
        return flux + mix, mix - flux
    return mix, mix


def second_pass(partial, loss, gain, lap, north, south, sea, count_ns):
    mix = (TIME_STEP * DIFFUSE) * ((north + south) - count_ns * lap)
    return sea * (partial - ((loss - gain) + mix))


class Band:
    def __init__(self, state, laps, part, flux, stat):
        self.state, self.laps, self.part, self.flux, self.stat = state, laps, part, flux, stat
        self.rows = range(8, state.shape[1] - 8, 8)

    def pad(self):
        nothing = jnp.zeros((8, LANES), jnp.float32)
        for row in (0, self.rows[-1] + 8):
            for i in range(FIELDS):
                self.state[i, row : row + 8, :] = nothing
                self.laps[i, row : row + 8, :] = nothing
            for i in range(STATS):
                self.stat[i, row : row + 8, :] = nothing

    def weigh(self, turning):
        for r in self.rows:
            at = slice(r, r + 8)
            sea = self.stat[0, at, :]
            north, south = self.stat[0, r + 1 : r + 9, :], self.stat[0, r - 1 : r + 7, :]
            east, west = roll(sea, -1), roll(sea, 1)
            self.stat[1, at, :] = (east + west) + (north + south)
            self.stat[2, at, :] = sea * east
            self.stat[3, at, :] = sea * north
            self.stat[4, at, :] = turning(r)
            self.stat[5, at, :] = north + south
            for i in range(FIELDS):
                self.state[i, at, :] = sea * self.state[i, at, :]

    def step(self, kept=None):
        kept = self.rows if kept is None else kept
        for r in self.rows:
            at, up, down = slice(r, r + 8), slice(r + 1, r + 9), slice(r - 1, r + 7)
            centre = [self.state[i, at, :] for i in range(FIELDS)]
            lap, partial, flux = first_pass(
                centre,
                [self.state[i, up, :] for i in range(FIELDS)],
                [self.state[i, down, :] for i in range(FIELDS)],
                [roll(x, -1) for x in centre],
                [roll(x, 1) for x in centre],
                [self.stat[i, at, :] for i in range(5)],
                self.stat[3, down, :],
            )
            for i in range(FIELDS):
                self.laps[i, at, :] = lap[i]
                if r in kept:
                    self.part[i, at, :] = partial[i]
                    if i < 3:
                        self.flux[i, at, :] = flux[i]
        for r in kept:
            at, up, down = slice(r, r + 8), slice(r + 1, r + 9), slice(r - 1, r + 7)
            sea, w_e, count_ns = (self.stat[i, at, :] for i in (0, 2, 5))
            for i in range(FIELDS):
                lap = self.laps[i, at, :]
                flux = self.flux[i, at, :] if i < 3 else None
                loss, gain = face_terms(i, lap, roll(lap, -1), w_e, flux)
                self.state[i, at, :] = second_pass(
                    self.part[i, at, :],
                    loss,
                    roll(gain, 1),
                    lap,
                    self.laps[i, up, :],
                    self.laps[i, down, :],
                    sea,
                    count_ns,
                )


def strip_own(low, high):
    lane = lane_index()
    second = lane >= 64
    west = jnp.where(second, roll(high, 72), roll(low, 8))
    east = jnp.where(second, roll(high, 112), roll(low, 48))
    return jnp.where(lax.rem(lane, 64) < 32, west, east)


def prepare(refs, fields, a_ref, e_ref, w_ref, inner, strip, ints, state, laps, part, flux, stat, sems):
    height = fields.shape[1]
    total_rows = height * lax.axis_size("lat")
    copies = []
    for i, ref in enumerate(refs):
        target = fields.at[i] if i < FIELDS else ints
        copies.append(pltpu.make_async_copy(ref.at[0], target, sems.at[i]))
    for copy in copies:
        copy.start()
    for copy in copies:
        copy.wait()
    fields[FIELDS] = ints[...].astype(jnp.float32)
    odd = is_odd()
    bands = Band(state, laps, part, flux, stat)
    bands.pad()
    for i in range(5):
        tiles = [fields[i, 8 * g : 8 * g + 8, :] for g in range(height // 8)]
        a_ref[i * 8 : i * 8 + 8, :] = jnp.where(odd, tiles[0], tiles[-1])
        e = w = jnp.zeros((8, LANES), jnp.float32)
        ref, at = (state, i) if i < FIELDS else (stat, 0)
        for g, tile in enumerate(tiles):
            e, w = add_columns(e, w, tile, g + 1)
            ref[at, 8 + 8 * g : 16 + 8 * g, :] = tile
        e_ref[i * 8 : i * 8 + 8, :] = e
        w_ref[i * 8 : i * 8 + 8, :] = w
        for n in range(STRIP):
            low, high = tiles[max(n - 1, 0)], tiles[min(n + STRIP_STEP - 1, len(tiles) - 1)]
            strip[i, 8 * n : 8 * n + 8, :] = strip_own(low, high)
    base_row = (lax.axis_index("lat") * height).astype(jnp.float32)
    sub = row_in_tile()
    bands.weigh(lambda r: turning_of(base_row + float(r - 8) + sub, total_rows))

    def step(n, carry):
        bands.step()
        return carry

    lax.fori_loop(0, STEPS, step, 0)
    for i in range(FIELDS):
        for g in range(height // 8):
            inner[i, 8 * g : 8 * g + 8, :] = state[i, 8 + 8 * g : 16 + 8 * g, :]


def early_kernel(*refs):
    @pl.when(is_early())
    def _():
        prepare(refs[:5], *refs[5:])


def late_kernel(*refs):
    early = is_early()

    @pl.when(early)
    def _():
        for source, target in zip(refs[6:12], refs[12:18]):
            target[...] = source[...]

    @pl.when(jnp.logical_not(early))
    def _():
        prepare(refs[:5], *refs[12:])


def strip_ghosts(blocks, old):
    before, here, after = blocks
    lane = lane_index(here.shape[0])
    new = jnp.where(lane < 96, roll(here, 72), roll(here, 112))
    new = jnp.where(lane < 72, roll(before, 64 - (LANES - HALO)), new)
    new = jnp.where(lane >= 112, roll(after, 112), new)
    return jnp.where(lane < 64, old, new)


def join_columns(centre, strip, second):
    lane = lane_index()
    start = 64 if second else 0
    west, east = roll(strip, -start - HALO), roll(strip, LANES - HALO - start - 40)
    return jnp.where(lane < HALO, west, jnp.where(lane >= LANES - HALO, east, centre))


def turning_of(row, total_rows):
    return (TIME_STEP * ROTATION) * (2.0 * (row + 0.5) / total_rows - 1.0)


def row_in_tile():
    return lax.broadcasted_iota(jnp.int32, (8, LANES), 0).astype(jnp.float32)


def frame_kernel(
    fields,
    strip,
    inner,
    sb_ref,
    ra_ref,
    rb_ref,
    first_in,
    second_in,
    t_out,
    s_out,
    u_out,
    v_out,
    upper_state,
    upper_stat,
    state,
    laps,
    part,
    flux,
    stat,
):
    rw_ref, re_ref = near_refs(first_in, second_in)
    odd, top = is_odd(), is_top()
    lane = lane_index()
    height = fields.shape[1]
    total_rows = height * lax.axis_size("lat")
    north_row, strip_row = 8 + UPPER, 8 + 2 * UPPER
    bands = Band(state, laps, part, flux, stat)
    bands.pad()
    side = lax.rem(lane, 64)

    for i in range(5):
        at = slice(i * 8, i * 8 + 8)
        ra, rb, from_w, from_e = ra_ref[at, :], rb_ref[at, :], rw_ref[at, :], re_ref[at, :]
        south, north = jnp.where(odd, ra, rb), jnp.where(odd, rb, ra)
        ref, at = (state, i) if i < FIELDS else (stat, 0)
        ref[at, 8:16, :] = south
        ref[at, 16 : 8 + UPPER, :] = fields[i, 0 : UPPER - 8, :]
        ref[at, north_row : north_row + UPPER - 8, :] = fields[i, height - UPPER + 8 : height, :]
        ref[at, north_row + UPPER - 8 : strip_row, :] = north
        for n in range(STRIP):
            own = strip[i, 8 * n : 8 * n + 8, :]
            if n == 0:
                own = jnp.where(lane < 64, strip_own(south, south), own)
            if n == STRIP - 1:
                own = jnp.where(lane >= 64, strip_own(north, north), own)
            own = jnp.where(side < HALO, roll(from_w, -8 * n), own)
            own = jnp.where(side >= 48, roll(from_e, 48 - 8 * n), own)
            ref[at, strip_row + 8 * n : strip_row + 8 * n + 8, :] = own

    @pl.when(top)
    def _():
        pairs = (
            (rw_ref, 40, rw_ref, 40 + CAP),
            (sb_ref, 0, rb_ref, 0),
            (re_ref, 40, re_ref, 40 + CAP),
        )
        for i in range(5):
            ghosts = []
            for own, own_at, facing, facing_at in pairs:
                index = lax.rem(own[own_at + 40 : own_at + 48, :].astype(jnp.int32), LANES)
                rows = facing[facing_at + 8 * i : facing_at + 8 * i + 8, :]
                ghosts.append(
                    (PARITY + (1.0,))[i]
                    * jnp.take_along_axis(rows, index, axis=1, mode="promise_in_bounds")
                )
            ref, at = (state, i) if i < FIELDS else (stat, 0)
            row = north_row + UPPER - HALO
            ref[at, row : row + 1, :] = ghosts[1][7:8, :]
            ref[at, row + 1 : row + 2, :] = ghosts[1][6:7, :]
            for n in (0, 1):
                row = strip_row + 8 * STRIP - HALO + n
                ref[at, row : row + 1, :] = strip_ghosts(
                    [ghost[7 - n : 8 - n, :] for ghost in ghosts], ref[at, row : row + 1, :]
                )

    base_row = (lax.axis_index("lat") * height - HALO).astype(jnp.float32)
    sub = row_in_tile()
    second = jnp.where(lane >= 64, 8.0 * STRIP_STEP, 0.0)

    def turning(r):
        if r < north_row:
            row = base_row + float(r - 8) + sub
        elif r < strip_row:
            row = base_row + float(height + 2 * HALO - UPPER + r - north_row) + sub
        else:
            row = base_row + float(r - strip_row) + sub + second
        return turning_of(row, total_rows)

    bands.weigh(turning)

    def step(n, carry):
        bands.step()

        @pl.when(top & (n == 0))
        def _():
            for which, row in enumerate((north_row, strip_row + 8 * STRIP - UPPER)):
                for i in range(FIELDS):
                    upper_state[i, which] = state[i, row : row + UPPER, :]
                for i in range(STATS):
                    upper_stat[i, which] = stat[i, row : row + UPPER, :]

        return carry

    lax.fori_loop(0, STEPS, step, 0)

    tiles_n = height // 8
    for i, out in enumerate((t_out, s_out, u_out, v_out)):
        for g in range(tiles_n):
            if g == 0:
                centre = state[i, 16:24, :]
            elif g == tiles_n - 1:
                centre = state[i, north_row + 8 : north_row + 16, :]
            else:
                centre = inner[i, 8 * g : 8 * g + 8, :]
            late = g + 1 > STRIP_STEP
            row = strip_row + 8 * (g + 1 - (STRIP_STEP if late else 0))
            out[0, 8 * g : 8 * g + 8, :] = join_columns(centre, state[i, row : row + 8, :], late)


def arc_east(blocks):
    lane, last = lane_index(), len(blocks) - 1
    e = [roll(x, -1) for x in blocks]
    return [jnp.where(lane == LANES - 1, e[min(k + 1, last)], e[k]) for k in range(last + 1)]


def arc_west(blocks):
    lane = lane_index()
    w = [roll(x, 1) for x in blocks]
    return [jnp.where(lane == 0, w[max(k - 1, 0)], w[k]) for k in range(len(blocks))]


def cap_kernel(
    t_in,
    s_in,
    u_in,
    v_in,
    upper_state,
    upper_stat,
    sb_ref,
    rb_ref,
    first_in,
    second_in,
    first_far,
    second_far,
    t_out,
    s_out,
    u_out,
    v_out,
    state,
    laps,
    part,
    flux,
    stat,
    cap,
    cap_lap,
    cap_part,
    cap_flux,
    cap_stat,
    cap_opp,
    rows_out,
    sems,
):
    rw_ref, re_ref = near_refs(first_in, second_in)
    far_flag = jnp.logical_not(is_odd_lon())
    w3_ref = Either(far_flag, second_far, first_far)
    e3_ref = Either(far_flag, first_far, second_far)
    lane = lane_index()
    height = t_out.shape[1]
    total_rows = height * lax.axis_size("lat")
    bands = Band(state, laps, part, flux, stat)
    nothing = jnp.zeros((8, LANES), jnp.float32)
    cap_turn = turning_of(float(total_rows - HALO + 1) + row_in_tile(), total_rows)

    def fill_ghosts(ref, parities, low, high, sides):
        for side in range(sides):
            ghosts = {}
            for k in range(low, high):
                index = cap_opp[side, k]
                for i, parity in enumerate(parities):
                    rows = ref[1 - side, i, ARC - 1 - k, 0:8, :]
                    ghosts[k, i] = parity * jnp.take_along_axis(
                        rows, index, axis=1, mode="promise_in_bounds"
                    )
            for (k, i), ghost in ghosts.items():
                ref[side, i, k, 8:9, :] = ghost[7:8, :]
                ref[side, i, k, 9:10, :] = ghost[6:7, :]

    def put_block(side, place, ref, base, n):
        sea = ref[base + 4 * n : base + 5 * n, :]
        cap_stat[side, 0, place, 8 - n : 8, :] = sea
        cap_stat[side, 0, place, 10:16, :] = nothing[0:6]
        if n < 8:
            cap_stat[side, 0, place, 0 : 8 - n, :] = nothing[n:8]
        for i in range(FIELDS):
            cap[side, i, place, 8 - n : 8, :] = sea * ref[base + n * i : base + n * i + n, :]
            if n < 8:
                cap[side, i, place, 0 : 8 - n, :] = nothing[n:8]
            cap[side, i, place, 10:16, :] = nothing[0:6]
            cap_lap[side, i, place, 0:8, :] = nothing
            cap_lap[side, i, place, 8:16, :] = nothing
        opp = jnp.broadcast_to(ref[base + 5 * n : base + 5 * n + 1, :], (8, LANES))
        cap_opp[side, place] = lax.rem(opp.astype(jnp.int32), LANES)

    def cap_weigh():
        for side in (0, 1):
            for start in (0, 1):
                seas = [cap_stat[side, 0, k, start : start + 8, :] for k in range(ARC)]
                east, west = arc_east(seas), arc_west(seas)
                for k in range(ARC):
                    north = cap_stat[side, 0, k, start + 1 : start + 9, :]
                    if start:
                        south = cap_stat[side, 0, k, start - 1 : start + 7, :]
                        cap_stat[side, 1, k, 1:9, :] = (east[k] + west[k]) + (north + south)
                        cap_stat[side, 4, k, 1:9, :] = north + south
                    cap_stat[side, 2, k, start : start + 8, :] = seas[k] * east[k]
                    cap_stat[side, 3, k, start : start + 8, :] = seas[k] * north

    def cap_first(side, low, high):
        span = range(low - 1, high + 1)
        fields = [[cap[side, i, k, 1:9, :] for k in span] for i in range(FIELDS)]
        east, west = [arc_east(f) for f in fields], [arc_west(f) for f in fields]
        for n, k in enumerate(span):
            lap, partial, fluxes = first_pass(
                [f[n] for f in fields],
                [cap[side, i, k, 2:10, :] for i in range(FIELDS)],
                [cap[side, i, k, 0:8, :] for i in range(FIELDS)],
                [f[n] for f in east],
                [f[n] for f in west],
                [cap_stat[side, i, k, 1:9, :] for i in range(4)] + [cap_turn],
                cap_stat[side, 3, k, 0:8, :],
            )
            for i in range(FIELDS):
                cap_lap[side, i, k, 1:9, :] = lap[i]
                if i < 3:
                    cap_flux[side, i, k, 0:8, :] = fluxes[i]
                if low <= k < high:
                    cap_part[side, i, k, 0:8, :] = partial[i]

    def cap_second(side, low, high):
        span = range(low - 1, high + 1)
        for i in range(FIELDS):
            blocks = [cap_lap[side, i, k, 1:9, :] for k in span]
            terms = [
                face_terms(
                    i,
                    blocks[n],
                    east,
                    cap_stat[side, 2, span[n], 1:9, :],
                    cap_flux[side, i, span[n], 0:8, :] if i < 3 else None,
                )
                for n, east in enumerate(arc_east(blocks))
            ]
            gains = arc_west([gain for _, gain in terms])
            for n, k in enumerate(span):
                if low <= k < high:
                    cap[side, i, k, 1:9, :] = second_pass(
                        cap_part[side, i, k, 0:8, :],
                        terms[n][0],
                        gains[n],
                        blocks[n],
                        cap_lap[side, i, k, 2:10, :],
                        cap_lap[side, i, k, 0:8, :],
                        cap_stat[side, 0, k, 1:9, :],
                        cap_stat[side, 4, k, 1:9, :],
                    )

    @pl.when(is_top())
    def _():
        parts = [(j, side, w3_ref, base, n) for j, side, n, base in far_places(FAR_ROWS)]
        parts += [
            (j + REACH + 2, side, e3_ref, base, n)
            for j, side, n, base in far_places(FAR_ROWS[::-1])
        ]
        for side in (0, 1):
            parts.append((REACH - 1, side, rw_ref, 40 + CAP * side, 8))
            parts.append((REACH, side, (sb_ref, rb_ref)[side], 0, 8))
            parts.append((REACH + 1, side, re_ref, 40 + CAP * side, 8))
        for k, side, ref, base, n in parts:
            put_block(side, ARC - 1 - k if side else k, ref, base, n)
        bands.pad()
        for which in (0, 1):
            row = 8 + UPPER * which
            for i in range(FIELDS):
                state[i, row : row + UPPER, :] = upper_state[i, which]
            for i in range(STATS):
                stat[i, row : row + UPPER, :] = upper_stat[i, which]
        fill_ghosts(cap_stat, (1.0,), 0, ARC, 2)
        fill_ghosts(cap, PARITY, 0, ARC, 2)
        cap_weigh()
        for n in range(STEPS - 1):
            low, high = n + 1, ARC - 1 - n
            first_side = 1 if n == STEPS - 2 else 0

            def one(side, carry, low=low, high=high):
                cap_first(side, low, high)
                cap_second(side, low, high)
                return carry

            lax.fori_loop(first_side, 2, one, 0)
            fill_ghosts(cap, PARITY, low, high, 2 - first_side)
            for i in range(FIELDS):
                ghosts = [cap[0, i, k, 8:10, :] for k in (REACH - 1, REACH, REACH + 1)]
                row = 8 + UPPER - HALO
                state[i, row : row + 2, :] = ghosts[1]
                row += UPPER
                state[i, row : row + 2, :] = strip_ghosts(ghosts, state[i, row : row + 2, :])
            start = 16 if n == STEPS - 2 else 8
            bands.step([r + UPPER * which for which in (0, 1) for r in range(start, 24, 8)])
        copies = []
        for i, out in enumerate((t_out, s_out, u_out, v_out)):
            row = 8 + UPPER - 2 * HALO
            rows_out[i] = join_columns(
                state[i, row : row + 8, :], state[i, row + UPPER : row + UPPER + 8, :], True
            )
            copies.append(
                pltpu.make_async_copy(
                    rows_out.at[i], out.at[0, pl.ds(height - HALO, HALO), :], sems.at[i]
                )
            )
        for copy in copies:
            copy.start()
        for copy in copies:
            copy.wait()


def body(lon_count, lat_count, t, s, u, v, m, opp):
    fields = (t, s, u, v, m)
    height = t.shape[1]
    vmem, anywhere = (
        pl.BlockSpec(memory_space=pltpu.VMEM),
        pl.BlockSpec(memory_space=pltpu.HBM),
    )
    f32, i32 = jnp.float32, jnp.int32

    def call(kernel, inputs, shapes, scratch=(), far=0, flops=0):
        inputs = [
            pltpu.with_memory_space_constraint(x, pltpu.HBM) if i < far else x
            for i, x in enumerate(inputs)
        ]
        return pl.pallas_call(
            kernel,
            out_shape=[jax.ShapeDtypeStruct(shape, f32) for shape in shapes],
            in_specs=[anywhere] * far + [vmem] * (len(inputs) - far),
            out_specs=[vmem] * len(shapes),
            scratch_shapes=list(scratch),
            compiler_params=pltpu.CompilerParams(vmem_limit_bytes=32 * 1024 * 1024),
            cost_estimate=pl.CostEstimate(flops=flops, bytes_accessed=flops, transcendentals=0),
        )(*inputs)

    def place(lon, lat):
        return (lon % lon_count) * lat_count + lat

    lons, lats = range(lon_count), range(lat_count)
    last = lat_count - 1
    pairs_a = [(place(i, j), place(i, j ^ 1)) for i in lons for j in lats]
    pairs_b = [(place(i, j), place(i, ((j - 1) ^ 1) + 1)) for i in lons for j in lats[1:last]]
    pairs_b += [(place(i, last), place(-i, last)) for i in lons]

    def swap(x, by, rest, rows):
        pairs = []
        for i in lons:
            other = i + by if i % 2 == rest else i - by
            pairs += [(place(i, j), place(other, j)) for j in rows]
        return exchange(x, pairs)

    def exchange(x, pairs):
        return lax.ppermute(x, ("lon", "lat"), pairs)

    def band_scratch(rows):
        return [
            pltpu.VMEM((n, 16 + rows, LANES), f32) for n in (FIELDS, FIELDS, FIELDS, 3, STATS)
        ]

    prepared = [(5, height, LANES), (40, LANES), (40, LANES), (40, LANES)]
    prepared += [(FIELDS, height, LANES), (5, 8 * STRIP, LANES)]
    scratch = [pltpu.VMEM((height, LANES), i32), *band_scratch(height), pltpu.SemaphoreType.DMA((5,))]
    own = call(early_kernel, fields, prepared, scratch, far=5, flops=10**7)
    (send_b,) = call(
        first_rows_kernel,
        (*fields, opp.reshape(1, LANES), own[1]),
        [(CAP, LANES)],
        [pltpu.VMEM((16, LANES), i32), pltpu.SemaphoreType.DMA((6,))],
        far=6,
    )
    from_b = exchange(send_b, pairs_b)
    stack, send_a, columns_e, columns_w, inner, strip = call(
        late_kernel, (*fields, send_b, *own), prepared, scratch, far=5, flops=10**7
    )
    from_a = exchange(send_a, pairs_a)
    send_1, send_2 = call(
        functools.partial(pair_kernel, height),
        (columns_e, columns_w, send_b, from_a, from_b),
        [(40 + 2 * CAP, LANES)] * 2,
    )
    near_1 = swap(send_1, 1, 1, lats)
    near_2 = swap(send_2, 1, 0, lats)
    far_send_1, far_send_2 = call(
        far_kernel, (send_b, from_b, near_1, near_2), [(FAR, LANES)] * 2
    )
    far_1 = swap(far_send_1, 3, 0, [last])
    far_2 = swap(far_send_2, 3, 1, [last])

    *outs, upper_state, upper_stat = call(
        frame_kernel,
        (stack, strip, inner, send_b, from_a, from_b, near_1, near_2),
        [t.shape] * 4 + [(FIELDS, 2, UPPER, LANES), (STATS, 2, UPPER, LANES)],
        band_scratch(2 * UPPER + 8 * STRIP),
        flops=10**7,
    )
    return tuple(
        pl.pallas_call(
            cap_kernel,
            out_shape=[jax.ShapeDtypeStruct(t.shape, f32)] * 4,
            in_specs=[anywhere] * 4 + [vmem] * 8,
            out_specs=[anywhere] * 4,
            scratch_shapes=band_scratch(2 * UPPER)
            + [
                pltpu.VMEM((2, FIELDS, ARC, 16, LANES), f32),
                pltpu.VMEM((2, FIELDS, ARC, 16, LANES), f32),
                pltpu.VMEM((2, FIELDS, ARC, 8, LANES), f32),
                pltpu.VMEM((2, 3, ARC, 8, LANES), f32),
                pltpu.VMEM((2, 5, ARC, 16, LANES), f32),
                pltpu.VMEM((2, ARC, 8, LANES), i32),
                pltpu.VMEM((FIELDS, 8, LANES), f32),
                pltpu.SemaphoreType.DMA((FIELDS,)),
            ],
            input_output_aliases={i: i for i in range(4)},
            compiler_params=pltpu.CompilerParams(vmem_limit_bytes=32 * 1024 * 1024),
        )(*outs, upper_state, upper_stat, send_b, from_b, near_1, near_2, far_1, far_2)
    )


def solution(mesh):
    placed = P(None, "lat", "lon")
    return jax.shard_map(
        functools.partial(body, mesh.shape["lon"], mesh.shape["lat"]),
        mesh=mesh,
        in_specs=(placed,) * 5 + (P("lon"),),
        out_specs=(placed,) * 4,
        check_vma=False,
    )
```

```python
import functools

import jax
import jax.numpy as jnp
from jax import lax
from jax.experimental import pallas as pl
from jax.experimental.pallas import tpu as pltpu
from jax.sharding import PartitionSpec as P

STEPS = 4
TIME_STEP = 0.1
DIFFUSE = 0.15
EXPAND = 0.2
CONTRACT = 0.8
ROTATION = 0.5

HALO = 2 * STEPS
LANES = 128
FIELDS = 4
REACH = 4
ARC = 2 * REACH + 1
CAP = 48
PARITY = (1.0, 1.0, -1.0, -1.0)
STATS = 6
STRIP = 8
STRIP_STEP = 6
FAR_ROWS = (2, 4, 6)
FAR = 128
UPPER = 24


def lane_index(rows=8):
    return lax.broadcasted_iota(jnp.int32, (rows, LANES), 1)


def roll(x, shift):
    shift = shift % LANES
    return x if shift == 0 else pltpu.roll(x, shift, 1)


def is_odd():
    return lax.rem(lax.axis_index("lat"), 2) == 1


def is_top():
    return lax.axis_index("lat") == lax.axis_size("lat") - 1


def is_early():
    return lax.axis_index("lon") < lax.axis_size("lon") // 4


def is_odd_lon():
    return lax.rem(lax.axis_index("lon"), 2) == 1


class Either:
    def __init__(self, flag, yes, no):
        self.flag, self.yes, self.no = flag, yes, no

    def __getitem__(self, index):
        return jnp.where(self.flag, self.yes[index], self.no[index])


def near_refs(first, second):
    odd_lon = is_odd_lon()
    return Either(odd_lon, second, first), Either(odd_lon, first, second)


def first_rows_kernel(t_ref, s_ref, u_ref, v_ref, m_ref, opp_ref, after, out, ints, sems):
    start = pl.multiple_of(jnp.where(is_odd(), t_ref.shape[1] - HALO, 0), 8)
    copies = [pltpu.make_async_copy(opp_ref, ints.at[pl.ds(8, 1), :], sems.at[5])]
    for i, ref in enumerate((t_ref, s_ref, u_ref, v_ref, m_ref)):
        target = out.at[pl.ds(8 * i, 8), :] if i < FIELDS else ints.at[pl.ds(0, 8), :]
        copies.append(
            pltpu.make_async_copy(ref.at[0, pl.ds(start, HALO), :], target, sems.at[i])
        )
    for copy in copies:
        copy.start()
    for copy in copies:
        copy.wait()
    out[32:40, :] = ints[0:8, :].astype(jnp.float32)
    out[40:48, :] = jnp.broadcast_to(ints[8:9, :].astype(jnp.float32), (8, LANES))


def add_columns(e, w, tile, g):
    lane = lane_index()
    slots = ([g] if g < STRIP else []) + ([g - STRIP_STEP + STRIP] if g >= STRIP_STEP else [])
    for slot in slots:
        here = (lane >= 8 * slot) & (lane < 8 * slot + 8)
        e = jnp.where(here, roll(tile, 8 * slot - (LANES - HALO)), e)
        w = jnp.where(here, roll(tile, 8 * slot), w)
    return e, w


def pair_kernel(height, e_in, w_in, sb_ref, ra_ref, rb_ref, first, second):
    odd, odd_lon = is_odd(), is_odd_lon()
    for i in range(5):
        at = slice(i * 8, i * 8 + 8)
        ra, rb = ra_ref[at, :], rb_ref[at, :]
        e, w = add_columns(e_in[at, :], w_in[at, :], jnp.where(odd, ra, rb), 0)
        e, w = add_columns(e, w, jnp.where(odd, rb, ra), height // 8 + 1)
        first[at, :] = jnp.where(odd_lon, e, w)
        second[at, :] = jnp.where(odd_lon, w, e)

    @pl.when(is_top())
    def _():
        for ref in (first, second):
            ref[40 : 40 + CAP, :] = sb_ref[...]
            ref[40 + CAP : 40 + 2 * CAP, :] = rb_ref[...]


def far_places(counts):
    base = 0
    for j, n in enumerate(counts):
        for side in (0, 1):
            yield j, side, n, base
            base += 5 * n + 1


def far_kernel(sb_ref, rb_ref, first_in, second_in, first, second):
    @pl.when(is_top())
    def _():
        far_flag = jnp.logical_not(is_odd_lon())
        rw_ref, re_ref = near_refs(first_in, second_in)
        sources = (
            ((rw_ref, 40), (rw_ref, 40 + CAP)),
            ((sb_ref, 0), (rb_ref, 0)),
            ((re_ref, 40), (re_ref, 40 + CAP)),
        )

        def fill(out, counts):
            for j, side, n, base in far_places(counts):
                ref, at = sources[j][side]
                for i in range(5):
                    out[base + i * n : base + i * n + n, :] = ref[
                        at + 8 * i + 8 - n : at + 8 * i + 8, :
                    ]
                out[base + 5 * n : base + 5 * n + 1, :] = ref[at + 40 : at + 41, :]
            out[FAR - 2 : FAR, :] = jnp.zeros((2, LANES), jnp.float32)

        @pl.when(far_flag)
        def _():
            fill(first, FAR_ROWS)
            fill(second, FAR_ROWS[::-1])

        @pl.when(jnp.logical_not(far_flag))
        def _():
            fill(first, FAR_ROWS[::-1])
            fill(second, FAR_ROWS)


def first_pass(centre, north, south, east, west, stat, w_s):
    sea, count, w_e, w_n, turn = stat
    laps = [
        sea * (((east[i] + west[i]) + (north[i] + south[i])) - count * centre[i])
        for i in range(FIELDS)
    ]
    t, s, u, v = centre
    flow_e = (0.25 * TIME_STEP) * w_e * (u + east[2])
    flow_n = (0.25 * TIME_STEP) * w_n * (v + north[3])
    flow_s = (0.25 * TIME_STEP) * w_s * (v + south[3])
    partial, flux = [], []
    for i in (0, 1):
        c = centre[i]
        flux.append(flow_e * (c + east[i]))
        partial.append(c - (flow_n * (c + north[i]) - flow_s * (c + south[i])))
    ratio = EXPAND / CONTRACT
    slope = 0.25 * TIME_STEP * CONTRACT
    q = s - ratio * t
    q_e = east[1] - ratio * east[0]
    q_n = north[1] - ratio * north[0]
    q_s = south[1] - ratio * south[0]
    flux.append(slope * w_e * (q_e - q))
    partial.append(u + turn * v)
    partial.append(v - (turn * u + slope * (w_n * (q_n - q) + w_s * (q - q_s))))
    return laps, partial, flux


def face_terms(i, lap, east, w_e, flux):
    mix = (TIME_STEP * DIFFUSE) * w_e * (east - lap)
    if i < 2:
        return flux + mix, flux + mix
    if i == 2:
        return flux + mix, mix - flux
    return mix, mix


def second_pass(partial, loss, gain, lap, north, south, sea, count_ns):
    mix = (TIME_STEP * DIFFUSE) * ((north + south) - count_ns * lap)
    return sea * (partial - ((loss - gain) + mix))


class Band:
    def __init__(self, state, laps, part, flux, stat):
        self.state, self.laps, self.part, self.flux, self.stat = state, laps, part, flux, stat
        self.rows = range(8, state.shape[1] - 8, 8)

    def pad(self):
        nothing = jnp.zeros((8, LANES), jnp.float32)
        for row in (0, self.rows[-1] + 8):
            for i in range(FIELDS):
                self.state[i, row : row + 8, :] = nothing
                self.laps[i, row : row + 8, :] = nothing
            for i in range(STATS):
                self.stat[i, row : row + 8, :] = nothing

    def weigh(self, turning):
        for r in self.rows:
            at = slice(r, r + 8)
            sea = self.stat[0, at, :]
            north, south = self.stat[0, r + 1 : r + 9, :], self.stat[0, r - 1 : r + 7, :]
            east, west = roll(sea, -1), roll(sea, 1)
            self.stat[1, at, :] = (east + west) + (north + south)
            self.stat[2, at, :] = sea * east
            self.stat[3, at, :] = sea * north
            self.stat[4, at, :] = turning(r)
            self.stat[5, at, :] = north + south
            for i in range(FIELDS):
                self.state[i, at, :] = sea * self.state[i, at, :]

    def step(self, kept=None):
        kept = self.rows if kept is None else kept
        for r in self.rows:
            at, up, down = slice(r, r + 8), slice(r + 1, r + 9), slice(r - 1, r + 7)
            centre = [self.state[i, at, :] for i in range(FIELDS)]
            lap, partial, flux = first_pass(
                centre,
                [self.state[i, up, :] for i in range(FIELDS)],
                [self.state[i, down, :] for i in range(FIELDS)],
                [roll(x, -1) for x in centre],
                [roll(x, 1) for x in centre],
                [self.stat[i, at, :] for i in range(5)],
                self.stat[3, down, :],
            )
            for i in range(FIELDS):
                self.laps[i, at, :] = lap[i]
                if r in kept:
                    self.part[i, at, :] = partial[i]
                    if i < 3:
                        self.flux[i, at, :] = flux[i]
        for r in kept:
            at, up, down = slice(r, r + 8), slice(r + 1, r + 9), slice(r - 1, r + 7)
            sea, w_e, count_ns = (self.stat[i, at, :] for i in (0, 2, 5))
            for i in range(FIELDS):
                lap = self.laps[i, at, :]
                flux = self.flux[i, at, :] if i < 3 else None
                loss, gain = face_terms(i, lap, roll(lap, -1), w_e, flux)
                self.state[i, at, :] = second_pass(
                    self.part[i, at, :],
                    loss,
                    roll(gain, 1),
                    lap,
                    self.laps[i, up, :],
                    self.laps[i, down, :],
                    sea,
                    count_ns,
                )


def strip_own(low, high):
    lane = lane_index()
    second = lane >= 64
    west = jnp.where(second, roll(high, 72), roll(low, 8))
    east = jnp.where(second, roll(high, 112), roll(low, 48))
    return jnp.where(lax.rem(lane, 64) < 32, west, east)


def prepare(refs, fields, a_ref, e_ref, w_ref, inner, strip, ints, state, laps, part, flux, stat, sems):
    height = fields.shape[1]
    total_rows = height * lax.axis_size("lat")
    copies = []
    for i, ref in enumerate(refs):
        target = fields.at[i] if i < FIELDS else ints
        copies.append(pltpu.make_async_copy(ref.at[0], target, sems.at[i]))
    for copy in copies:
        copy.start()
    for copy in copies:
        copy.wait()
    fields[FIELDS] = ints[...].astype(jnp.float32)
    odd = is_odd()
    bands = Band(state, laps, part, flux, stat)
    bands.pad()
    for i in range(5):
        tiles = [fields[i, 8 * g : 8 * g + 8, :] for g in range(height // 8)]
        a_ref[i * 8 : i * 8 + 8, :] = jnp.where(odd, tiles[0], tiles[-1])
        e = w = jnp.zeros((8, LANES), jnp.float32)
        ref, at = (state, i) if i < FIELDS else (stat, 0)
        for g, tile in enumerate(tiles):
            e, w = add_columns(e, w, tile, g + 1)
            ref[at, 8 + 8 * g : 16 + 8 * g, :] = tile
        e_ref[i * 8 : i * 8 + 8, :] = e
        w_ref[i * 8 : i * 8 + 8, :] = w
        for n in range(STRIP):
            low, high = tiles[max(n - 1, 0)], tiles[min(n + STRIP_STEP - 1, len(tiles) - 1)]
            strip[i, 8 * n : 8 * n + 8, :] = strip_own(low, high)
    base_row = (lax.axis_index("lat") * height).astype(jnp.float32)
    sub = row_in_tile()
    bands.weigh(lambda r: turning_of(base_row + float(r - 8) + sub, total_rows))

    def step(n, carry):
        bands.step()
        return carry

    lax.fori_loop(0, STEPS, step, 0)
    for i in range(FIELDS):
        for g in range(height // 8):
            inner[i, 8 * g : 8 * g + 8, :] = state[i, 8 + 8 * g : 16 + 8 * g, :]


def early_kernel(*refs):
    @pl.when(is_early())
    def _():
        prepare(refs[:5], *refs[5:])


def late_kernel(*refs):
    early = is_early()

    @pl.when(early)
    def _():
        for source, target in zip(refs[6:12], refs[12:18]):
            target[...] = source[...]

    @pl.when(jnp.logical_not(early))
    def _():
        prepare(refs[:5], *refs[12:])


def strip_ghosts(blocks, old):
    before, here, after = blocks
    lane = lane_index(here.shape[0])
    new = jnp.where(lane < 96, roll(here, 72), roll(here, 112))
    new = jnp.where(lane < 72, roll(before, 64 - (LANES - HALO)), new)
    new = jnp.where(lane >= 112, roll(after, 112), new)
    return jnp.where(lane < 64, old, new)


def join_columns(centre, strip, second):
    lane = lane_index()
    start = 64 if second else 0
    west, east = roll(strip, -start - HALO), roll(strip, LANES - HALO - start - 40)
    return jnp.where(lane < HALO, west, jnp.where(lane >= LANES - HALO, east, centre))


def turning_of(row, total_rows):
    return (TIME_STEP * ROTATION) * (2.0 * (row + 0.5) / total_rows - 1.0)


def row_in_tile():
    return lax.broadcasted_iota(jnp.int32, (8, LANES), 0).astype(jnp.float32)


def frame_kernel(
    fields,
    strip,
    inner,
    sb_ref,
    ra_ref,
    rb_ref,
    first_in,
    second_in,
    t_out,
    s_out,
    u_out,
    v_out,
    upper_state,
    upper_stat,
    state,
    laps,
    part,
    flux,
    stat,
):
    rw_ref, re_ref = near_refs(first_in, second_in)
    odd, top = is_odd(), is_top()
    lane = lane_index()
    height = fields.shape[1]
    total_rows = height * lax.axis_size("lat")
    north_row, strip_row = 8 + UPPER, 8 + 2 * UPPER
    bands = Band(state, laps, part, flux, stat)
    bands.pad()
    side = lax.rem(lane, 64)

    for i in range(5):
        at = slice(i * 8, i * 8 + 8)
        ra, rb, from_w, from_e = ra_ref[at, :], rb_ref[at, :], rw_ref[at, :], re_ref[at, :]
        south, north = jnp.where(odd, ra, rb), jnp.where(odd, rb, ra)
        ref, at = (state, i) if i < FIELDS else (stat, 0)
        ref[at, 8:16, :] = south
        ref[at, 16 : 8 + UPPER, :] = fields[i, 0 : UPPER - 8, :]
        ref[at, north_row : north_row + UPPER - 8, :] = fields[i, height - UPPER + 8 : height, :]
        ref[at, north_row + UPPER - 8 : strip_row, :] = north
        for n in range(STRIP):
            own = strip[i, 8 * n : 8 * n + 8, :]
            if n == 0:
                own = jnp.where(lane < 64, strip_own(south, south), own)
            if n == STRIP - 1:
                own = jnp.where(lane >= 64, strip_own(north, north), own)
            own = jnp.where(side < HALO, roll(from_w, -8 * n), own)
            own = jnp.where(side >= 48, roll(from_e, 48 - 8 * n), own)
            ref[at, strip_row + 8 * n : strip_row + 8 * n + 8, :] = own

    @pl.when(top)
    def _():
        pairs = (
            (rw_ref, 40, rw_ref, 40 + CAP),
            (sb_ref, 0, rb_ref, 0),
            (re_ref, 40, re_ref, 40 + CAP),
        )
        for i in range(5):
            ghosts = []
            for own, own_at, facing, facing_at in pairs:
                index = lax.rem(own[own_at + 40 : own_at + 48, :].astype(jnp.int32), LANES)
                rows = facing[facing_at + 8 * i : facing_at + 8 * i + 8, :]
                ghosts.append(
                    (PARITY + (1.0,))[i]
                    * jnp.take_along_axis(rows, index, axis=1, mode="promise_in_bounds")
                )
            ref, at = (state, i) if i < FIELDS else (stat, 0)
            row = north_row + UPPER - HALO
            ref[at, row : row + 1, :] = ghosts[1][7:8, :]
            ref[at, row + 1 : row + 2, :] = ghosts[1][6:7, :]
            for n in (0, 1):
                row = strip_row + 8 * STRIP - HALO + n
                ref[at, row : row + 1, :] = strip_ghosts(
                    [ghost[7 - n : 8 - n, :] for ghost in ghosts], ref[at, row : row + 1, :]
                )

    base_row = (lax.axis_index("lat") * height - HALO).astype(jnp.float32)
    sub = row_in_tile()
    second = jnp.where(lane >= 64, 8.0 * STRIP_STEP, 0.0)

    def turning(r):
        if r < north_row:
            row = base_row + float(r - 8) + sub
        elif r < strip_row:
            row = base_row + float(height + 2 * HALO - UPPER + r - north_row) + sub
        else:
            row = base_row + float(r - strip_row) + sub + second
        return turning_of(row, total_rows)

    bands.weigh(turning)

    def step(n, carry):
        bands.step()

        @pl.when(top & (n == 0))
        def _():
            for which, row in enumerate((north_row, strip_row + 8 * STRIP - UPPER)):
                for i in range(FIELDS):
                    upper_state[i, which] = state[i, row : row + UPPER, :]
                for i in range(STATS):
                    upper_stat[i, which] = stat[i, row : row + UPPER, :]

        return carry

    lax.fori_loop(0, STEPS, step, 0)

    tiles_n = height // 8
    for i, out in enumerate((t_out, s_out, u_out, v_out)):
        for g in range(tiles_n):
            if g == 0:
                centre = state[i, 16:24, :]
            elif g == tiles_n - 1:
                centre = state[i, north_row + 8 : north_row + 16, :]
            else:
                centre = inner[i, 8 * g : 8 * g + 8, :]
            late = g + 1 > STRIP_STEP
            row = strip_row + 8 * (g + 1 - (STRIP_STEP if late else 0))
            out[0, 8 * g : 8 * g + 8, :] = join_columns(centre, state[i, row : row + 8, :], late)


class Each:
    def __init__(self, make):
        self.make, self.made = make, {}

    def __call__(self, k):
        if k not in self.made:
            self.made[k] = self.make(k)
        return self.made[k]


def beside(block, first, last):
    lane = lane_index()
    e = Each(lambda k: roll(block(k), -1))
    w = Each(lambda k: roll(block(k), 1))
    return (
        Each(lambda k: jnp.where(lane == LANES - 1, e(min(k + 1, last)), e(k))),
        Each(lambda k: jnp.where(lane == 0, w(max(k - 1, first)), w(k))),
    )


def cap_kernel(
    t_in,
    s_in,
    u_in,
    v_in,
    upper_state,
    upper_stat,
    sb_ref,
    rb_ref,
    first_in,
    second_in,
    first_far,
    second_far,
    t_out,
    s_out,
    u_out,
    v_out,
    state,
    laps,
    part,
    flux,
    stat,
    cap,
    cap_lap,
    cap_part,
    cap_flux,
    cap_stat,
    cap_opp,
    rows_out,
    sems,
):
    rw_ref, re_ref = near_refs(first_in, second_in)
    far_flag = jnp.logical_not(is_odd_lon())
    w3_ref = Either(far_flag, second_far, first_far)
    e3_ref = Either(far_flag, first_far, second_far)
    lane = lane_index()
    height = t_out.shape[1]
    total_rows = height * lax.axis_size("lat")
    bands = Band(state, laps, part, flux, stat)
    nothing = jnp.zeros((8, LANES), jnp.float32)
    cap_turn = turning_of(float(total_rows - HALO + 1) + row_in_tile(), total_rows)

    def fill_ghosts(ref, parities, low, high, sides):
        for side in sides:
            ghosts = {}
            for k in range(low, high):
                index = cap_opp[side, k]
                for i, parity in enumerate(parities):
                    rows = ref[1 - side, i, ARC - 1 - k, 0:8, :]
                    ghosts[k, i] = parity * jnp.take_along_axis(
                        rows, index, axis=1, mode="promise_in_bounds"
                    )
            for (k, i), ghost in ghosts.items():
                ref[side, i, k, 8:9, :] = ghost[7:8, :]
                ref[side, i, k, 9:10, :] = ghost[6:7, :]

    def put_block(side, place, ref, base, n):
        sea = ref[base + 4 * n : base + 5 * n, :]
        cap_stat[side, 0, place, 8 - n : 8, :] = sea
        cap_stat[side, 0, place, 10:16, :] = nothing[0:6]
        if n < 8:
            cap_stat[side, 0, place, 0 : 8 - n, :] = nothing[n:8]
        for i in range(FIELDS):
            cap[side, i, place, 8 - n : 8, :] = sea * ref[base + n * i : base + n * i + n, :]
            if n < 8:
                cap[side, i, place, 0 : 8 - n, :] = nothing[n:8]
            cap[side, i, place, 10:16, :] = nothing[0:6]
            cap_lap[side, i, place, 0:8, :] = nothing
            cap_lap[side, i, place, 8:16, :] = nothing
        opp = jnp.broadcast_to(ref[base + 5 * n : base + 5 * n + 1, :], (8, LANES))
        cap_opp[side, place] = lax.rem(opp.astype(jnp.int32), LANES)

    def cap_weigh():
        for side in (0, 1):
            for start in (0, 1):
                seas = Each(lambda k: cap_stat[side, 0, k, start : start + 8, :])
                east, west = beside(seas, 0, ARC - 1)
                for k in range(ARC):
                    north = cap_stat[side, 0, k, start + 1 : start + 9, :]
                    if start:
                        south = cap_stat[side, 0, k, start - 1 : start + 7, :]
                        cap_stat[side, 1, k, 1:9, :] = (east(k) + west(k)) + (north + south)
                        cap_stat[side, 4, k, 1:9, :] = north + south
                    cap_stat[side, 2, k, start : start + 8, :] = seas(k) * east(k)
                    cap_stat[side, 3, k, start : start + 8, :] = seas(k) * north

    def cap_first(side, low, high):
        west_end, east_end = low - 1, high

        def field(i):
            centre = Each(lambda k: cap[side, i, k, 1:9, :])
            return centre, *beside(centre, west_end, east_end)

        fields = [field(i) for i in range(FIELDS)]
        for k in range(west_end, east_end + 1):
            lap, partial, fluxes = first_pass(
                [centre(k) for centre, _, _ in fields],
                [cap[side, i, k, 2:10, :] for i in range(FIELDS)],
                [cap[side, i, k, 0:8, :] for i in range(FIELDS)],
                [east(k) for _, east, _ in fields],
                [west(k) for _, _, west in fields],
                [cap_stat[side, i, k, 1:9, :] for i in range(4)] + [cap_turn],
                cap_stat[side, 3, k, 0:8, :],
            )
            for i in range(FIELDS):
                cap_lap[side, i, k, 1:9, :] = lap[i]
                if i < 3:
                    cap_flux[side, i, k, 0:8, :] = fluxes[i]
                if low <= k < high:
                    cap_part[side, i, k, 0:8, :] = partial[i]

    def cap_second(side, low, high):
        def field(i):
            lap = Each(lambda k: cap_lap[side, i, k, 1:9, :])
            east, _ = beside(lap, low - 1, high)
            terms = Each(
                lambda k: face_terms(
                    i,
                    lap(k),
                    east(k),
                    cap_stat[side, 2, k, 1:9, :],
                    cap_flux[side, i, k, 0:8, :] if i < 3 else None,
                )
            )
            _, gain = beside(lambda k: terms(k)[1], low - 1, high)
            return lap, terms, gain

        fields = [field(i) for i in range(FIELDS)]
        for k in range(low, high):
            for i, (lap, terms, gain) in enumerate(fields):
                cap[side, i, k, 1:9, :] = second_pass(
                    cap_part[side, i, k, 0:8, :],
                    terms(k)[0],
                    gain(k),
                    lap(k),
                    cap_lap[side, i, k, 2:10, :],
                    cap_lap[side, i, k, 0:8, :],
                    cap_stat[side, 0, k, 1:9, :],
                    cap_stat[side, 4, k, 1:9, :],
                )

    @pl.when(is_top())
    def _():
        parts = [(j, side, w3_ref, base, n) for j, side, n, base in far_places(FAR_ROWS)]
        parts += [
            (j + REACH + 2, side, e3_ref, base, n)
            for j, side, n, base in far_places(FAR_ROWS[::-1])
        ]
        for side in (0, 1):
            parts.append((REACH - 1, side, rw_ref, 40 + CAP * side, 8))
            parts.append((REACH, side, (sb_ref, rb_ref)[side], 0, 8))
            parts.append((REACH + 1, side, re_ref, 40 + CAP * side, 8))
        for k, side, ref, base, n in parts:
            put_block(side, ARC - 1 - k if side else k, ref, base, n)
        bands.pad()
        for which in (0, 1):
            row = 8 + UPPER * which
            for i in range(FIELDS):
                state[i, row : row + UPPER, :] = upper_state[i, which]
            for i in range(STATS):
                stat[i, row : row + UPPER, :] = upper_stat[i, which]
        fill_ghosts(cap_stat, (1.0,), 0, ARC, (0, 1))
        fill_ghosts(cap, PARITY, 0, ARC, (0, 1))
        cap_weigh()
        for n in range(STEPS - 1):
            low, high = n + 1, ARC - 1 - n
            first_side = 1 if n == STEPS - 2 else 0

            def one(side, carry, low=low, high=high):
                cap_first(side, low, high)
                cap_second(side, low, high)
                return carry

            lax.fori_loop(first_side, 2, one, 0)
            if n == STEPS - 3:
                fill_ghosts(cap, PARITY, REACH - 1, REACH + 2, (0,))
                fill_ghosts(cap, PARITY, low, high, (1,))
            else:
                fill_ghosts(cap, PARITY, low, high, range(2 - first_side))
            for i in range(FIELDS):
                ghosts = [cap[0, i, k, 8:10, :] for k in (REACH - 1, REACH, REACH + 1)]
                row = 8 + UPPER - HALO
                state[i, row : row + 2, :] = ghosts[1]
                row += UPPER
                state[i, row : row + 2, :] = strip_ghosts(ghosts, state[i, row : row + 2, :])
            start = 16 if n == STEPS - 2 else 8
            bands.step([r + UPPER * which for which in (0, 1) for r in range(start, 24, 8)])
        copies = []
        for i, out in enumerate((t_out, s_out, u_out, v_out)):
            row = 8 + UPPER - 2 * HALO
            rows_out[i] = join_columns(
                state[i, row : row + 8, :], state[i, row + UPPER : row + UPPER + 8, :], True
            )
            copies.append(
                pltpu.make_async_copy(
                    rows_out.at[i], out.at[0, pl.ds(height - HALO, HALO), :], sems.at[i]
                )
            )
            copies[-1].start()
        for copy in copies:
            copy.wait()


def body(lon_count, lat_count, t, s, u, v, m, opp):
    fields = (t, s, u, v, m)
    height = t.shape[1]
    vmem, anywhere = (
        pl.BlockSpec(memory_space=pltpu.VMEM),
        pl.BlockSpec(memory_space=pltpu.HBM),
    )
    f32, i32 = jnp.float32, jnp.int32

    def call(kernel, inputs, shapes, scratch=(), far=0, flops=0):
        inputs = [
            pltpu.with_memory_space_constraint(x, pltpu.HBM) if i < far else x
            for i, x in enumerate(inputs)
        ]
        return pl.pallas_call(
            kernel,
            out_shape=[jax.ShapeDtypeStruct(shape, f32) for shape in shapes],
            in_specs=[anywhere] * far + [vmem] * (len(inputs) - far),
            out_specs=[vmem] * len(shapes),
            scratch_shapes=list(scratch),
            compiler_params=pltpu.CompilerParams(vmem_limit_bytes=32 * 1024 * 1024),
            cost_estimate=pl.CostEstimate(flops=flops, bytes_accessed=flops, transcendentals=0),
        )(*inputs)

    def place(lon, lat):
        return (lon % lon_count) * lat_count + lat

    lons, lats = range(lon_count), range(lat_count)
    last = lat_count - 1
    pairs_a = [(place(i, j), place(i, j ^ 1)) for i in lons for j in lats]
    pairs_b = [(place(i, j), place(i, ((j - 1) ^ 1) + 1)) for i in lons for j in lats[1:last]]
    pairs_b += [(place(i, last), place(-i, last)) for i in lons]

    def swap(x, by, rest, rows):
        pairs = []
        for i in lons:
            other = i + by if i % 2 == rest else i - by
            pairs += [(place(i, j), place(other, j)) for j in rows]
        return exchange(x, pairs)

    def exchange(x, pairs):
        return lax.ppermute(x, ("lon", "lat"), pairs)

    def band_scratch(rows):
        return [
            pltpu.VMEM((n, 16 + rows, LANES), f32) for n in (FIELDS, FIELDS, FIELDS, 3, STATS)
        ]

    prepared = [(5, height, LANES), (40, LANES), (40, LANES), (40, LANES)]
    prepared += [(FIELDS, height, LANES), (5, 8 * STRIP, LANES)]
    scratch = [pltpu.VMEM((height, LANES), i32), *band_scratch(height), pltpu.SemaphoreType.DMA((5,))]
    own = call(early_kernel, fields, prepared, scratch, far=5, flops=10**7)
    (send_b,) = call(
        first_rows_kernel,
        (*fields, opp.reshape(1, LANES), own[1]),
        [(CAP, LANES)],
        [pltpu.VMEM((16, LANES), i32), pltpu.SemaphoreType.DMA((6,))],
        far=6,
    )
    from_b = exchange(send_b, pairs_b)
    stack, send_a, columns_e, columns_w, inner, strip = call(
        late_kernel, (*fields, send_b, *own), prepared, scratch, far=5, flops=10**7
    )
    from_a = exchange(send_a, pairs_a)
    send_1, send_2 = call(
        functools.partial(pair_kernel, height),
        (columns_e, columns_w, send_b, from_a, from_b),
        [(40 + 2 * CAP, LANES)] * 2,
    )
    near_1 = swap(send_1, 1, 1, lats)
    near_2 = swap(send_2, 1, 0, lats)
    far_send_1, far_send_2 = call(
        far_kernel, (send_b, from_b, near_1, near_2), [(FAR, LANES)] * 2
    )
    far_1 = swap(far_send_1, 3, 0, [last])
    far_2 = swap(far_send_2, 3, 1, [last])

    *outs, upper_state, upper_stat = call(
        frame_kernel,
        (stack, strip, inner, send_b, from_a, from_b, near_1, near_2),
        [t.shape] * 4 + [(FIELDS, 2, UPPER, LANES), (STATS, 2, UPPER, LANES)],
        band_scratch(2 * UPPER + 8 * STRIP),
        flops=10**7,
    )
    return tuple(
        pl.pallas_call(
            cap_kernel,
            out_shape=[jax.ShapeDtypeStruct(t.shape, f32)] * 4,
            in_specs=[anywhere] * 4 + [vmem] * 8,
            out_specs=[anywhere] * 4,
            scratch_shapes=band_scratch(2 * UPPER)
            + [
                pltpu.VMEM((2, FIELDS, ARC, 16, LANES), f32),
                pltpu.VMEM((2, FIELDS, ARC, 16, LANES), f32),
                pltpu.VMEM((2, FIELDS, ARC, 8, LANES), f32),
                pltpu.VMEM((2, 3, ARC, 8, LANES), f32),
                pltpu.VMEM((2, 5, ARC, 16, LANES), f32),
                pltpu.VMEM((2, ARC, 8, LANES), i32),
                pltpu.VMEM((FIELDS, 8, LANES), f32),
                pltpu.SemaphoreType.DMA((FIELDS,)),
            ],
            input_output_aliases={i: i for i in range(4)},
            compiler_params=pltpu.CompilerParams(vmem_limit_bytes=32 * 1024 * 1024),
        )(*outs, upper_state, upper_stat, send_b, from_b, near_1, near_2, far_1, far_2)
    )


def solution(mesh):
    placed = P(None, "lat", "lon")
    return jax.shard_map(
        functools.partial(body, mesh.shape["lon"], mesh.shape["lat"]),
        mesh=mesh,
        in_specs=(placed,) * 5 + (P("lon"),),
        out_specs=(placed,) * 4,
        check_vma=False,
    )
```
